32 devices in a mesh: section: 2 (over x), tensor: 4 (over y, core), dp: 4 (over z).
Axes of the slice: x: 2, y: 2, z: 4, core: 2. Of those that a mesh axis runs over, the one named last changes fastest.
Arguments:
- endpoints: bfloat16 [2, 2, 4, 1024, 1024], P('section', None, 'dp', 'tensor'), may hold values from -6 to 6
- lengths: int32 [2, 4, 6], P(None, 'dp'), may hold values from 0 to 1024, as said below
- timesteps: int32 [2, 4, 6], P(None, 'dp'), may hold values from 0 to 999
- w_qkv: bfloat16 [2, 3, 1024, 1024], P('section', None, 'dp', 'tensor'), may hold values from -0.1875 to 0.1875
- b_qkv: bfloat16 [2, 3, 1024], P('section', None, ('tensor', 'dp')), may hold values from -3 to 3
- w_out: bfloat16 [2, 1024, 1024], P('section', 'tensor', 'dp'), may hold values from -1.5 to 1.5
- b_out: bfloat16 [2, 1024], P('section', 'dp'), may hold values from -3 to 3
- w_up: bfloat16 [2, 1024, 2048], P('section', 'dp', 'tensor'), may hold values from -0.1875 to 0.1875
- b_up: bfloat16 [2, 2048], P('section', ('tensor', 'dp')), may hold values from -3 to 3
- w_down: bfloat16 [2, 2048, 1024], P('section', 'tensor', 'dp'), may hold values from -0.125 to 0.125
- b_down: bfloat16 [2, 1024], P('section', 'dp'), may hold values from -3 to 3
- w_mod: bfloat16 [2, 1024, 6144], P('section', 'dp'), may hold values from -0.375 to 0.375
- b_mod: bfloat16 [2, 6144], P('section', 'dp'), may hold values from -3 to 3
Outputs:
- activations: bfloat16 [2, 2, 4, 1024, 1024], P('section', None, 'dp', 'tensor')
- input_grads: bfloat16 [2, 2, 4, 1024, 1024], P('section', None, 'dp', 'tensor')
- grad_w_qkv: float32 [2, 3, 1024, 1024], P('section', None, 'dp', 'tensor')
- grad_b_qkv: float32 [2, 3, 1024], P('section', None, ('tensor', 'dp'))
- grad_w_out: float32 [2, 1024, 1024], P('section', 'tensor', 'dp')
- grad_b_out: float32 [2, 1024], P('section', 'dp')
- grad_w_up: float32 [2, 1024, 2048], P('section', 'dp', 'tensor')
- grad_b_up: float32 [2, 2048], P('section', ('tensor', 'dp'))
- grad_w_down: float32 [2, 2048, 1024], P('section', 'tensor', 'dp')
- grad_b_down: float32 [2, 1024], P('section', 'dp')
- grad_w_mod: float32 [2, 1024, 6144], P('section', 'dp')
- grad_b_mod: float32 [2, 6144], P('section', 'dp')
The draws below stay inside these ranges and needn't reach their ends.
Inputs may be any that keep to these rules, and one draw needn't show every extreme that they name: lengths[m, g] lists the frame counts of the 6 utterance slots of buffer (m, g), laid one after another from frame 0 in slot order (a slot may be empty); they sum to at most 1024, the frames after them are padding; in one buffer of each group one utterance begins before frame 256 and ends after frame 1024 - 256, and in some group it fills its whole buffer.
All inputs are finite; a program needn't handle non-finite values.
Results may differ from the reference program's by a relative error of at most 0.035.
Values may be sent and summed in bfloat16 or wider, within the bound.
No kernel may reach another device: no remote copies, remote signals or barrier semaphores. Data moves between devices by JAX's collectives and lax.ppermute only.
A program may use at most 256 MiB of HBM per device.

```python
import math
import jax
import jax.numpy as jnp
from jax import lax

D = 1024
HEAD_DIM = 64
FF = 2048
MICRO = 2
UPB = 6
LAYERS = 2
GROUPS = 4
SEQ = 1024
ROWS = 256


def draw_lengths(key, part):
    key = jax.random.fold_in(key, 7)
    subkeys = jax.random.split(key, 5)
    cut_points = jnp.sort(jax.random.randint(subkeys[0], (MICRO, GROUPS, UPB), 0, SEQ + 1), axis=-1)
    before = jnp.concatenate([jnp.zeros((MICRO, GROUPS, 1), jnp.int32), cut_points[:, :, :-1]], axis=-1)
    ragged = (cut_points - before).astype(jnp.int32)
    leading = jax.random.randint(subkeys[1], (MICRO, GROUPS), 0, ROWS)
    trailing = jax.random.randint(subkeys[2], (MICRO, GROUPS), 0, ROWS)
    full_group = jax.random.randint(subkeys[3], (), 0, GROUPS)
    span_micro = jax.random.randint(subkeys[4], (GROUPS,), 0, MICRO)
    group_id = jnp.arange(GROUPS, dtype=jnp.int32)[None, :]
    leading = jnp.where(group_id == full_group, 0, leading)
    trailing = jnp.where(group_id == full_group, 0, trailing)
    central = SEQ - leading - trailing
    spanning = jnp.concatenate([leading[:, :, None], central[:, :, None], trailing[:, :, None], jnp.zeros((MICRO, GROUPS, UPB - 3), jnp.int32)], axis=-1)
    chosen = (jnp.arange(MICRO, dtype=jnp.int32)[:, None] == span_micro[None, :])[:, :, None]
    return jnp.where(chosen, spanning, ragged).astype(jnp.int32)


def plant(result, key, least, top_value):
    index_at = [jax.random.randint(jax.random.fold_in(key, axis), (), 0, length) for axis, length in enumerate(result.shape)]
    main_axis = result.shape.index(max(result.shape))
    next_to = index_at[:main_axis] + [(index_at[main_axis] + 1) % result.shape[main_axis]] + index_at[main_axis + 1:]
    return result.at[tuple(index_at)].set(least).at[tuple(next_to)].set(top_value)


def level_of(rng, extent, shards, low, high):
    def one(axis_at, blocks):
        draws = jax.random.uniform(jax.random.fold_in(jax.random.fold_in(rng, 6), axis_at), (blocks,), jnp.float32, low / len(shards), high / len(shards))
        return jnp.repeat(jnp.exp(draws), extent[axis_at] // blocks).reshape((-1,) + (1,) * (len(extent) - axis_at - 1))

    factor_of = one(*shards[0])
    for cut in shards[1:]:
        factor_of = factor_of * one(*cut)
    return factor_of


def normal_values(stream_key, shape, scale, bound, cuts=(), kind=jnp.bfloat16):
    loudness = level_of(stream_key, shape, cuts, -0.22, 0.18) if cuts else 1.0
    array = jax.random.normal(stream_key, shape, jnp.float32) * scale * loudness
    return jnp.minimum(jnp.maximum(array, -bound), bound).astype(kind)


def setup_inputs(seed: int = 0) -> dict:
    streams_of = jax.random.split(jax.random.key(seed), 14)
    return {
        "endpoints": normal_values(streams_of[0], (LAYERS, MICRO, GROUPS, SEQ, D), 1.0, 6.0, ((0, 2), (2, 4), (3, 4))),
        "lengths": draw_lengths(jax.random.fold_in(streams_of[13], 71), 0),
        "timesteps": plant(jax.random.randint(streams_of[2], (MICRO, GROUPS, UPB), 0, 1000), jax.random.fold_in(streams_of[2], 1), 0, 999).astype(jnp.int32),
        "w_qkv": normal_values(streams_of[3], (LAYERS, 3, D, D), D ** -0.5, 0.1875, ((0, 2), (2, 4), (3, 4))),
        "b_qkv": normal_values(streams_of[4], (LAYERS, 3, D), 0.5, 3.0, ((0, 2), (2, 16))),
        "w_out": normal_values(streams_of[5], (LAYERS, D, D), (max(1, D * 16 // SEQ)) ** -0.5, 1.5, ((0, 2), (1, 4), (2, 4))),
        "b_out": normal_values(streams_of[6], (LAYERS, D), 0.5, 3.0, ((0, 2), (1, 4))),
        "w_up": normal_values(streams_of[7], (LAYERS, D, FF), D ** -0.5, 0.1875, ((0, 2), (1, 4), (2, 4))),
        "b_up": normal_values(streams_of[8], (LAYERS, FF), 0.5, 3.0, ((0, 2), (1, 16))),
        "w_down": normal_values(streams_of[9], (LAYERS, FF, D), FF ** -0.5, 0.125, ((0, 2), (1, 4), (2, 4))),
        "b_down": normal_values(streams_of[10], (LAYERS, D), 0.5, 3.0, ((0, 2), (1, 4))),
        "w_mod": normal_values(streams_of[11], (LAYERS, D, 6 * D), (D // 4) ** -0.5, 0.375, ((0, 2), (1, 4))),
        "b_mod": normal_values(streams_of[12], (LAYERS, 6 * D), 0.5, 3.0, ((0, 2), (1, 4))),
    }


norm_eps = 1e-06
big_negative = -1e+30
highest = lax.Precision.HIGHEST

@jax.custom_vjp
def low(v):
    return lax.optimization_barrier(v.astype(jnp.bfloat16)).astype(jnp.float32)

@jax.custom_vjp
def low_back(v):
    return v

def low_keep(v):
    return (low(v), None)

def low_pass(kept, grad):
    return (grad,)

def back_keep(v):
    return (v, None)

def back_low(kept, grad):
    return (low(grad),)
low.defvjp(low_keep, low_pass)
low_back.defvjp(back_keep, back_low)

def layer_norm_mod(residual_stream, scale_part, shift_part):
    centre = residual_stream - lax.optimization_barrier(jnp.mean(residual_stream, axis=-1, keepdims=True))
    spread = lax.optimization_barrier(jnp.mean(centre * centre, axis=-1, keepdims=True))
    return centre * lax.rsqrt(spread + norm_eps) * (1.0 + scale_part) + shift_part

def rotary_tables(token_position, table_width, head_width):
    column = jnp.arange(table_width, dtype=jnp.int32) % head_width
    inverse = jnp.exp((column // 2).astype(jnp.float32) * (-2.0 * math.log(10000.0) / head_width))
    angles = token_position.astype(jnp.float32)[:, None] * inverse[None, :]
    return (jnp.cos(angles), jnp.sin(angles))

def rotate(values, cos_table, sin_table):
    row_total, table_width = values.shape
    paired = values.reshape(row_total, table_width // 2, 2)
    turned = jnp.stack([-paired[:, :, 1], paired[:, :, 0]], axis=-1).reshape(row_total, table_width)
    return values * cos_table + turned * sin_table

def segment_layout(lengths_here, total_rows):
    seg_end = jnp.cumsum(lengths_here).astype(jnp.int32)
    seg_start = (seg_end - lengths_here).astype(jnp.int32)
    frames = jnp.arange(total_rows, dtype=jnp.int32)
    utterance_segment = lax.optimization_barrier(jnp.sum((frames[:, None] >= seg_end[None, :]).astype(jnp.int32), axis=1)).astype(jnp.int32)
    member = utterance_segment[:, None] == jnp.arange(lengths_here.shape[0], dtype=jnp.int32)[None, :]
    seg_begin = lax.optimization_barrier(jnp.sum(jnp.where(member, seg_start[None, :], 0), axis=1)).astype(jnp.int32)
    return (utterance_segment, (frames - seg_begin).astype(jnp.int32))

def time_silu(step_values, code_width):
    half_width = code_width // 2
    frequency = jnp.exp(jnp.arange(half_width, dtype=jnp.float32) * (-math.log(10000.0) / (half_width - 1)))
    angles = step_values.astype(jnp.float32)[:, None] * frequency[None, :]
    return jax.nn.silu(jnp.concatenate([jnp.sin(angles), jnp.cos(angles)], axis=1))

def attention(queries, key_rows, values, utterance_segment):
    row_total = queries.shape[0]
    head_count = queries.shape[1] // HEAD_DIM
    score_scale = 1.0 / math.sqrt(HEAD_DIM)
    allowed = utterance_segment[:, None] == utterance_segment[None, :]

    def by_heads(matrix):
        return matrix.reshape(row_total, head_count, HEAD_DIM).transpose(1, 0, 2)

    @jax.checkpoint
    def one_head(operands):
        q_head, k_head, v_head = operands
        scores = low_back(jnp.dot(q_head, k_head.T, precision=highest) * score_scale)
        scores = jnp.where(allowed, scores, big_negative)
        row_max = lax.optimization_barrier(jnp.max(scores, axis=-1, keepdims=True))
        weight = jnp.exp(scores - row_max)
        attn_prob = weight / lax.optimization_barrier(jnp.sum(weight, axis=-1, keepdims=True))
        return jnp.dot(low(attn_prob), v_head, precision=highest)
    mixed_all = lax.map(one_head, (by_heads(queries), by_heads(key_rows), by_heads(values)))
    return mixed_all.transpose(1, 0, 2).reshape(row_total, head_count * HEAD_DIM)

def diffusion_transformer_layer(residual_stream, layer_weights, utterance_segment, token_position, timestep_silu_embedding):
    w_qkv, b_qkv, w_out, b_out, w_up, b_up, w_down, b_down, w_mod, b_mod = layer_weights
    modulation = jnp.dot(low(timestep_silu_embedding), w_mod, precision=highest) + b_mod
    padded = jnp.concatenate([modulation, jnp.zeros((1, modulation.shape[1]), jnp.float32)], axis=0)
    shift_a, scale_a, gate_a, shift_b, scale_b, gate_b = jnp.split(padded[utterance_segment], 6, axis=1)
    normed = low(layer_norm_mod(residual_stream, scale_a, shift_a))
    cos_table, sin_table = rotary_tables(token_position, D, HEAD_DIM)
    queries = low(rotate(low_back(jnp.dot(normed, w_qkv[0], precision=highest) + b_qkv[0]), cos_table, sin_table))
    key_rows = low(rotate(low_back(jnp.dot(normed, w_qkv[1], precision=highest) + b_qkv[1]), cos_table, sin_table))
    values = low(low_back(jnp.dot(normed, w_qkv[2], precision=highest) + b_qkv[2]))
    mixed_heads = low(low_back(attention(queries, key_rows, values, utterance_segment)))
    attn_sum = low_back(jnp.dot(mixed_heads, w_out, precision=highest) + b_out)
    residual1 = residual_stream + gate_a * attn_sum
    normed2 = low(layer_norm_mod(residual1, scale_b, shift_b))
    pre_act = low_back(jnp.dot(normed2, w_up, precision=highest) + b_up)
    activated = low(jax.nn.gelu(pre_act, approximate=True))
    ffn_sum = low_back(jnp.dot(activated, w_down, precision=highest) + b_down)
    return residual1 + gate_b * ffn_sum

def reference(endpoints, lengths, timesteps, w_qkv, b_qkv, w_out, b_out, w_up, b_up, w_down, b_down, w_mod, b_mod):
    stacked = (w_qkv, b_qkv, w_out, b_out, w_up, b_up, w_down, b_down, w_mod, b_mod)
    layer_slices = tuple((tuple((weight_arr[layer_number].astype(jnp.float32) for weight_arr in stacked)) for layer_number in range(LAYERS)))

    def one_buffer(totals, buffer_index):
        micro_index = buffer_index // GROUPS
        group_index = buffer_index % GROUPS
        utterance_segment, token_position = segment_layout(lengths[micro_index, group_index], SEQ)
        timestep_silu_embedding = time_silu(timesteps[micro_index, group_index], D)
        hidden_rows = endpoints[0, micro_index, group_index].astype(jnp.float32)
        layer_outs = []
        pullbacks = []
        for layer_number in range(LAYERS):
            layer_output, backward_function = jax.vjp(lambda input_rows, incoming_weights: diffusion_transformer_layer(input_rows, incoming_weights, utterance_segment, token_position, timestep_silu_embedding), hidden_rows, layer_slices[layer_number])
            hidden_rows = low(layer_output)
            layer_outs.append(hidden_rows)
            pullbacks.append(backward_function)
        live_rows = (utterance_segment < UPB).astype(jnp.float32)[:, None]
        grad_rows = endpoints[1, micro_index, group_index].astype(jnp.float32) * live_rows
        input_list = [None] * LAYERS
        param_list = [None] * LAYERS
        for layer_number in reversed(range(LAYERS)):
            d_rows, d_params = pullbacks[layer_number](grad_rows)
            grad_rows = low(d_rows)
            input_list[layer_number] = grad_rows
            param_list[layer_number] = d_params
        totals = jax.tree.map(jnp.add, totals, tuple(param_list))
        return (totals, (jnp.stack(layer_outs).astype(jnp.bfloat16), jnp.stack(input_list).astype(jnp.bfloat16)))
    initial = jax.tree.map(jnp.zeros_like, layer_slices)
    totals, (layer_stack, grad_stack) = lax.scan(one_buffer, initial, jnp.arange(MICRO * GROUPS, dtype=jnp.int32))

    def arrange(stacked_arr):
        return stacked_arr.reshape(MICRO, GROUPS, LAYERS, SEQ, D).transpose(2, 0, 1, 3, 4)
    grad_list = [jnp.stack([totals[layer_number][member] for layer_number in range(LAYERS)]) for member in range(10)]
    return (arrange(layer_stack), arrange(grad_stack), grad_list[0], grad_list[1], grad_list[2], grad_list[3], grad_list[4], grad_list[5], grad_list[6], grad_list[7], grad_list[8], grad_list[9])
```

```python
import functools
import math

import jax
import jax.numpy as jnp
from jax import lax
from jax.experimental import pallas as pl
from jax.experimental.pallas import tpu as pltpu
from jax.sharding import PartitionSpec as P

HEAD_DIM = 64
SLOT_ROWS = 8
norm_eps = 1e-06
big_negative = -1e30
f32 = jnp.float32
bf16 = jnp.bfloat16
vmem_limit = 52 * 1024 * 1024


def swap(block, axis, bit):
    return lax.ppermute(block, axis, [(i, i ^ bit) for i in range(lax.axis_size(axis))])


def bits_of(count):
    bit = 1
    while bit < count:
        yield bit
        bit *= 2


def gather_rows(block):
    blocks = {0: block}
    for bit in reversed(list(bits_of(lax.axis_size("tensor")))):
        blocks.update({j | bit: swap(part, "tensor", bit) for j, part in list(blocks.items())})
    return [blocks[j] for j in range(len(blocks))]


def scatter_rows(parts):
    kept = dict(enumerate(parts))
    addends = [parts[0]]
    for bit in bits_of(len(parts)):
        arrived = {j: swap(kept[j | bit], "tensor", bit) for j in kept if not j & bit}
        addends.append(arrived.pop(0))
        kept = {
            0: parts[0],
            **{
                j: (kept[j].astype(f32) + part.astype(f32)).astype(parts[0].dtype)
                for j, part in arrived.items()
            },
        }
    return addends


def gather_groups(block):
    return lax.all_gather(block, "dp", axis=0, tiled=False)


def call(body, outs, *args, scratch=(), flops=0):
    moved = sum(x.size * x.dtype.itemsize for x in args)
    moved += sum(math.prod(x.shape) * jnp.dtype(x.dtype).itemsize for x in outs)
    return pl.pallas_call(
        body,
        out_shape=tuple(outs),
        scratch_shapes=scratch,
        compiler_params=pltpu.CompilerParams(vmem_limit_bytes=vmem_limit),
        cost_estimate=pl.CostEstimate(flops=flops, bytes_accessed=moved, transcendentals=0),
    )(*args)


def shape(dims, dtype):
    return jax.ShapeDtypeStruct(dims, dtype)


def mm(left, right):
    return lax.dot_general(left, right, (((1,), (0,)), ((), ())), preferred_element_type=f32)


def mm_last(left, right):
    return lax.dot_general(left, right, (((1,), (1,)), ((), ())), preferred_element_type=f32)


def mm_first(left, right):
    return lax.dot_general(left, right, (((0,), (0,)), ((), ())), preferred_element_type=f32)


def slot_pick(seg_col):
    rows = seg_col.shape[0]
    lane = lax.broadcasted_iota(jnp.int32, (rows, SLOT_ROWS), 1)
    return (lane == seg_col).astype(f32).astype(bf16)


def part_of(picked, mod_ref, index, width):
    values = mod_ref[:, index * width : (index + 1) * width]
    high = values.astype(bf16)
    rest = (values - high.astype(f32)).astype(bf16)
    return mm(picked, high) + mm(picked, rest)


def slot_sums(seg_row, slots, values):
    row = lax.broadcasted_iota(jnp.int32, (SLOT_ROWS, seg_row.shape[1]), 0)
    picked = ((row == seg_row) & (row < slots)).astype(f32).astype(bf16)
    return mm(picked, values.astype(bf16))


def normed(values):
    centre = values - jnp.mean(values, axis=-1, keepdims=True)
    spread = jnp.mean(centre * centre, axis=-1, keepdims=True)
    inverse = lax.rsqrt(spread + norm_eps)
    return centre * inverse, inverse


def norm_back(norm, inverse, d_norm):
    mean_d = jnp.mean(d_norm, axis=-1, keepdims=True)
    mean_dn = jnp.mean(d_norm * norm, axis=-1, keepdims=True)
    return inverse * (d_norm - mean_d - norm * mean_dn)


def total(refs):
    value = refs[0][...].astype(f32)
    for ref in refs[1:]:
        value = value + ref[...].astype(f32)
    return value


def first_norm_kernel(width, h_ref, seg_ref, mod_ref, a1_ref):
    picked = slot_pick(seg_ref[...])
    norm, _ = normed(h_ref[...].astype(f32))
    scale = part_of(picked, mod_ref, 1, width)
    shift = part_of(picked, mod_ref, 0, width)
    a1_ref[...] = (norm * (1.0 + scale) + shift).astype(bf16)


def middle_kernel(width, terms, *refs):
    sums = refs[:terms]
    h_ref, bias_ref, seg_ref, mod_ref, z1_ref, h1_ref, a2_ref = refs[terms:]
    picked = slot_pick(seg_ref[...])
    z1 = total(sums) + bias_ref[...]
    z1_ref[...] = z1.astype(bf16)
    h1 = h_ref[...].astype(f32) + part_of(picked, mod_ref, 2, width) * z1
    h1_ref[...] = h1
    norm, _ = normed(h1)
    a2_ref[...] = (
        norm * (1.0 + part_of(picked, mod_ref, 4, width)) + part_of(picked, mod_ref, 3, width)
    ).astype(bf16)


def layer_end_kernel(width, terms, *refs):
    sums = refs[:terms]
    h1_ref, bias_ref, seg_ref, mod_ref, next_ref, z2_ref, y_ref, a1_ref = refs[terms:]
    picked = slot_pick(seg_ref[...])
    z2 = total(sums) + bias_ref[...]
    z2_ref[...] = z2.astype(bf16)
    y = (h1_ref[...] + part_of(picked, mod_ref, 5, width) * z2).astype(bf16)
    y_ref[...] = y
    norm, _ = normed(y.astype(f32))
    a1_ref[...] = (
        norm * (1.0 + part_of(picked, next_ref, 1, width)) + part_of(picked, next_ref, 0, width)
    ).astype(bf16)


def branch_back(width, slots, grad, z2, picked, seg_row, mod_ref, dz2_ref, dgate_ref):
    dz2_ref[...] = (grad * part_of(picked, mod_ref, 5, width)).astype(bf16)
    dgate_ref[...] = slot_sums(seg_row, slots, grad * z2)


def turn_kernel(width, slots, terms, *refs):
    sums = refs[:terms]
    (h1_ref, bias_ref, seg_ref, seg_row_ref, mod_ref, cot_ref) = refs[terms : terms + 6]
    y_ref, c_ref, dz2_ref, dgate_ref = refs[terms + 6 :]
    seg = seg_ref[...]
    picked = slot_pick(seg)
    z2 = total(sums) + bias_ref[...]
    y_ref[...] = (h1_ref[...] + part_of(picked, mod_ref, 5, width) * z2).astype(bf16)
    grad = jnp.where(seg < slots, cot_ref[...].astype(f32), 0.0)
    c_ref[...] = grad.astype(bf16)
    branch_back(width, slots, grad, z2, picked, seg_row_ref[...], mod_ref, dz2_ref, dgate_ref)


def middle_back_kernel(width, slots, terms, *refs):
    sums = refs[:terms]
    h1_ref, c_ref, z1_ref, seg_ref, seg_row_ref, mod_ref = refs[terms : terms + 6]
    dh1_ref, dz1_ref, dgate_ref, dshift_ref, dscale_ref = refs[terms + 6 :]
    picked = slot_pick(seg_ref[...])
    seg_row = seg_row_ref[...]
    da2 = total(sums)
    norm, inverse = normed(h1_ref[...])
    dshift_ref[...] = slot_sums(seg_row, slots, da2)
    dscale_ref[...] = slot_sums(seg_row, slots, da2 * norm)
    d_norm = da2 * (1.0 + part_of(picked, mod_ref, 4, width))
    dh1 = c_ref[...].astype(f32) + norm_back(norm, inverse, d_norm)
    dh1_ref[...] = dh1
    dz1_ref[...] = (dh1 * part_of(picked, mod_ref, 2, width)).astype(bf16)
    dgate_ref[...] = slot_sums(seg_row, slots, dh1 * z1_ref[...].astype(f32))


def layer_back_kernel(width, slots, terms, more, *refs):
    sums = refs[:terms]
    h_ref, dh1_ref, seg_ref, seg_row_ref, mod_ref = refs[terms : terms + 5]
    rest = refs[terms + 5 :]
    if more:
        z2_ref, before_ref = rest[:2]
        rest = rest[2:]
    g_ref, dshift_ref, dscale_ref = rest[:3]
    picked = slot_pick(seg_ref[...])
    seg_row = seg_row_ref[...]
    da1 = total(sums)
    norm, inverse = normed(h_ref[...].astype(f32))
    dshift_ref[...] = slot_sums(seg_row, slots, da1)
    dscale_ref[...] = slot_sums(seg_row, slots, da1 * norm)
    d_norm = da1 * (1.0 + part_of(picked, mod_ref, 1, width))
    grad = (dh1_ref[...] + norm_back(norm, inverse, d_norm)).astype(bf16)
    g_ref[...] = grad
    if more:
        branch_back(
            width,
            slots,
            grad.astype(f32),
            z2_ref[...].astype(f32),
            picked,
            seg_row,
            before_ref,
            *rest[3:],
        )


def turned(values, cos, sin):
    groups = []
    for start in range(0, values.shape[1], 128):
        part = values[:, start : start + 128]
        lane = lax.broadcasted_iota(jnp.int32, part.shape, 1)
        other = jnp.where(lane % 2 == 0, pltpu.roll(part, 127, 1), pltpu.roll(part, 1, 1))
        groups.append(part * cos + other * sin)
    return groups[0] if len(groups) == 1 else jnp.concatenate(groups, axis=1)


def head_mask(lane, head):
    return (lane >= head * HEAD_DIM) & (lane < (head + 1) * HEAD_DIM)


def attend_kernel(blocks, *refs):
    x_refs = refs[:blocks]
    (
        w_ref,
        bias_ref,
        cos_ref,
        sin_ref,
        seg_ref,
        seg_row_ref,
        w_out_ref,
        q_ref,
        k_ref,
        v_ref,
        o_ref,
        lse_ref,
    ) = refs[blocks : blocks + 12]
    part_refs = refs[blocks + 12 :]
    rows, width = x_refs[0].shape
    groups, _, local = w_out_ref.shape[0], 0, w_ref.shape[2]
    depth = width // groups
    heads = local // HEAD_DIM
    weights = [w_ref[:, p * depth : (p + 1) * depth, :].reshape(width, local) for p in range(3)]
    for j in range(blocks):
        here = slice(j * rows, (j + 1) * rows)
        x = x_refs[j][...]
        cos, sin = cos_ref[here, :], sin_ref[here, :]
        q = turned(mm(x, weights[0]) + bias_ref[0:1, :], cos, sin)
        q_ref[here, :] = (q.astype(bf16).astype(f32) * (HEAD_DIM**-0.5)).astype(bf16)
        k_ref[here, :] = turned(mm(x, weights[1]) + bias_ref[1:2, :], cos, sin).astype(bf16)
        v_ref[here, :] = (mm(x, weights[2]) + bias_ref[2:3, :]).astype(bf16)

    def one_block(i, carry):
        here = pl.ds(pl.multiple_of(i * rows, rows), rows)
        q = q_ref[here, :]
        allowed = seg_ref[here, :] == seg_row_ref[...]
        lane = lax.broadcasted_iota(jnp.int32, (rows, local), 1)
        wide_lane = lax.broadcasted_iota(jnp.int32, (rows, 128), 1)
        mixed = jnp.zeros((rows, local), f32)
        lse = jnp.zeros((rows, 128), f32)
        for head in range(heads):
            mine = head_mask(lane, head)
            scores = mm_last(jnp.where(mine, q, jnp.zeros_like(q)), k_ref[...])
            scores = jnp.where(allowed, scores, big_negative)
            top = jnp.max(scores, axis=-1, keepdims=True)
            weight = jnp.exp(scores - top)
            weight_sum = jnp.sum(weight, axis=-1, keepdims=True)
            mixed = jnp.where(mine, mm(weight.astype(bf16), v_ref[...]) / weight_sum, mixed)
            lse = jnp.where(wide_lane == head, top + jnp.log(weight_sum), lse)
        o_ref[here, :] = mixed.astype(bf16)
        lse_ref[here, :] = lse
        return carry

    lax.fori_loop(0, blocks, one_block, 0)
    for j in range(blocks):
        mixed = o_ref[j * rows : (j + 1) * rows, :]
        for g in range(groups):
            part_refs[j][:, g * depth : (g + 1) * depth] = mm(mixed, w_out_ref[g]).astype(bf16)


def attend_back_kernel(blocks, *refs):
    dz_refs = refs[:blocks]
    (
        w_ref,
        w_out_ref,
        q_ref,
        k_ref,
        v_ref,
        lse_ref,
        cos_ref,
        sin_ref,
        seg_ref,
        seg_row_ref,
        dq_ref,
        dk_ref,
        dv_ref,
    ) = refs[blocks : blocks + 13]
    part_refs = refs[blocks + 13 : 2 * blocks + 13]
    do_ref, dk_sum, dv_sum = refs[2 * blocks + 13 :]
    rows, width = dz_refs[0].shape
    groups, local = w_out_ref.shape[0], w_ref.shape[2]
    depth = width // groups
    heads = local // HEAD_DIM
    scale = HEAD_DIM**-0.5
    for j in range(blocks):
        value = jnp.zeros((rows, local), f32)
        for g in range(groups):
            value = value + mm_last(dz_refs[j][:, g * depth : (g + 1) * depth], w_out_ref[g])
        do_ref[j * rows : (j + 1) * rows, :] = value.astype(bf16)
    dk_sum[...] = jnp.zeros_like(dk_sum)
    dv_sum[...] = jnp.zeros_like(dv_sum)

    def one_block(i, carry):
        here = pl.ds(pl.multiple_of(i * rows, rows), rows)
        q, do = q_ref[here, :], do_ref[here, :]
        lse = lse_ref[here, :]
        allowed = seg_ref[here, :] == seg_row_ref[...]
        lane = lax.broadcasted_iota(jnp.int32, (rows, local), 1)
        dq = jnp.zeros((rows, local), f32)
        for head in range(heads):
            mine = head_mask(lane, head)
            q_head = jnp.where(mine, q, jnp.zeros_like(q))
            do_head = jnp.where(mine, do, jnp.zeros_like(do))
            scores = mm_last(q_head, k_ref[...])
            prob = jnp.exp(jnp.where(allowed, scores, big_negative) - lse[:, head : head + 1])
            d_prob = mm_last(do_head, v_ref[...])
            product = prob * d_prob
            centre = jnp.sum(product, axis=-1, keepdims=True)
            d_scores = (product - prob * centre).astype(bf16)
            dv_sum[...] += mm_first(prob.astype(bf16), do_head)
            dk_sum[...] += mm_first(d_scores, q_head)
            dq = jnp.where(mine, mm(d_scores, k_ref[...]), dq)
        dq_ref[here, :] = turned(dq * scale, cos_ref[here, :], -sin_ref[here, :]).astype(bf16)
        return carry

    lax.fori_loop(0, blocks, one_block, 0)
    weights = [w_ref[:, p * depth : (p + 1) * depth, :].reshape(width, local) for p in range(3)]
    for j in range(blocks):
        here = slice(j * rows, (j + 1) * rows)
        dk = turned(dk_sum[here, :], cos_ref[here, :], -sin_ref[here, :]).astype(bf16)
        dv = dv_sum[here, :].astype(bf16)
        dk_ref[here, :] = dk
        dv_ref[here, :] = dv
        part_refs[j][...] = (
            mm_last(dq_ref[here, :], weights[0]) + mm_last(dk, weights[1]) + mm_last(dv, weights[2])
        ).astype(bf16)


def feed_kernel(blocks, *refs):
    a_refs = refs[:blocks]
    w_up_ref, bias_ref, w_down_ref, u_ref, g_ref = refs[blocks : blocks + 5]
    part_refs = refs[blocks + 5 :]
    rows, width = a_refs[0].shape
    groups, units, depth = w_down_ref.shape
    w_up = w_up_ref[...].reshape(width, units)
    for j in range(blocks):
        here = slice(j * rows, (j + 1) * rows)
        u = mm(a_refs[j][...], w_up) + bias_ref[...]
        u_ref[here, :] = u
        inner = math.sqrt(2.0 / math.pi) * (u + 0.044715 * (u * u * u))
        g = (0.5 * u * (1.0 + jnp.tanh(inner))).astype(bf16)
        g_ref[here, :] = g
        for k in range(groups):
            part_refs[j][:, k * depth : (k + 1) * depth] = mm(g, w_down_ref[k]).astype(bf16)


def feed_back_kernel(blocks, *refs):
    dz_refs = refs[:blocks]
    w_up_ref, w_down_ref, u_ref, du_ref = refs[blocks : blocks + 4]
    part_refs = refs[blocks + 4 :]
    rows, width = dz_refs[0].shape
    groups, units, depth = w_down_ref.shape
    w_up = w_up_ref[...].reshape(width, units)
    root = math.sqrt(2.0 / math.pi)
    for j in range(blocks):
        here = slice(j * rows, (j + 1) * rows)
        dg = jnp.zeros((rows, units), f32)
        for k in range(groups):
            dg = dg + mm_last(dz_refs[j][:, k * depth : (k + 1) * depth], w_down_ref[k])
        u = u_ref[here, :]
        square = u * u
        th = jnp.tanh(root * u * (1.0 + 0.044715 * square))
        slope = 0.5 * (1.0 + th) + 0.5 * u * (1.0 - th * th) * (root * (1.0 + 0.134145 * square))
        du = (dg * slope).astype(bf16)
        du_ref[here, :] = du
        part_refs[j][...] = mm_last(du, w_up).astype(bf16)


def feed_grads_kernel(blocks, *refs):
    a_refs, dz_refs = refs[:blocks], refs[blocks : 2 * blocks]
    g_ref, du_ref, up_ref, down_ref, bias_up_ref, bias_down_ref = refs[2 * blocks :]
    rows = a_refs[0].shape[0]
    groups, units, depth = down_ref.shape
    dz = jnp.concatenate([ref[...] for ref in dz_refs], axis=0)
    a2 = jnp.concatenate([ref[...] for ref in a_refs], axis=0)
    for k in range(groups):
        here = slice(k * depth, (k + 1) * depth)
        down_ref[k] = mm_first(g_ref[...], dz[:, here]).astype(bf16)
        up_ref[k] = mm_first(a2[:, here], du_ref[...]).astype(bf16)
    ones = jnp.ones((SLOT_ROWS, rows * blocks), bf16)
    bias_up_ref[...] = mm(ones, du_ref[...])
    bias_down_ref[...] = mm(ones, dz)


def out_grads_kernel(blocks, *refs):
    dz_refs = refs[:blocks]
    o_ref, out_ref, bias_ref = refs[blocks:]
    rows = dz_refs[0].shape[0]
    groups, _, depth = out_ref.shape
    dz = jnp.concatenate([ref[...] for ref in dz_refs], axis=0)
    for k in range(groups):
        out_ref[k] = mm_first(o_ref[...], dz[:, k * depth : (k + 1) * depth]).astype(bf16)
    bias_ref[...] = mm(jnp.ones((SLOT_ROWS, rows * blocks), bf16), dz)


def qkv_grads_kernel(blocks, *refs):
    a_refs = refs[:blocks]
    dq_ref, dk_ref, dv_ref, w_ref, bias_ref = refs[blocks:]
    rows = a_refs[0].shape[0]
    groups, packed, _ = w_ref.shape
    depth = a_refs[0].shape[1] // groups
    a1 = jnp.concatenate([ref[...] for ref in a_refs], axis=0)
    ones = jnp.ones((SLOT_ROWS, rows * blocks), bf16)
    for p, ref in enumerate((dq_ref, dk_ref, dv_ref)):
        bias_ref[p] = mm(ones, ref[...])
        for k in range(groups):
            w_ref[k, p * depth : (p + 1) * depth, :] = mm_first(
                a1[:, k * depth : (k + 1) * depth], ref[...]
            ).astype(bf16)


def per_device(
    endpoints,
    lengths,
    timesteps,
    w_qkv,
    b_qkv,
    w_out,
    b_out,
    w_up,
    b_up,
    w_down,
    b_down,
    w_mod,
    b_mod,
):
    section = lax.axis_index("section")
    tensor = lax.axis_index("tensor")
    group = lax.axis_index("dp")
    tensors, groups = lax.axis_size("tensor"), lax.axis_size("dp")
    micros, rows, width = endpoints.shape[1], endpoints.shape[3], endpoints.shape[4]
    slots = lengths.shape[2]
    frames = rows * tensors
    depth = width // groups
    local = w_qkv.shape[3]
    units = w_up.shape[2]
    first = section == 0
    terms = len(list(bits_of(tensors))) + 1

    def pick(here, other):
        return jnp.where(first, here, other), jnp.where(first, other, here)

    kept = lax.dynamic_index_in_dim(endpoints[0, :, 0], section, 0, keepdims=False)
    given = lax.dynamic_index_in_dim(endpoints[0, :, 0], 1 - section, 0, keepdims=False)
    taken = swap(given, "section", 1)
    h0, cotangent = jnp.where(first, kept, taken), jnp.where(first, taken, kept)

    def lane_row(vector):
        flat = vector.reshape(-1, vector.shape[-1])
        return jnp.pad(flat, ((0, 0), (0, local - flat.shape[1])))

    qkv_pack = jnp.concatenate(
        [
            w_qkv[0].reshape(3 * depth, local),
            lane_row(b_qkv[0]),
            lane_row(b_out),
            lane_row(b_up),
            lane_row(b_down),
            jnp.zeros((2, local), bf16),
        ],
        axis=0,
    )
    shards = [qkv_pack, w_out[0], w_up[0], w_down[0]]
    layer_shards = [pick(shard, swap(shard, "section", 1)) for shard in shards]
    full = []
    for layer in range(2):
        full.append([gather_groups(shard[layer]) for shard in layer_shards])

    def biases(layer):
        tail = full[layer][0][:, 3 * depth :, :].astype(f32)
        qkv = tail[:, :3, : local // groups].transpose(1, 0, 2).reshape(3, local)
        out = tail[:, 3, :depth].reshape(1, width)
        up = tail[:, 4, : units // groups].reshape(1, units)
        down = tail[:, 5, :depth].reshape(1, width)
        return jnp.pad(qkv, ((0, SLOT_ROWS - 3), (0, 0))), out, up, down

    steps = jnp.pad(timesteps[:, 0], ((0, 0), (0, SLOT_ROWS - slots)))
    all_steps = jnp.stack(
        [steps] + [swap(steps, "dp", j) for j in range(1, groups)]
    )
    column = group * depth + jnp.arange(depth, dtype=jnp.int32)
    half = width // 2
    frequency = jnp.exp((column % half).astype(f32) * (-math.log(10000.0) / (half - 1)))
    angle = all_steps.astype(f32)[..., None] * frequency
    codes = jax.nn.silu(jnp.where(column < half, jnp.sin(angle), jnp.cos(angle))).astype(bf16)
    mod_width = w_mod.shape[2]
    strip = mod_width // tensors
    strip_start = tensor * strip
    bias_all = lax.dynamic_update_slice(
        jnp.zeros((mod_width,), f32), b_mod[0].astype(f32), (group * b_mod.shape[1],)
    )
    mod_part = jnp.einsum(
        "zmud,de->zmue",
        codes,
        lax.dynamic_slice_in_dim(w_mod[0], strip_start, strip, 1),
        preferred_element_type=f32,
    ) + lax.dynamic_slice_in_dim(bias_all, strip_start, strip)
    mine = lax.dynamic_index_in_dim(mod_part, section, 1, keepdims=False)
    other = swap(
        lax.dynamic_index_in_dim(mod_part, 1 - section, 1, keepdims=False), "section", 1
    )
    both = jnp.stack(pick(mine, other), axis=1)
    mod_strip = both[0]
    for j in range(1, groups):
        mod_strip = mod_strip + swap(both[j], "dp", j)
    mod_all = jnp.zeros((2, SLOT_ROWS, tensors, strip), f32)
    for j, block in enumerate(gather_rows(mod_strip)):
        mod_all = lax.dynamic_update_slice(mod_all, block[:, :, None], (0, 0, tensor ^ j, 0))
    live_slots = jnp.arange(SLOT_ROWS) < slots
    mod_all = jnp.where(
        live_slots[None, :, None], mod_all.reshape(2, SLOT_ROWS, mod_width), 0.0
    )

    lengths_here = lax.dynamic_index_in_dim(lengths[:, 0], section, 0, keepdims=False)
    block_index = tensor ^ jnp.arange(tensors, dtype=jnp.int32)
    frame = (block_index[:, None] * rows + jnp.arange(rows, dtype=jnp.int32)).reshape(-1)
    ends = jnp.cumsum(lengths_here)
    segment = jnp.sum((frame[:, None] >= ends[None, :]).astype(jnp.int32), axis=1)
    member = segment[:, None] == jnp.arange(slots, dtype=jnp.int32)[None, :]
    begin = jnp.sum(jnp.where(member, (ends - lengths_here)[None, :], 0), axis=1)
    position = (frame - begin).astype(f32)
    lane = jnp.arange(128, dtype=jnp.int32) % HEAD_DIM
    inverse = jnp.exp((lane // 2).astype(f32) * (-2.0 * math.log(10000.0) / HEAD_DIM))
    angles = position[:, None] * inverse[None, :]
    cos_table = jnp.cos(angles)
    sin_table = jnp.sin(angles) * jnp.where(lane % 2 == 0, -1.0, 1.0)
    seg_col, seg_row = segment[:, None], segment[None, :]
    own_col, own_row = seg_col[:rows], seg_row[:, :rows]

    frame_block = shape((rows, width), bf16)
    frame_block32 = shape((rows, width), f32)
    wide_local = shape((frames, local), bf16)
    slot_block = shape((SLOT_ROWS, width), f32)
    project = 2 * frames * width * local

    (a1,) = call(
        functools.partial(first_norm_kernel, width), [frame_block], h0, own_col, mod_all[0]
    )
    layer_in = h0
    saved = []
    outputs = []
    for layer in range(2):
        packed, w_out_all, w_up_all, w_down_all = full[layer]
        bias_qkv, bias_out, bias_up, bias_down = biases(layer)
        a1_all = gather_rows(a1)
        q, k, v, o, lse, *parts = call(
            functools.partial(attend_kernel, tensors),
            [wide_local] * 4 + [shape((frames, 128), f32)] + [frame_block] * tensors,
            *a1_all,
            packed,
            bias_qkv,
            cos_table,
            sin_table,
            seg_col,
            seg_row,
            w_out_all,
            flops=4 * project + 8 * frames * frames * local,
        )
        z1, h1, a2 = call(
            functools.partial(middle_kernel, width, terms),
            [frame_block, frame_block32, frame_block],
            *scatter_rows(parts),
            layer_in,
            bias_out,
            own_col,
            mod_all[layer],
        )
        a2_all = gather_rows(a2)
        u, g, *parts = call(
            functools.partial(feed_kernel, tensors),
            [shape((frames, units), f32), shape((frames, units), bf16)] + [frame_block] * tensors,
            *a2_all,
            w_up_all,
            bias_up,
            w_down_all,
            flops=4 * frames * width * units,
        )
        sums = scatter_rows(parts)
        kept_state = [layer_in, a1_all, q, k, v, o, lse, z1, h1, a2_all, u, g]
        if layer == 0:
            z2, y, a1 = call(
                functools.partial(layer_end_kernel, width, terms),
                [frame_block] * 3,
                *sums,
                h1,
                bias_down,
                own_col,
                mod_all[layer],
                mod_all[layer + 1],
            )
            layer_in = y
        else:
            z2 = None
            y, grad, dz2, dgate_b = call(
                functools.partial(turn_kernel, width, slots, terms),
                [frame_block, frame_block, frame_block, slot_block],
                *sums,
                h1,
                bias_down,
                own_col,
                own_row,
                mod_all[layer],
                cotangent,
            )
        outputs.append(y)
        saved.append(kept_state + [z2])

    grads = [None, None]
    in_grads = [None, None]
    d_mods = [None, None]
    for layer in (1, 0):
        packed, w_out_all, w_up_all, w_down_all = full[layer]
        layer_in, a1_all, q, k, v, o, lse, z1, h1, a2_all, u, g, _ = saved[layer]
        dz2_all = gather_rows(dz2)
        du, *parts = call(
            functools.partial(feed_back_kernel, tensors),
            [shape((frames, units), bf16)] + [frame_block] * tensors,
            *dz2_all,
            w_up_all,
            w_down_all,
            u,
            flops=4 * frames * width * units,
        )
        sums = scatter_rows(parts)
        d_up, d_down, d_bias_up, d_bias_down = call(
            functools.partial(feed_grads_kernel, tensors),
            [
                shape((groups, depth, units), bf16),
                shape((groups, units, depth), bf16),
                shape((SLOT_ROWS, units), f32),
                shape((SLOT_ROWS, width), f32),
            ],
            *a2_all,
            *dz2_all,
            g,
            du,
            flops=4 * frames * width * units,
        )
        dh1, dz1, dgate_a, dshift_b, dscale_b = call(
            functools.partial(middle_back_kernel, width, slots, terms),
            [frame_block32, frame_block] + [slot_block] * 3,
            *sums,
            h1,
            grad,
            z1,
            own_col,
            own_row,
            mod_all[layer],
        )
        dz1_all = gather_rows(dz1)
        dq, dk, dv, *parts = call(
            functools.partial(attend_back_kernel, tensors),
            [wide_local] * 3 + [frame_block] * tensors,
            *dz1_all,
            packed,
            w_out_all,
            q,
            k,
            v,
            lse,
            cos_table,
            sin_table,
            seg_col,
            seg_row,
            scratch=[
                pltpu.VMEM((frames, local), bf16),
                pltpu.VMEM((frames, local), f32),
                pltpu.VMEM((frames, local), f32),
            ],
            flops=4 * project + 20 * frames * frames * local,
        )
        sums = scatter_rows(parts)
        d_out, d_bias_out = call(
            functools.partial(out_grads_kernel, tensors),
            [shape((groups, local, depth), bf16), shape((SLOT_ROWS, width), f32)],
            *dz1_all,
            o,
            flops=project,
        )
        d_qkv, d_bias_qkv = call(
            functools.partial(qkv_grads_kernel, tensors),
            [shape((groups, 3 * depth, local), bf16), shape((3, SLOT_ROWS, local), f32)],
            *a1_all,
            dq,
            dk,
            dv,
            flops=3 * project,
        )
        kernel = functools.partial(layer_back_kernel, width, slots, terms, layer > 0)
        arrays = [*sums, layer_in, dh1, own_col, own_row, mod_all[layer]]
        if layer > 0:
            grad_out, dshift_a, dscale_a, dz2, next_dgate = call(
                kernel,
                [frame_block, slot_block, slot_block, frame_block, slot_block],
                *arrays,
                saved[layer - 1][-1],
                mod_all[layer - 1],
            )
        else:
            grad_out, dshift_a, dscale_a = call(
                kernel, [frame_block, slot_block, slot_block], *arrays
            )
            next_dgate = None
        grad = grad_out
        in_grads[layer] = grad_out
        d_mods[layer] = jnp.concatenate(
            [dshift_a, dscale_a, dgate_a, dshift_b, dscale_b, dgate_b], axis=1
        )
        dgate_b = next_dgate

        def by_group(vector, count):
            return jnp.pad(
                vector.reshape(groups, 1, count), ((0, 0), (0, 0), (0, local - count))
            )

        bias_rows = jnp.concatenate(
            [by_group(d_bias_qkv[p, 0], local // groups) for p in range(3)]
            + [
                by_group(d_bias_out[0], depth),
                by_group(d_bias_up[0], units // groups),
                by_group(d_bias_down[0], depth),
                jnp.zeros((groups, 2, local), f32),
            ],
            axis=1,
        ).astype(bf16)
        grads[layer] = [
            lax.psum_scatter(value, "dp", scatter_dimension=0, tiled=False)
            for value in (
                d_up,
                d_down,
                d_out,
                jnp.concatenate([d_qkv, bias_rows], axis=1),
            )
        ]

    def to_section(pair):
        low, high = pair
        up = lax.ppermute(high, "section", [(0, 1)])
        down = lax.ppermute(low, "section", [(1, 0)])
        return jnp.where(
            first,
            low.astype(f32) + down.astype(f32),
            high.astype(f32) + up.astype(f32),
        )

    def frames_out(pair):
        low, high = pair
        arrived = lax.ppermute(high, "section", [(0, 1)]) + lax.ppermute(
            low, "section", [(1, 0)]
        )
        own = jnp.where(first, low, high)
        return jnp.where(first, jnp.stack([own, arrived]), jnp.stack([arrived, own]))

    activations = frames_out(outputs)
    input_grads = frames_out(in_grads)
    g_up, g_down, g_out, g_qkv = [to_section(pair) for pair in zip(*grads, strict=True)]
    tail = g_qkv[3 * depth :]

    def strips(value):
        return [
            lax.dynamic_slice_in_dim(value, (tensor ^ j) * strip, strip, 1) for j in range(tensors)
        ]

    own_mod = []
    for layer in range(2):
        added = scatter_rows(strips(d_mods[layer]))
        own_mod.append(functools.reduce(jnp.add, added))
    low, high = own_mod
    arrived = lax.ppermute(high, "section", [(0, 1)]) + lax.ppermute(low, "section", [(1, 0)])
    pair = jnp.stack([jnp.where(first, low, high), arrived]).astype(bf16)
    pairs = jnp.stack([pair] + [swap(pair, "dp", j) for j in range(1, groups)])
    d_mod = jnp.zeros((groups, micros, SLOT_ROWS, tensors, strip), bf16)
    for j, block in enumerate(gather_rows(pairs)):
        d_mod = lax.dynamic_update_slice(d_mod, block[:, :, :, None], (0, 0, 0, tensor ^ j, 0))
    d_mod = d_mod.reshape(groups * micros * SLOT_ROWS, mod_width)
    own_first = jnp.where(first, codes, codes[:, ::-1]).reshape(-1, depth)
    g_wmod = lax.dot_general(
        own_first, d_mod, (((0,), (0,)), ((), ())), preferred_element_type=f32
    )
    g_bmod = jnp.sum(
        lax.dynamic_slice_in_dim(d_mod, group * b_mod.shape[1], b_mod.shape[1], 1).astype(f32),
        axis=0,
    )
    return (
        activations[None, :, None],
        input_grads[None, :, None],
        g_qkv[: 3 * depth].reshape(1, 3, depth, local),
        tail[:3, : local // groups][None],
        g_out[None],
        tail[3:4, :depth],
        g_up[None],
        tail[4:5, : units // groups],
        g_down[None],
        tail[5:6, :depth],
        g_wmod[None],
        g_bmod[None],
    )


def solution(mesh):
    return jax.shard_map(
        per_device,
        mesh=mesh,
        in_specs=(
            P("section", None, "dp", "tensor", None),
            P(None, "dp", None),
            P(None, "dp", None),
            P("section", None, "dp", "tensor"),
            P("section", None, ("tensor", "dp")),
            P("section", "tensor", "dp"),
            P("section", "dp"),
            P("section", "dp", "tensor"),
            P("section", ("tensor", "dp")),
            P("section", "tensor", "dp"),
            P("section", "dp"),
            P("section", "dp", None),
            P("section", "dp"),
        ),
        out_specs=(
            P("section", None, "dp", "tensor", None),
            P("section", None, "dp", "tensor", None),
            P("section", None, "dp", "tensor"),
            P("section", None, ("tensor", "dp")),
            P("section", "tensor", "dp"),
            P("section", "dp"),
            P("section", "dp", "tensor"),
            P("section", ("tensor", "dp")),
            P("section", "tensor", "dp"),
            P("section", "dp"),
            P("section", "dp", None),
            P("section", "dp"),
        ),
        check_vma=False,
    )
```

```python
import functools
import math

import jax
import jax.numpy as jnp
from jax import lax
from jax.experimental import pallas as pl
from jax.experimental.pallas import tpu as pltpu
from jax.sharding import PartitionSpec as P

HEAD_DIM = 64
SLOT_ROWS = 8
norm_eps = 1e-06
big_negative = -1e30
f32 = jnp.float32
bf16 = jnp.bfloat16
vmem_limit = 52 * 1024 * 1024


def swap(block, axis, bit):
    return lax.ppermute(block, axis, [(i, i ^ bit) for i in range(lax.axis_size(axis))])


def after(value, *others):
    return lax.optimization_barrier((value, *others))[0]


def bits_of(count):
    bit = 1
    while bit < count:
        yield bit
        bit *= 2


def gather_near(block):
    blocks = {0: block}
    for bit in reversed(list(bits_of(lax.axis_size("tensor") // 2))):
        blocks.update({j | bit: swap(part, "tensor", bit) for j, part in list(blocks.items())})
    return [blocks[j] for j in range(len(blocks))]


def cross(block):
    return swap(block, "tensor", lax.axis_size("tensor") // 2)


def gather_rows(block):
    far = cross(block)
    return gather_near(block) + gather_near(far)


def reduce_rows(parts, bits):
    kept = dict(enumerate(parts))
    addends = [parts[0]]
    for bit in bits:
        arrived = {j: swap(kept[j | bit], "tensor", bit) for j in kept if not j & bit}
        addends.append(arrived.pop(0))
        kept = {
            0: parts[0],
            **{
                j: (kept[j].astype(f32) + part.astype(f32)).astype(parts[0].dtype)
                for j, part in arrived.items()
            },
        }
    return addends


def near_sum(parts):
    near = reduce_rows(parts, list(bits_of(len(parts))))
    summed = functools.reduce(jnp.add, [part.astype(f32) for part in near])
    return summed.astype(parts[0].dtype)


def scatter_near(parts):
    return reduce_rows(parts, list(bits_of(len(parts))))


def absolute(blocks, index):
    for bit in bits_of(len(blocks)):
        blocks = [
            jnp.where(index & bit, blocks[b ^ bit], blocks[b]) for b in range(len(blocks))
        ]
    return blocks


def gather_groups(block):
    return lax.all_gather(block, "dp", axis=0, tiled=False)


def tie(*values):
    return lax.optimization_barrier(values)


class Half:
    def __init__(self, array, index):
        self.array, self.index = array, index


def spec_of(arg):
    if isinstance(arg, Half):
        dims = arg.array.shape
        place = (arg.index,) + (0,) * (len(dims) - 1)
        return pl.BlockSpec((dims[0] // 2, *dims[1:]), lambda i: place)
    return pl.BlockSpec(memory_space=pltpu.VMEM)


def call(name, body, outs, *args, scratch=(), flops=0):
    whole = pl.BlockSpec(memory_space=pltpu.VMEM)
    grid = {"grid": (1,)} if any(isinstance(arg, Half) for arg in args) else {}
    return pl.pallas_call(
        body,
        in_specs=[spec_of(arg) for arg in args],
        out_specs=(whole,) * len(outs),
        **grid,
        out_shape=tuple(outs),
        name=name,
        scratch_shapes=scratch,
        compiler_params=pltpu.CompilerParams(vmem_limit_bytes=vmem_limit),
        cost_estimate=pl.CostEstimate(flops=flops, bytes_accessed=0, transcendentals=0),
    )(*[arg.array if isinstance(arg, Half) else arg for arg in args])


def shape(dims, dtype):
    return jax.ShapeDtypeStruct(dims, dtype)


def mm(left, right):
    return lax.dot_general(left, right, (((1,), (0,)), ((), ())), preferred_element_type=f32)


def mm_last(left, right):
    return lax.dot_general(left, right, (((1,), (1,)), ((), ())), preferred_element_type=f32)


def mm_first(left, right):
    return lax.dot_general(left, right, (((0,), (0,)), ((), ())), preferred_element_type=f32)


def slot_pick(seg_col):
    rows = seg_col.shape[0]
    lane = lax.broadcasted_iota(jnp.int32, (rows, SLOT_ROWS), 1)
    return (lane == seg_col).astype(f32).astype(bf16)


def part_of(picked, mod_ref, index, width):
    values = mod_ref[:, index * width : (index + 1) * width]
    high = values.astype(bf16)
    rest = (values - high.astype(f32)).astype(bf16)
    return mm(picked, high) + mm(picked, rest)


def slot_sums(seg_row, slots, values):
    row = lax.broadcasted_iota(jnp.int32, (SLOT_ROWS, seg_row.shape[1]), 0)
    picked = ((row == seg_row) & (row < slots)).astype(f32).astype(bf16)
    return mm(picked, values.astype(bf16))


def normed(values):
    centre = values - jnp.mean(values, axis=-1, keepdims=True)
    spread = jnp.mean(centre * centre, axis=-1, keepdims=True)
    inverse = lax.rsqrt(spread + norm_eps)
    return centre * inverse, inverse


def norm_back(norm, inverse, d_norm):
    mean_d = jnp.mean(d_norm, axis=-1, keepdims=True)
    mean_dn = jnp.mean(d_norm * norm, axis=-1, keepdims=True)
    return inverse * (d_norm - mean_d - norm * mean_dn)


def total(refs):
    value = refs[0][...].astype(f32)
    for ref in refs[1:]:
        value = value + ref[...].astype(f32)
    return value


def first_norm_kernel(width, blocks, *refs):
    seg_ref, mod_ref = refs[blocks : blocks + 2]
    rows = refs[0].shape[0]
    for j in range(blocks):
        picked = slot_pick(seg_ref[j * rows : (j + 1) * rows, :])
        norm, _ = normed(refs[j][...].astype(f32))
        scale = part_of(picked, mod_ref, 1, width)
        shift = part_of(picked, mod_ref, 0, width)
        refs[blocks + 2 + j][...] = (norm * (1.0 + scale) + shift).astype(bf16)


def middle_kernel(width, terms, *refs):
    sums = refs[:terms]
    h_ref, bias_ref, seg_ref, mod_ref, z1_ref, h1_ref, a2_ref = refs[terms:]
    picked = slot_pick(seg_ref[...])
    z1 = total(sums) + bias_ref[...]
    z1_ref[...] = z1.astype(bf16)
    h1 = h_ref[...].astype(f32) + part_of(picked, mod_ref, 2, width) * z1
    h1_ref[...] = h1
    norm, _ = normed(h1)
    a2_ref[...] = (
        norm * (1.0 + part_of(picked, mod_ref, 4, width)) + part_of(picked, mod_ref, 3, width)
    ).astype(bf16)


def layer_end_kernel(width, terms, *refs):
    sums = refs[:terms]
    h1_ref, bias_ref, seg_ref, mod_ref, next_ref, z2_ref, y_ref, a1_ref = refs[terms:]
    picked = slot_pick(seg_ref[...])
    z2 = total(sums) + bias_ref[...]
    z2_ref[...] = z2.astype(bf16)
    y = (h1_ref[...] + part_of(picked, mod_ref, 5, width) * z2).astype(bf16)
    y_ref[...] = y
    norm, _ = normed(y.astype(f32))
    a1_ref[...] = (
        norm * (1.0 + part_of(picked, next_ref, 1, width)) + part_of(picked, next_ref, 0, width)
    ).astype(bf16)


def column_sums(values):
    return mm(jnp.ones((SLOT_ROWS, values.shape[0]), bf16), values)


def branch_back(width, slots, grad, z2, picked, seg_row, mod_ref, dz2_ref, dgate_ref, bias_ref):
    dz2 = (grad * part_of(picked, mod_ref, 5, width)).astype(bf16)
    dz2_ref[...] = dz2
    dgate_ref[...] = slot_sums(seg_row, slots, grad * z2)
    bias_ref[...] = column_sums(dz2)


def turn_kernel(width, slots, terms, *refs):
    sums = refs[:terms]
    (h1_ref, bias_ref, seg_ref, seg_row_ref, mod_ref, cot_ref) = refs[terms : terms + 6]
    y_ref, c_ref = refs[terms + 6 : terms + 8]
    seg = seg_ref[...]
    picked = slot_pick(seg)
    z2 = total(sums) + bias_ref[...]
    y_ref[...] = (h1_ref[...] + part_of(picked, mod_ref, 5, width) * z2).astype(bf16)
    grad = jnp.where(seg < slots, cot_ref[...].astype(f32), 0.0)
    c_ref[...] = grad.astype(bf16)
    branch_back(width, slots, grad, z2, picked, seg_row_ref[...], mod_ref, *refs[terms + 8 :])


def middle_back_kernel(width, slots, terms, *refs):
    sums = refs[:terms]
    h1_ref, c_ref, z1_ref, seg_ref, seg_row_ref, mod_ref = refs[terms : terms + 6]
    dh1_ref, dz1_ref, d_mod_ref, bias_ref = refs[terms + 6 :]
    picked = slot_pick(seg_ref[...])
    seg_row = seg_row_ref[...]
    da2 = total(sums)
    norm, inverse = normed(h1_ref[...])
    d_mod_ref[:, width : 2 * width] = slot_sums(seg_row, slots, da2)
    d_mod_ref[:, 2 * width :] = slot_sums(seg_row, slots, da2 * norm)
    d_norm = da2 * (1.0 + part_of(picked, mod_ref, 4, width))
    dh1 = c_ref[...].astype(f32) + norm_back(norm, inverse, d_norm)
    dh1_ref[...] = dh1
    dz1 = (dh1 * part_of(picked, mod_ref, 2, width)).astype(bf16)
    dz1_ref[...] = dz1
    d_mod_ref[:, :width] = slot_sums(seg_row, slots, dh1 * z1_ref[...].astype(f32))
    bias_ref[...] = column_sums(dz1)


def layer_back_kernel(width, slots, terms, more, *refs):
    sums = refs[:terms]
    h_ref, dh1_ref, seg_ref, seg_row_ref, mod_ref = refs[terms : terms + 5]
    rest = refs[terms + 5 :]
    if more:
        z2_ref, before_ref = rest[:2]
        rest = rest[2:]
    g_ref, d_mod_ref = rest[:2]
    picked = slot_pick(seg_ref[...])
    seg_row = seg_row_ref[...]
    da1 = total(sums)
    norm, inverse = normed(h_ref[...].astype(f32))
    d_mod_ref[:, :width] = slot_sums(seg_row, slots, da1)
    d_mod_ref[:, width:] = slot_sums(seg_row, slots, da1 * norm)
    d_norm = da1 * (1.0 + part_of(picked, mod_ref, 1, width))
    grad = (dh1_ref[...] + norm_back(norm, inverse, d_norm)).astype(bf16)
    g_ref[...] = grad
    if more:
        branch_back(
            width,
            slots,
            grad.astype(f32),
            z2_ref[...].astype(f32),
            picked,
            seg_row,
            before_ref,
            *rest[2:],
        )


def turned(values, cos, sin):
    groups = []
    for start in range(0, values.shape[1], 128):
        part = values[:, start : start + 128]
        lane = lax.broadcasted_iota(jnp.int32, part.shape, 1)
        other = jnp.where(lane % 2 == 0, pltpu.roll(part, 127, 1), pltpu.roll(part, 1, 1))
        groups.append(part * cos + other * sin)
    return groups[0] if len(groups) == 1 else jnp.concatenate(groups, axis=1)


def head_mask(lane, head):
    return (lane >= head * HEAD_DIM) & (lane < (head + 1) * HEAD_DIM)


class Attention:
    def __init__(self, refs, width):
        self.refs, self.width = refs, width
        self.groups, _, self.local = refs[0].shape
        self.depth = width // self.groups
        self.offset = 3 * self.depth if len(refs) == 1 else 0

    def project(self, p):
        part = self.refs[0][:, p * self.depth : (p + 1) * self.depth, :]
        return part.reshape(self.width, self.local)

    def out(self, g):
        return self.refs[-1][g, self.offset : self.offset + self.local, :]


class Feed:
    def __init__(self, refs, width, units):
        self.refs, self.width, self.units = refs, width, units
        self.groups, _, lanes = refs[0].shape
        self.depth = width // self.groups
        self.chunks = units // lanes
        self.offset = self.chunks * self.depth if len(refs) == 1 else 0

    def up(self):
        parts = [
            self.refs[0][:, i * self.depth : (i + 1) * self.depth, :].reshape(self.width, -1)
            for i in range(self.chunks)
        ]
        return parts

    def down(self, g):
        return self.refs[-1][g, self.offset : self.offset + self.units, :]


def qkv_of(x, weights, bias_ref, cos, sin):
    q = turned(mm(x, weights[0]) + bias_ref[0:1, :], cos, sin).astype(bf16)
    k = turned(mm(x, weights[1]) + bias_ref[1:2, :], cos, sin).astype(bf16)
    v = (mm(x, weights[2]) + bias_ref[2:3, :]).astype(bf16)
    return (q.astype(f32) * (HEAD_DIM**-0.5)).astype(bf16), k, v


def attend_rows(q, allowed, k_ref, v_ref):
    rows, local = q.shape
    lane = lax.broadcasted_iota(jnp.int32, (rows, local), 1)
    wide_lane = lax.broadcasted_iota(jnp.int32, (rows, 128), 1)
    mixed = jnp.zeros((rows, local), f32)
    lse = jnp.zeros((rows, 128), f32)
    for head in range(local // HEAD_DIM):
        mine = head_mask(lane, head)
        scores = mm_last(jnp.where(mine, q, jnp.zeros_like(q)), k_ref[...])
        scores = jnp.where(allowed, scores, big_negative)
        top = jnp.max(scores, axis=-1, keepdims=True)
        weight = jnp.exp(scores - top)
        weight_sum = jnp.sum(weight, axis=-1, keepdims=True)
        mixed = jnp.where(mine, mm(weight.astype(bf16), v_ref[...]) / weight_sum, mixed)
        lse = jnp.where(wide_lane == head, top + jnp.log(weight_sum), lse)
    return mixed.astype(bf16), lse


def project_kernel(blocks, parts, *refs):
    x_refs = refs[:blocks]
    weights = Attention(refs[blocks : blocks + parts], x_refs[0].shape[1])
    bias_ref, cos_ref, sin_ref, q_ref, k_ref, v_ref = refs[blocks + parts :]
    rows = x_refs[0].shape[0]
    mats = [weights.project(p) for p in range(3)]
    for j in range(blocks):
        here = slice(j * rows, (j + 1) * rows)
        q, k, v = qkv_of(x_refs[j][...], mats, bias_ref, cos_ref[here, :], sin_ref[here, :])
        q_ref[here, :] = q
        k_ref[here, :] = k
        v_ref[here, :] = v


def attend_far_kernel(blocks, parts, *refs):
    x_refs = refs[:blocks]
    rows, width = x_refs[0].shape
    weights = Attention(refs[blocks : blocks + parts], width)
    (
        bias_ref,
        cos_ref,
        sin_ref,
        seg_ref,
        seg_row_ref,
        near_k_ref,
        near_v_ref,
        q_ref,
        k_ref,
        v_ref,
        o_ref,
        lse_ref,
    ) = refs[blocks + parts : blocks + parts + 12]
    part_refs = refs[blocks + parts + 12 :]
    half = rows * blocks
    mats = [weights.project(p) for p in range(3)]
    k_ref[:half, :] = near_k_ref[...]
    v_ref[:half, :] = near_v_ref[...]
    for j in range(blocks):
        here = slice(j * rows, (j + 1) * rows)
        there = slice(half + j * rows, half + (j + 1) * rows)
        q, k, v = qkv_of(x_refs[j][...], mats, bias_ref, cos_ref[there, :], sin_ref[there, :])
        q_ref[here, :] = q
        k_ref[there, :] = k
        v_ref[there, :] = v
    attend_blocks(blocks, half, weights, seg_ref, seg_row_ref, q_ref, k_ref, v_ref, o_ref, lse_ref, part_refs)


def attend_blocks(blocks, start, weights, seg_ref, seg_row_ref, q_ref, k_ref, v_ref, o_ref, lse_ref, part_refs):
    rows = q_ref.shape[0] // blocks
    for j in reversed(range(blocks)):
        here = slice(j * rows, (j + 1) * rows)
        there = slice(start + j * rows, start + (j + 1) * rows)
        allowed = seg_ref[there, :] == seg_row_ref[...]
        mixed, lse = attend_rows(q_ref[here, :], allowed, k_ref, v_ref)
        o_ref[here, :] = mixed
        lse_ref[here, :] = lse
        for g in range(weights.groups):
            columns = slice(g * weights.depth, (g + 1) * weights.depth)
            part_refs[j][:, columns] = mm(mixed, weights.out(g)).astype(bf16)


def attend_near_kernel(blocks, parts, width, *refs):
    weights = Attention(refs[:parts], width)
    seg_ref, seg_row_ref, q_ref, k_ref, v_ref, o_ref, lse_ref = refs[parts : parts + 7]
    attend_blocks(
        blocks, 0, weights, seg_ref, seg_row_ref, q_ref, k_ref, v_ref, o_ref, lse_ref, refs[parts + 7 :]
    )


def input_terms(weights, dq, dk, dv):
    return (
        mm_last(dq, weights.project(0))
        + mm_last(dk, weights.project(1))
        + mm_last(dv, weights.project(2))
    ).astype(bf16)


def attend_back_kernel(blocks, parts, *refs):
    dz_refs = refs[:blocks]
    rows, width = dz_refs[0].shape
    weights = Attention(refs[blocks : blocks + parts], width)
    (
        near_q_ref,
        far_q_ref,
        k_ref,
        v_ref,
        near_lse_ref,
        far_lse_ref,
        cos_ref,
        sin_ref,
        seg_ref,
        seg_row_ref,
        dq_ref,
        dk_ref,
        dv_ref,
    ) = refs[blocks + parts : blocks + parts + 13]
    part_refs = refs[blocks + parts + 13 : -3]
    do_ref, dk_sum, dv_sum = refs[-3:]
    local, depth = weights.local, weights.depth
    half = blocks // 2
    for j in range(blocks):
        value = jnp.zeros((rows, local), f32)
        for g in range(weights.groups):
            value = value + mm_last(dz_refs[j][:, g * depth : (g + 1) * depth], weights.out(g))
        do_ref[j * rows : (j + 1) * rows, :] = value.astype(bf16)
    dk_sum[...] = jnp.zeros_like(dk_sum)
    dv_sum[...] = jnp.zeros_like(dv_sum)

    def one_side(start, q_ref, lse_ref):
        def one_block(i, carry):
            here = pl.ds(pl.multiple_of(i * rows, rows), rows)
            there = pl.ds(pl.multiple_of(start + i * rows, rows), rows)
            q, do, lse = q_ref[here, :], do_ref[there, :], lse_ref[here, :]
            allowed = seg_ref[there, :] == seg_row_ref[...]
            lane = lax.broadcasted_iota(jnp.int32, (rows, local), 1)
            dq = jnp.zeros((rows, local), f32)
            for head in range(local // HEAD_DIM):
                mine = head_mask(lane, head)
                q_head = jnp.where(mine, q, jnp.zeros_like(q))
                do_head = jnp.where(mine, do, jnp.zeros_like(do))
                scores = mm_last(q_head, k_ref[...])
                prob = jnp.exp(jnp.where(allowed, scores, big_negative) - lse[:, head : head + 1])
                d_prob = mm_last(do_head, v_ref[...])
                product = prob * d_prob
                centre = jnp.sum(product, axis=-1, keepdims=True)
                d_scores = (product - prob * centre).astype(bf16)
                dv_sum[...] += mm_first(prob.astype(bf16), do_head)
                dk_sum[...] += mm_first(d_scores, q_head)
                dq = jnp.where(mine, mm(d_scores, k_ref[...]), dq)
            dq = turned(dq * (HEAD_DIM**-0.5), cos_ref[there, :], -sin_ref[there, :])
            dq_ref[there, :] = dq.astype(bf16)
            return carry

        lax.fori_loop(0, half, one_block, 0)

    one_side(0, near_q_ref, near_lse_ref)
    one_side(half * rows, far_q_ref, far_lse_ref)
    for j in reversed(range(blocks)):
        here = slice(j * rows, (j + 1) * rows)
        dk_ref[here, :] = turned(dk_sum[here, :], cos_ref[here, :], -sin_ref[here, :]).astype(bf16)
        dv_ref[here, :] = dv_sum[here, :].astype(bf16)
        if j >= half:
            part_refs[j - half][...] = input_terms(
                weights, dq_ref[here, :], dk_ref[here, :], dv_ref[here, :]
            )


def gelu_parts(u):
    root = math.sqrt(2.0 / math.pi)
    square = u * u
    th = jnp.tanh(root * u * (1.0 + 0.044715 * square))
    return root, square, th


def feed_kernel(blocks, parts, *refs):
    a_refs = refs[:blocks]
    rows, width = a_refs[0].shape
    bias_ref, u_ref, g_ref = refs[blocks + parts : blocks + parts + 3]
    weights = Feed(refs[blocks : blocks + parts], width, bias_ref.shape[1])
    part_refs = refs[blocks + parts + 3 :]
    depth = weights.depth
    ups = weights.up()
    lanes = ups[0].shape[1]
    for j in reversed(range(blocks)):
        here = slice(j * rows, (j + 1) * rows)
        for i, w_up in enumerate(ups):
            columns = slice(i * lanes, (i + 1) * lanes)
            u = mm(a_refs[j][...], w_up) + bias_ref[:, columns]
            u_ref[here, columns] = u
            _, _, th = gelu_parts(u)
            g_ref[here, columns] = (0.5 * u * (1.0 + th)).astype(bf16)
        for k in range(weights.groups):
            part_refs[j][:, k * depth : (k + 1) * depth] = mm(
                g_ref[here, :], weights.down(k)
            ).astype(bf16)


def feed_back_kernel(blocks, parts, *refs):
    dz_refs = refs[:blocks]
    rows, width = dz_refs[0].shape
    u_ref, du_ref = refs[blocks + parts : blocks + parts + 2]
    weights = Feed(refs[blocks : blocks + parts], width, u_ref.shape[1])
    part_refs = refs[blocks + parts + 2 :]
    depth = weights.depth
    ups = weights.up()
    lanes = ups[0].shape[1]
    for j in reversed(range(blocks)):
        here = slice(j * rows, (j + 1) * rows)
        dg = jnp.zeros((rows, weights.units), f32)
        for k in range(weights.groups):
            dg = dg + mm_last(dz_refs[j][:, k * depth : (k + 1) * depth], weights.down(k))
        u = u_ref[here, :]
        root, square, th = gelu_parts(u)
        slope = 0.5 * (1.0 + th) + 0.5 * u * (1.0 - th * th) * (root * (1.0 + 0.134145 * square))
        du = (dg * slope).astype(bf16)
        du_ref[here, :] = du
        part_refs[j][...] = sum(
            mm_last(du[:, i * lanes : (i + 1) * lanes], w_up) for i, w_up in enumerate(ups)
        ).astype(bf16)


def feed_grads_kernel(blocks, *refs):
    a_refs, dz_refs = refs[:blocks], refs[blocks : 2 * blocks]
    near_g_ref, far_g_ref, near_du_ref, far_du_ref = refs[2 * blocks : 2 * blocks + 4]
    outs = refs[2 * blocks + 4 : -1]
    bias_up_ref = refs[-1]
    width, units = a_refs[0].shape[1], near_g_ref.shape[1]
    groups, _, lanes = outs[0].shape
    depth = width // groups
    chunks = units // lanes
    offset = chunks * depth if len(outs) == 1 else 0
    dz = jnp.concatenate([ref[...] for ref in dz_refs], axis=0)
    a2 = jnp.concatenate([ref[...] for ref in a_refs], axis=0)
    g = jnp.concatenate([near_g_ref[...], far_g_ref[...]], axis=0)
    du = jnp.concatenate([near_du_ref[...], far_du_ref[...]], axis=0)
    for k in range(groups):
        here = slice(k * depth, (k + 1) * depth)
        outs[-1][k, offset : offset + units, :] = mm_first(g, dz[:, here]).astype(bf16)
        for i in range(chunks):
            outs[0][k, i * depth : (i + 1) * depth, :] = mm_first(
                a2[:, here], du[:, i * lanes : (i + 1) * lanes]
            ).astype(bf16)
    bias_up_ref[...] = column_sums(du)


def attention_grads_kernel(blocks, parts, *refs):
    a_refs, dz_refs = refs[:blocks], refs[blocks : 2 * blocks]
    rows, width = a_refs[0].shape
    weights = Attention(refs[2 * blocks : 2 * blocks + parts], width)
    rest = refs[2 * blocks + parts :]
    dq_ref, dk_ref, dv_ref, near_o_ref, far_o_ref = rest[:5]
    half = blocks // 2
    part_refs, outs, bias_ref = rest[5 : 5 + half], rest[5 + half : -1], rest[-1]
    depth, local = weights.depth, weights.local
    for j in reversed(range(half)):
        here = slice(j * rows, (j + 1) * rows)
        part_refs[j][...] = input_terms(
            weights, dq_ref[here, :], dk_ref[here, :], dv_ref[here, :]
        )
    dz = jnp.concatenate([ref[...] for ref in dz_refs], axis=0)
    a1 = jnp.concatenate([ref[...] for ref in a_refs], axis=0)
    o = jnp.concatenate([near_o_ref[...], far_o_ref[...]], axis=0)
    for p, ref in enumerate((dq_ref, dk_ref, dv_ref)):
        bias_ref[p] = column_sums(ref[...])
        for k in range(weights.groups):
            outs[0][k, p * depth : (p + 1) * depth, :] = mm_first(
                a1[:, k * depth : (k + 1) * depth], ref[...]
            ).astype(bf16)
    for k in range(weights.groups):
        outs[-1][k, weights.offset : weights.offset + local, :] = mm_first(
            o, dz[:, k * depth : (k + 1) * depth]
        ).astype(bf16)


def mod_grads_kernel(blocks, codes_ref, place_ref, *refs):
    out_ref = refs[-1]
    strip = refs[0].shape[1]
    for j in range(blocks):
        here = pl.ds(pl.multiple_of(place_ref[j] * strip, 128), strip)
        out_ref[:, here] = mm_first(codes_ref[...], refs[j][...])


def per_device(
    endpoints,
    lengths,
    timesteps,
    w_qkv,
    b_qkv,
    w_out,
    b_out,
    w_up,
    b_up,
    w_down,
    b_down,
    w_mod,
    b_mod,
):
    section = lax.axis_index("section")
    tensor = lax.axis_index("tensor")
    group = lax.axis_index("dp")
    tensors, groups = lax.axis_size("tensor"), lax.axis_size("dp")
    half = tensors // 2
    rows, width = endpoints.shape[3], endpoints.shape[4]
    slots = lengths.shape[2]
    frames = rows * tensors
    depth = width // groups
    local = w_qkv.shape[3]
    units = w_up.shape[2]
    mod_width = w_mod.shape[2]
    strip = mod_width // tensors
    first = section == 0
    terms = len(list(bits_of(tensors))) + 1
    packed = depth == local

    def pick(here, other):
        return jnp.where(first, here, other), jnp.where(first, other, here)

    def mine_of(array):
        return jnp.where(first, array[0], array[1])

    def others_of(array):
        return jnp.where(first, array[1], array[0])

    flat_qkv = w_qkv[0].reshape(3 * depth, local)
    packs = [jnp.concatenate([flat_qkv, w_out[0]], axis=0)] if packed else [flat_qkv, w_out[0]]
    wholes = [lax.all_gather(pack, ("section", "dp"), axis=0, tiled=False) for pack in packs]
    attention = [[Half(pack, layer) for pack in wholes] for layer in range(2)]
    steps = jnp.pad(timesteps[:, 0], ((0, 0), (0, SLOT_ROWS - slots)))
    steps = after(steps, *packs)
    all_steps = jnp.stack([steps] + [swap(steps, "dp", j) for j in range(1, groups)])
    taken = swap(others_of(endpoints[0, :, 0]), "section", 1)
    kept = mine_of(endpoints[0, :, 0])
    h0, cotangent = pick(kept, taken)
    h_all = gather_rows(h0)

    column = group * depth + jnp.arange(depth, dtype=jnp.int32)
    frequency = jnp.exp(
        (column % (width // 2)).astype(f32) * (-math.log(10000.0) / (width // 2 - 1))
    )
    angle = all_steps.astype(f32)[..., None] * frequency
    codes = jax.nn.silu(
        jnp.where(column < width // 2, jnp.sin(angle), jnp.cos(angle))
    ).astype(bf16)
    share = b_mod.shape[1]
    bias_all = jnp.where(
        jnp.arange(mod_width)[None] // share == group,
        jnp.concatenate([b_mod] * groups, axis=1),
        jnp.zeros((), bf16),
    )
    mod_part = jnp.dot(
        codes.reshape(-1, depth),
        lax.dynamic_slice_in_dim(w_mod[0], tensor * strip, strip, 1),
        preferred_element_type=f32,
    ) + lax.dynamic_slice_in_dim(bias_all, tensor * strip, strip, 1).astype(f32)
    bias_sizes = [local // groups] * 3 + [depth, units // groups, depth]
    bias_row = jnp.concatenate([b_qkv[:, p] for p in range(3)] + [b_out, b_up, b_down], axis=1)
    bias_row = jnp.pad(bias_row, ((0, 0), (0, strip - bias_row.shape[1]))).astype(f32)
    slot_row = jnp.arange(SLOT_ROWS)[:, None]
    mod_part = jnp.where(
        slot_row < slots, mod_part.reshape(groups, 2, SLOT_ROWS, strip), bias_row
    )
    own_layer, other_layer = [], []
    for j in range(groups):
        for across, terms_of in enumerate((own_layer, other_layer)):
            term = (others_of if across else mine_of)(mod_part[j])
            here = across * groups + j
            route = [(i, i ^ here) for i in range(2 * groups)]
            terms_of.append(lax.ppermute(term, ("section", "dp"), route) if here else term)

    def with_biases(parts):
        biases_of = jnp.stack([part[slots] for part in parts])
        return jnp.concatenate([functools.reduce(jnp.add, parts), biases_of], axis=0)

    layer_mods = jnp.stack(pick(with_biases(own_layer), with_biases(other_layer)))
    other_up = swap(after(w_up[0], layer_mods), "section", 1)
    other_down = swap(after(w_down[0], layer_mods), "section", 1)
    own_strip = layer_mods[:, :SLOT_ROWS]
    strips_all = [own_strip] + [swap(own_strip, "tensor", j) for j in range(1, tensors)]
    strips_all = absolute(strips_all, tensor)
    mod_all = jnp.where(slot_row < slots, jnp.concatenate(strips_all, axis=-1), 0.0)

    def biases(layer):
        rel = [layer_mods[layer, SLOT_ROWS + j].astype(f32) for j in range(groups)]
        full = jnp.stack(absolute(rel, group))
        pieces, start = [], 0
        for size in bias_sizes:
            pieces.append(full[:, start : start + size].reshape(1, groups * size))
            start += size
        qkv = jnp.concatenate(pieces[:3] + [jnp.zeros((SLOT_ROWS - 3, local), f32)], axis=0)
        return qkv, *pieces[3:]

    lengths_here = mine_of(lengths[:, 0])
    block_index = tensor ^ jnp.arange(tensors, dtype=jnp.int32)
    frame = (block_index[:, None] * rows + jnp.arange(rows, dtype=jnp.int32)).reshape(-1)
    ends = jnp.cumsum(lengths_here)
    segment = jnp.sum((frame[:, None] >= ends[None, :]).astype(jnp.int32), axis=1)
    member = segment[:, None] == jnp.arange(slots, dtype=jnp.int32)[None, :]
    begin = jnp.sum(jnp.where(member, (ends - lengths_here)[None, :], 0), axis=1)
    position = (frame - begin).astype(f32)
    lane = jnp.arange(128, dtype=jnp.int32) % HEAD_DIM
    inverse = jnp.exp((lane // 2).astype(f32) * (-2.0 * math.log(10000.0) / HEAD_DIM))
    angles = position[:, None] * inverse[None, :]
    cos_table = jnp.cos(angles)
    sin_table = jnp.sin(angles) * jnp.where(lane % 2 == 0, -1.0, 1.0)
    seg_col, seg_row = segment[:, None], segment[None, :]
    own_col, own_row = seg_col[:rows], seg_row[:, :rows]

    block = shape((rows, width), bf16)
    block32 = shape((rows, width), f32)
    half_local = shape((frames // 2, local), bf16)
    wide_local = shape((frames, local), bf16)
    half_lse = shape((frames // 2, 128), f32)
    slot_block = shape((SLOT_ROWS, width), f32)
    project = 2 * frames * width * local
    scores = 2 * frames * frames * max(local, 256)

    a1_all = call(
        "first_norm",
        functools.partial(first_norm_kernel, width, tensors),
        [block] * tensors,
        *h_all,
        seg_col,
        mod_all[0],
    )
    a1_near, a1_far = list(a1_all[:half]), a1_all[half:]


    def feed_packs(layer, layer_up, layer_down):
        if packed:
            chunks = [layer_up[layer][:, i : i + local] for i in range(0, units, local)]
            return [jnp.concatenate([*chunks, layer_down[layer]], axis=0)]
        return [layer_up[layer], layer_down[layer]]

    other_up, other_down, a1_near[0] = tie(other_up, other_down, a1_near[0])
    pairs = pick(w_up[0], other_up), pick(w_down[0], other_down)
    feed = [[gather_groups(pack) for pack in feed_packs(layer, *pairs)] for layer in range(2)]

    layer_in = h0
    saved = []
    outputs = []
    for layer in range(2):
        mods = mod_all[layer]
        bias_qkv, bias_out, bias_up, bias_down = biases(layer)
        w_att = attention[layer]
        near_q, near_k, near_v = call(
            "project_near",
            functools.partial(project_kernel, half, len(w_att)),
            [half_local] * 3,
            *a1_near,
            *w_att,
            bias_qkv,
            cos_table,
            sin_table,
            flops=3 * project // 2,
        )
        a1_all = a1_near + (
            gather_near(after(a1_far, near_k)) if layer else list(a1_far)
        )
        far_q, k, v, far_o, far_lse, *parts = call(
            "attend_far",
            functools.partial(attend_far_kernel, half, len(w_att)),
            [half_local, wide_local, wide_local, half_local, half_lse] + [block] * half,
            *a1_all[half:],
            *w_att,
            bias_qkv,
            cos_table,
            sin_table,
            seg_col,
            seg_row,
            near_k,
            near_v,
        )
        summed, near_q = tie(near_sum(parts), near_q)
        far = cross(summed)
        near_o, near_lse, *parts = call(
            "attend_near",
            functools.partial(attend_near_kernel, half, len(w_att), width),
            [half_local, half_lse] + [block] * half,
            *w_att,
            seg_col,
            seg_row,
            near_q,
            k,
            v,
            flops=project // 2 + scores,
        )
        far = after(far, near_o)
        z1, h1, a2 = call(
            "middle",
            functools.partial(middle_kernel, width, terms),
            [block, block32, block],
            *scatter_near(parts),
            far,
            layer_in,
            bias_out,
            own_col,
            mods,
        )
        w_feed = feed[layer]
        a2_near, a2_far = gather_near(a2), cross(a2)

        def feed_half(blocks_of):
            return call(
                "feed",
                functools.partial(feed_kernel, half, len(w_feed)),
                [shape((frames // 2, units), f32), shape((frames // 2, units), bf16)]
                + [block] * half,
                *blocks_of,
                *w_feed,
                bias_up,
                flops=2 * frames * width * units,
            )

        near_u, near_g, *near_parts = feed_half(a2_near)
        a2_all = a2_near + gather_near(after(a2_far, near_u))
        far_u, far_g, *far_parts = feed_half(a2_all[half:])
        sums = [*scatter_near(near_parts), cross(near_sum(far_parts))]
        kept_state = (layer_in, a1_all, near_q, far_q, k, v, near_o, far_o, near_lse, far_lse)
        kept_state += (z1, h1, a2_all, near_u, far_u, near_g, far_g)
        if layer == 0:
            z2, y, a1 = call(
                "layer_end",
                functools.partial(layer_end_kernel, width, terms),
                [block] * 3,
                *sums,
                h1,
                bias_down,
                own_col,
                mods,
                mod_all[layer + 1],
            )
            layer_in = y
            a1_near, a1_far = gather_near(a1), cross(a1)
        else:
            z2 = None
            y, grad, dz2, dgate_b, d_bias_down = call(
                "turn",
                functools.partial(turn_kernel, width, slots, terms),
                [block, block, block, slot_block, slot_block],
                *sums,
                h1,
                bias_down,
                own_col,
                own_row,
                mods,
                cotangent,
            )
        outputs.append(y)
        saved.append((*kept_state, z2))

    attention_shards, feed_shards, in_grads, d_mods, d_biases = ([None, None] for _ in range(5))
    strip_index = jnp.arange(SLOT_ROWS)[:, None]
    for layer in (1, 0):
        mods = mod_all[layer]
        w_att, w_feed = attention[layer], feed[layer]
        (layer_in, a1_all, near_q, far_q, k, v, near_o, far_o, near_lse, far_lse) = saved[layer][:10]
        (z1, h1, a2_all, near_u, far_u, near_g, far_g, _) = saved[layer][10:]
        dz2_near, dz2_far = gather_near(dz2), cross(dz2)

        def feed_back_half(blocks_of, u):
            return call(
                "feed_back",
                functools.partial(feed_back_kernel, half, len(w_feed)),
                [shape((frames // 2, units), bf16)] + [block] * half,
                *blocks_of,
                *w_feed,
                u,
            )

        near_du, *near_parts = feed_back_half(dz2_near, near_u)
        dz2_all = dz2_near + gather_near(after(dz2_far, near_du))
        far_du, *far_parts = feed_back_half(dz2_all[half:], far_u)
        summed, far_du = tie(near_sum(far_parts), far_du)
        sums = [*scatter_near(near_parts), cross(summed)]
        feed_outs = (
            [(groups, units // local * depth + units, local)]
            if packed
            else [(groups, depth, units), (groups, units, depth)]
        )
        *d_feed, d_bias_up = call(
            "feed_grads",
            functools.partial(feed_grads_kernel, tensors),
            [shape(dims, bf16) for dims in feed_outs] + [shape((SLOT_ROWS, units), f32)],
            *a2_all,
            *dz2_all,
            near_g,
            far_g,
            near_du,
            far_du,
            flops=4 * frames * width * units,
        )
        feed_shards[layer] = [
            lax.psum_scatter(value, "dp", scatter_dimension=0, tiled=False) for value in d_feed
        ]
        sums = [*sums[:-1], after(sums[-1], d_bias_up)]
        dh1, dz1, d_mod_middle, d_bias_out = call(
            "middle_back",
            functools.partial(middle_back_kernel, width, slots, terms),
            [block32, block, shape((SLOT_ROWS, 3 * width), f32), slot_block],
            *sums,
            h1,
            grad,
            z1,
            own_col,
            own_row,
            mods,
        )
        dz1_all = gather_rows(dz1)
        dq, dk, dv, *far_parts = call(
            "attend_back",
            functools.partial(attend_back_kernel, tensors, len(w_att)),
            [wide_local] * 3 + [block] * half,
            *dz1_all,
            *w_att,
            near_q,
            far_q,
            k,
            v,
            near_lse,
            far_lse,
            cos_table,
            sin_table,
            seg_col,
            seg_row,
            scratch=[
                pltpu.VMEM((frames, local), bf16),
                pltpu.VMEM((frames, local), f32),
                pltpu.VMEM((frames, local), f32),
            ],
        )
        summed, dk = tie(near_sum(far_parts), dk)
        far = cross(summed)
        att_outs = (
            [(groups, 3 * depth + local, local)]
            if packed
            else [(groups, 3 * depth, local), (groups, local, depth)]
        )
        results = call(
            "attention_grads",
            functools.partial(attention_grads_kernel, tensors, len(w_att)),
            [block] * half
            + [shape(dims, bf16) for dims in att_outs]
            + [shape((3, SLOT_ROWS, local), f32)],
            *a1_all,
            *dz1_all,
            *w_att,
            dq,
            dk,
            dv,
            near_o,
            far_o,
            flops=11 * project // 2,
        )
        near_parts, d_att, d_bias_qkv = results[:half], results[half:-1], results[-1]
        far = after(far, d_bias_qkv)
        tied = tie(*d_att, *feed_shards[layer])
        d_att, feed_shards[layer] = tied[: len(d_att)], tied[len(d_att) :]
        attention_shards[layer] = [
            lax.psum_scatter(value, "dp", scatter_dimension=0, tiled=False) for value in d_att
        ]
        sums = [*scatter_near(near_parts), far]
        kernel = functools.partial(layer_back_kernel, width, slots, terms, layer > 0)
        arrays = [*sums, layer_in, dh1, own_col, own_row, mods]
        outs = [block, shape((SLOT_ROWS, 2 * width), f32)]
        bias_sums = jnp.concatenate([d_bias_out[:1], d_bias_down[:1]], axis=1)
        gate_sums = dgate_b
        if layer > 0:
            grad, d_mod_first, dz2, dgate_b, d_bias_down = call(
                "layer_back",
                kernel,
                outs + [block, slot_block, slot_block],
                *arrays,
                saved[layer - 1][-1],
                mod_all[layer - 1],
            )
        else:
            grad, d_mod_first = call("first_back", kernel, outs, *arrays)
        in_grads[layer] = grad
        bias_sums = jnp.pad(bias_sums, ((0, 0), (0, mod_width - bias_sums.shape[1])))
        d_mod = jnp.concatenate([d_mod_first, d_mod_middle, gate_sums], axis=1)
        d_mod = jnp.where(strip_index == slots, bias_sums, d_mod)
        blocks = [d_mod[:, b * strip : (b + 1) * strip] for b in range(tensors)]
        own = functools.reduce(
            jnp.add, reduce_rows(absolute(blocks, tensor), list(bits_of(tensors)))
        )
        own_bias = jnp.concatenate([d_bias_qkv[p, :1] for p in range(3)] + [d_bias_up[:1]], axis=1)
        own_bias = jnp.pad(own_bias, ((0, 0), (0, strip - own_bias.shape[1])))
        d_mods[layer] = jnp.where(strip_index == slots + 1, own_bias, own)

    def to_section(low, high):
        own = jnp.where(first, low, high)
        return own, swap(jnp.where(first, high, low), "section", 1)

    def add_sections(low, high):
        own, arrived = to_section(low, high)
        return own.astype(f32) + arrived.astype(f32)

    def frames_out(low, high):
        own, arrived = to_section(low, high)
        return jnp.where(first, jnp.stack([own, arrived]), jnp.stack([arrived, own]))

    activations = frames_out(*outputs)
    g_feed = [add_sections(*pair) for pair in zip(*feed_shards, strict=True)]
    input_grads = frames_out(*in_grads)
    d_mod, d_mod_other = to_section(*d_mods)
    pair = jnp.stack([d_mod, d_mod_other]).astype(bf16)
    pairs = jnp.stack([pair] + [swap(pair, "dp", j) for j in range(1, groups)])
    g_attention = [add_sections(*pair) for pair in zip(*attention_shards, strict=True)]
    everything = gather_rows(pairs.reshape(-1, strip))
    own_first = jnp.where(first, codes, codes[:, ::-1])
    live = jnp.where(slot_row < slots, own_first, jnp.zeros_like(own_first))
    places = tensor ^ jnp.arange(tensors, dtype=jnp.int32)
    (g_wmod,) = pl.pallas_call(
        functools.partial(mod_grads_kernel, tensors),
        name="mod_grads",
        out_shape=(shape((depth, mod_width), f32),),
        in_specs=[
            pl.BlockSpec(memory_space=pltpu.VMEM),
            pl.BlockSpec(memory_space=pltpu.SMEM),
        ]
        + [pl.BlockSpec(memory_space=pltpu.VMEM)] * tensors,
        compiler_params=pltpu.CompilerParams(vmem_limit_bytes=vmem_limit),
    )(live.reshape(-1, depth), places, *everything)
    row_sums = [
        jnp.sum(part.reshape(2 * groups, SLOT_ROWS, strip).astype(f32), axis=0)
        for part in everything
    ]
    own_sums = row_sums[0][slots + 1]
    all_sums = jnp.concatenate(absolute(row_sums, tensor), axis=1)

    def my_share(vector):
        count = vector.shape[-1] // groups
        return lax.dynamic_slice_in_dim(vector, group * count, count, vector.ndim - 1)

    g_bmod = my_share(jnp.sum(all_sums[:slots], axis=0))
    g_bqkv = my_share(own_sums[: 3 * local].reshape(3, local))
    g_bup = my_share(own_sums[3 * local : 3 * local + units])
    g_bout = my_share(all_sums[slots, :width])
    g_bdown = my_share(all_sums[slots, width : 2 * width])
    chunks = units // local * depth
    if packed:
        g_qkv, g_out = g_attention[0][: 3 * depth], g_attention[0][3 * depth :]
        g_up = jnp.concatenate(
            [g_feed[0][i : i + depth] for i in range(0, chunks, depth)], axis=1
        )
        g_down = g_feed[0][chunks:]
    else:
        g_qkv, g_out = g_attention
        g_up, g_down = g_feed
    return (
        activations[None, :, None],
        input_grads[None, :, None],
        g_qkv.reshape(1, 3, depth, local),
        g_bqkv[None],
        g_out[None],
        g_bout[None],
        g_up[None],
        g_bup[None],
        g_down[None],
        g_bdown[None],
        g_wmod[None],
        g_bmod[None],
    )


def solution(mesh):
    return jax.shard_map(
        per_device,
        mesh=mesh,
        in_specs=(
            P("section", None, "dp", "tensor", None),
            P(None, "dp", None),
            P(None, "dp", None),
            P("section", None, "dp", "tensor"),
            P("section", None, ("tensor", "dp")),
            P("section", "tensor", "dp"),
            P("section", "dp"),
            P("section", "dp", "tensor"),
            P("section", ("tensor", "dp")),
            P("section", "tensor", "dp"),
            P("section", "dp"),
            P("section", "dp", None),
            P("section", "dp"),
        ),
        out_specs=(
            P("section", None, "dp", "tensor", None),
            P("section", None, "dp", "tensor", None),
            P("section", None, "dp", "tensor"),
            P("section", None, ("tensor", "dp")),
            P("section", "tensor", "dp"),
            P("section", "dp"),
            P("section", "dp", "tensor"),
            P("section", ("tensor", "dp")),
            P("section", "tensor", "dp"),
            P("section", "dp"),
            P("section", "dp", None),
            P("section", "dp"),
        ),
        check_vma=False,
    )
```

```python
import functools
import math

import jax
import jax.numpy as jnp
from jax import lax
from jax.experimental import pallas as pl
from jax.experimental.pallas import tpu as pltpu
from jax.sharding import PartitionSpec as P

HEAD_DIM = 64
SLOT_ROWS = 8
norm_eps = 1e-06
big_negative = -1e30
f32 = jnp.float32
bf16 = jnp.bfloat16
vmem_limit = 52 * 1024 * 1024


def swap(block, axis, bit):
    return lax.ppermute(block, axis, [(i, i ^ bit) for i in range(lax.axis_size(axis))])


def after(value, *others):
    return lax.optimization_barrier((value, *others))[0]


def bits_of(count):
    bit = 1
    while bit < count:
        yield bit
        bit *= 2


def gather_near(block):
    blocks = {0: block}
    for bit in reversed(list(bits_of(lax.axis_size("tensor") // 2))):
        blocks.update({j | bit: swap(part, "tensor", bit) for j, part in list(blocks.items())})
    return [blocks[j] for j in range(len(blocks))]


def cross(block):
    return swap(block, "tensor", lax.axis_size("tensor") // 2)


def gather_rows(block):
    far = cross(block)
    return gather_near(block) + gather_near(far)


def reduce_rows(parts, bits):
    kept = dict(enumerate(parts))
    addends = [parts[0]]
    for bit in bits:
        arrived = {j: swap(kept[j | bit], "tensor", bit) for j in kept if not j & bit}
        addends.append(arrived.pop(0))
        kept = {
            0: parts[0],
            **{
                j: (kept[j].astype(f32) + part.astype(f32)).astype(parts[0].dtype)
                for j, part in arrived.items()
            },
        }
    return addends


def near_sum(parts):
    near = reduce_rows(parts, list(bits_of(len(parts))))
    summed = functools.reduce(jnp.add, [part.astype(f32) for part in near])
    return summed.astype(parts[0].dtype)


def scatter_near(parts):
    return reduce_rows(parts, list(bits_of(len(parts))))


def absolute(blocks, index):
    for bit in bits_of(len(blocks)):
        blocks = [
            jnp.where(index & bit, blocks[b ^ bit], blocks[b]) for b in range(len(blocks))
        ]
    return blocks


def gather_groups(block):
    return lax.all_gather(block, "dp", axis=0, tiled=False)


def tie(*values):
    return lax.optimization_barrier(values)


class Half:
    def __init__(self, array, index):
        self.array, self.index = array, index


def spec_of(arg):
    if isinstance(arg, Half):
        dims = arg.array.shape
        place = (arg.index,) + (0,) * (len(dims) - 1)
        return pl.BlockSpec((dims[0] // 2, *dims[1:]), lambda i: place)
    return pl.BlockSpec(memory_space=pltpu.VMEM)


def call(name, body, outs, *args, scratch=(), flops=0):
    whole = pl.BlockSpec(memory_space=pltpu.VMEM)
    grid = {"grid": (1,)} if any(isinstance(arg, Half) for arg in args) else {}
    return pl.pallas_call(
        body,
        in_specs=[spec_of(arg) for arg in args],
        out_specs=(whole,) * len(outs),
        **grid,
        out_shape=tuple(outs),
        name=name,
        scratch_shapes=scratch,
        compiler_params=pltpu.CompilerParams(vmem_limit_bytes=vmem_limit),
        cost_estimate=pl.CostEstimate(flops=flops, bytes_accessed=0, transcendentals=0),
    )(*[arg.array if isinstance(arg, Half) else arg for arg in args])


def shape(dims, dtype):
    return jax.ShapeDtypeStruct(dims, dtype)


def mm(left, right):
    return lax.dot_general(left, right, (((1,), (0,)), ((), ())), preferred_element_type=f32)


def mm_last(left, right):
    return lax.dot_general(left, right, (((1,), (1,)), ((), ())), preferred_element_type=f32)


def mm_first(left, right):
    return lax.dot_general(left, right, (((0,), (0,)), ((), ())), preferred_element_type=f32)


def slot_pick(seg_col):
    rows = seg_col.shape[0]
    lane = lax.broadcasted_iota(jnp.int32, (rows, SLOT_ROWS), 1)
    return (lane == seg_col).astype(f32).astype(bf16)


def part_of(picked, mod_ref, index, width):
    values = mod_ref[:, index * width : (index + 1) * width]
    high = values.astype(bf16)
    rest = (values - high.astype(f32)).astype(bf16)
    return mm(picked, high) + mm(picked, rest)


def slot_sums(seg_row, slots, values):
    row = lax.broadcasted_iota(jnp.int32, (SLOT_ROWS, seg_row.shape[1]), 0)
    picked = ((row == seg_row) & (row < slots)).astype(f32).astype(bf16)
    return mm(picked, values.astype(bf16))


def normed(values):
    centre = values - jnp.mean(values, axis=-1, keepdims=True)
    spread = jnp.mean(centre * centre, axis=-1, keepdims=True)
    inverse = lax.rsqrt(spread + norm_eps)
    return centre * inverse, inverse


def norm_back(norm, inverse, d_norm):
    mean_d = jnp.mean(d_norm, axis=-1, keepdims=True)
    mean_dn = jnp.mean(d_norm * norm, axis=-1, keepdims=True)
    return inverse * (d_norm - mean_d - norm * mean_dn)


def total(refs):
    value = refs[0][...].astype(f32)
    for ref in refs[1:]:
        value = value + ref[...].astype(f32)
    return value


def first_norm_kernel(width, blocks, *refs):
    seg_ref, mod_ref = refs[blocks : blocks + 2]
    rows = refs[0].shape[0]
    for j in range(blocks):
        picked = slot_pick(seg_ref[j * rows : (j + 1) * rows, :])
        norm, _ = normed(refs[j][...].astype(f32))
        scale = part_of(picked, mod_ref, 1, width)
        shift = part_of(picked, mod_ref, 0, width)
        refs[blocks + 2 + j][...] = (norm * (1.0 + scale) + shift).astype(bf16)


def middle_kernel(width, terms, *refs):
    sums = refs[:terms]
    h_ref, bias_ref, seg_ref, mod_ref, z1_ref, h1_ref, a2_ref = refs[terms:]
    picked = slot_pick(seg_ref[...])
    z1 = total(sums) + bias_ref[...]
    z1_ref[...] = z1.astype(bf16)
    h1 = h_ref[...].astype(f32) + part_of(picked, mod_ref, 2, width) * z1
    h1_ref[...] = h1
    norm, _ = normed(h1)
    a2_ref[...] = (
        norm * (1.0 + part_of(picked, mod_ref, 4, width)) + part_of(picked, mod_ref, 3, width)
    ).astype(bf16)


def layer_end_kernel(width, terms, *refs):
    sums = refs[:terms]
    h1_ref, bias_ref, seg_ref, mod_ref, next_ref, z2_ref, y_ref, a1_ref = refs[terms:]
    picked = slot_pick(seg_ref[...])
    z2 = total(sums) + bias_ref[...]
    z2_ref[...] = z2.astype(bf16)
    y = (h1_ref[...] + part_of(picked, mod_ref, 5, width) * z2).astype(bf16)
    y_ref[...] = y
    norm, _ = normed(y.astype(f32))
    a1_ref[...] = (
        norm * (1.0 + part_of(picked, next_ref, 1, width)) + part_of(picked, next_ref, 0, width)
    ).astype(bf16)


def column_sums(values):
    return mm(jnp.ones((SLOT_ROWS, values.shape[0]), bf16), values)


def branch_back(width, slots, grad, z2, picked, seg_row, mod_ref, dz2_ref, dgate_ref, bias_ref):
    dz2 = (grad * part_of(picked, mod_ref, 5, width)).astype(bf16)
    dz2_ref[...] = dz2
    dgate_ref[...] = slot_sums(seg_row, slots, grad * z2)
    bias_ref[...] = column_sums(dz2)


def turn_kernel(width, slots, terms, *refs):
    sums = refs[:terms]
    (h1_ref, bias_ref, seg_ref, seg_row_ref, mod_ref, cot_ref) = refs[terms : terms + 6]
    y_ref, c_ref = refs[terms + 6 : terms + 8]
    seg = seg_ref[...]
    picked = slot_pick(seg)
    z2 = total(sums) + bias_ref[...]
    y_ref[...] = (h1_ref[...] + part_of(picked, mod_ref, 5, width) * z2).astype(bf16)
    grad = jnp.where(seg < slots, cot_ref[...].astype(f32), 0.0)
    c_ref[...] = grad.astype(bf16)
    branch_back(width, slots, grad, z2, picked, seg_row_ref[...], mod_ref, *refs[terms + 8 :])


def middle_back_kernel(width, slots, terms, *refs):
    sums = refs[:terms]
    h1_ref, c_ref, z1_ref, seg_ref, seg_row_ref, mod_ref = refs[terms : terms + 6]
    dh1_ref, dz1_ref, d_mod_ref, bias_ref = refs[terms + 6 :]
    picked = slot_pick(seg_ref[...])
    seg_row = seg_row_ref[...]
    da2 = total(sums)
    norm, inverse = normed(h1_ref[...])
    d_mod_ref[:, width : 2 * width] = slot_sums(seg_row, slots, da2)
    d_mod_ref[:, 2 * width :] = slot_sums(seg_row, slots, da2 * norm)
    d_norm = da2 * (1.0 + part_of(picked, mod_ref, 4, width))
    dh1 = c_ref[...].astype(f32) + norm_back(norm, inverse, d_norm)
    dh1_ref[...] = dh1
    dz1 = (dh1 * part_of(picked, mod_ref, 2, width)).astype(bf16)
    dz1_ref[...] = dz1
    d_mod_ref[:, :width] = slot_sums(seg_row, slots, dh1 * z1_ref[...].astype(f32))
    bias_ref[...] = column_sums(dz1)


def layer_back_kernel(width, slots, terms, more, *refs):
    sums = refs[:terms]
    h_ref, dh1_ref, seg_ref, seg_row_ref, mod_ref = refs[terms : terms + 5]
    rest = refs[terms + 5 :]
    if more:
        z2_ref, before_ref = rest[:2]
        rest = rest[2:]
    g_ref, d_mod_ref = rest[:2]
    picked = slot_pick(seg_ref[...])
    seg_row = seg_row_ref[...]
    da1 = total(sums)
    norm, inverse = normed(h_ref[...].astype(f32))
    d_mod_ref[:, :width] = slot_sums(seg_row, slots, da1)
    d_mod_ref[:, width:] = slot_sums(seg_row, slots, da1 * norm)
    d_norm = da1 * (1.0 + part_of(picked, mod_ref, 1, width))
    grad = (dh1_ref[...] + norm_back(norm, inverse, d_norm)).astype(bf16)
    g_ref[...] = grad
    if more:
        branch_back(
            width,
            slots,
            grad.astype(f32),
            z2_ref[...].astype(f32),
            picked,
            seg_row,
            before_ref,
            *rest[2:],
        )


def turned(values, cos, sin):
    groups = []
    for start in range(0, values.shape[1], 128):
        part = values[:, start : start + 128]
        lane = lax.broadcasted_iota(jnp.int32, part.shape, 1)
        other = jnp.where(lane % 2 == 0, pltpu.roll(part, 127, 1), pltpu.roll(part, 1, 1))
        groups.append(part * cos + other * sin)
    return groups[0] if len(groups) == 1 else jnp.concatenate(groups, axis=1)


def head_mask(lane, head):
    return (lane >= head * HEAD_DIM) & (lane < (head + 1) * HEAD_DIM)


class Attention:
    def __init__(self, refs, width):
        self.refs, self.width = refs, width
        self.groups, _, self.local = refs[0].shape
        self.depth = width // self.groups
        self.offset = 3 * self.depth if len(refs) == 1 else 0

    def project(self, p):
        part = self.refs[0][:, p * self.depth : (p + 1) * self.depth, :]
        return part.reshape(self.width, self.local)

    def out(self, g):
        return self.refs[-1][g, self.offset : self.offset + self.local, :]


class Feed:
    def __init__(self, refs, width, units, copies):
        self.refs, self.width, self.units, self.copies = refs, width, units, copies
        self.groups, _, self.lanes = refs[0].shape
        self.depth = width // self.groups
        self.chunks = units // self.lanes
        self.packed = len(refs) == 1

    def up_place(self, copy, chunk):
        if self.packed:
            return self.refs[0], copy * (self.chunks * self.depth + self.units) + chunk * self.depth
        return self.refs[2 * copy], 0

    def down_place(self, copy):
        if self.packed:
            return self.refs[0], self.up_place(copy, self.chunks)[1]
        return self.refs[2 * copy + 1], 0

    def ups(self):
        for copy in range(self.copies):
            for chunk in range(self.chunks):
                ref, row = self.up_place(copy, chunk)
                block = ref[:, row : row + self.depth, :].reshape(self.width, self.lanes)
                yield copy * self.units + chunk * self.lanes, block

    def down(self, copy, g):
        ref, row = self.down_place(copy)
        return ref[g, row : row + self.units, :]


def qkv_of(x, weights, bias_ref, cos, sin):
    q = turned(mm(x, weights[0]) + bias_ref[0:1, :], cos, sin).astype(bf16)
    k = turned(mm(x, weights[1]) + bias_ref[1:2, :], cos, sin).astype(bf16)
    v = (mm(x, weights[2]) + bias_ref[2:3, :]).astype(bf16)
    return (q.astype(f32) * (HEAD_DIM**-0.5)).astype(bf16), k, v


def attend_rows(q, allowed, k_ref, v_ref):
    rows, local = q.shape
    lane = lax.broadcasted_iota(jnp.int32, (rows, local), 1)
    wide_lane = lax.broadcasted_iota(jnp.int32, (rows, 128), 1)
    mixed = jnp.zeros((rows, local), f32)
    lse = jnp.zeros((rows, 128), f32)
    for head in range(local // HEAD_DIM):
        mine = head_mask(lane, head)
        scores = mm_last(jnp.where(mine, q, jnp.zeros_like(q)), k_ref[...])
        scores = jnp.where(allowed, scores, big_negative)
        top = jnp.max(scores, axis=-1, keepdims=True)
        weight = jnp.exp(scores - top)
        weight_sum = jnp.sum(weight, axis=-1, keepdims=True)
        mixed = jnp.where(mine, mm(weight.astype(bf16), v_ref[...]) / weight_sum, mixed)
        lse = jnp.where(wide_lane == head, top + jnp.log(weight_sum), lse)
    return mixed.astype(bf16), lse


def project_kernel(blocks, parts, *refs):
    x_refs = refs[:blocks]
    weights = Attention(refs[blocks : blocks + parts], x_refs[0].shape[1])
    bias_ref, cos_ref, sin_ref, q_ref, k_ref, v_ref = refs[blocks + parts :]
    rows = x_refs[0].shape[0]
    mats = [weights.project(p) for p in range(3)]
    for j in range(blocks):
        here = slice(j * rows, (j + 1) * rows)
        q, k, v = qkv_of(x_refs[j][...], mats, bias_ref, cos_ref[here, :], sin_ref[here, :])
        q_ref[here, :] = q
        k_ref[here, :] = k
        v_ref[here, :] = v


def attend_far_kernel(blocks, parts, *refs):
    x_refs = refs[:blocks]
    rows, width = x_refs[0].shape
    weights = Attention(refs[blocks : blocks + parts], width)
    (
        bias_ref,
        cos_ref,
        sin_ref,
        seg_ref,
        seg_row_ref,
        near_k_ref,
        near_v_ref,
        q_ref,
        k_ref,
        v_ref,
        o_ref,
        lse_ref,
    ) = refs[blocks + parts : blocks + parts + 12]
    part_refs = refs[blocks + parts + 12 :]
    half = rows * blocks
    mats = [weights.project(p) for p in range(3)]
    k_ref[:half, :] = near_k_ref[...]
    v_ref[:half, :] = near_v_ref[...]
    for j in range(blocks):
        here = slice(j * rows, (j + 1) * rows)
        there = slice(half + j * rows, half + (j + 1) * rows)
        q, k, v = qkv_of(x_refs[j][...], mats, bias_ref, cos_ref[there, :], sin_ref[there, :])
        q_ref[here, :] = q
        k_ref[there, :] = k
        v_ref[there, :] = v
    attend_blocks(blocks, half, weights, seg_ref, seg_row_ref, q_ref, k_ref, v_ref, o_ref, lse_ref, part_refs)


def attend_blocks(blocks, start, weights, seg_ref, seg_row_ref, q_ref, k_ref, v_ref, o_ref, lse_ref, part_refs):
    rows = q_ref.shape[0] // blocks
    for j in reversed(range(blocks)):
        here = slice(j * rows, (j + 1) * rows)
        there = slice(start + j * rows, start + (j + 1) * rows)
        allowed = seg_ref[there, :] == seg_row_ref[...]
        mixed, lse = attend_rows(q_ref[here, :], allowed, k_ref, v_ref)
        o_ref[here, :] = mixed
        lse_ref[here, :] = lse
        for g in range(weights.groups):
            columns = slice(g * weights.depth, (g + 1) * weights.depth)
            part_refs[j][:, columns] = mm(mixed, weights.out(g)).astype(bf16)


def attend_near_kernel(blocks, parts, width, *refs):
    weights = Attention(refs[:parts], width)
    seg_ref, seg_row_ref, q_ref, k_ref, v_ref, o_ref, lse_ref = refs[parts : parts + 7]
    attend_blocks(
        blocks, 0, weights, seg_ref, seg_row_ref, q_ref, k_ref, v_ref, o_ref, lse_ref, refs[parts + 7 :]
    )


def input_terms(weights, dq, dk, dv):
    return (
        mm_last(dq, weights.project(0))
        + mm_last(dk, weights.project(1))
        + mm_last(dv, weights.project(2))
    ).astype(bf16)


def attend_back_kernel(blocks, parts, *refs):
    dz_refs = refs[:blocks]
    rows, width = dz_refs[0].shape
    weights = Attention(refs[blocks : blocks + parts], width)
    (
        near_q_ref,
        far_q_ref,
        k_ref,
        v_ref,
        near_lse_ref,
        far_lse_ref,
        cos_ref,
        sin_ref,
        seg_ref,
        seg_row_ref,
        dq_ref,
        dk_ref,
        dv_ref,
    ) = refs[blocks + parts : blocks + parts + 13]
    part_refs = refs[blocks + parts + 13 : -3]
    do_ref, dk_sum, dv_sum = refs[-3:]
    local, depth = weights.local, weights.depth
    half = blocks // 2
    for j in range(blocks):
        value = jnp.zeros((rows, local), f32)
        for g in range(weights.groups):
            value = value + mm_last(dz_refs[j][:, g * depth : (g + 1) * depth], weights.out(g))
        do_ref[j * rows : (j + 1) * rows, :] = value.astype(bf16)
    dk_sum[...] = jnp.zeros_like(dk_sum)
    dv_sum[...] = jnp.zeros_like(dv_sum)

    def one_side(start, q_ref, lse_ref):
        def one_block(i, carry):
            here = pl.ds(pl.multiple_of(i * rows, rows), rows)
            there = pl.ds(pl.multiple_of(start + i * rows, rows), rows)
            q, do, lse = q_ref[here, :], do_ref[there, :], lse_ref[here, :]
            allowed = seg_ref[there, :] == seg_row_ref[...]
            lane = lax.broadcasted_iota(jnp.int32, (rows, local), 1)
            dq = jnp.zeros((rows, local), f32)
            for head in range(local // HEAD_DIM):
                mine = head_mask(lane, head)
                q_head = jnp.where(mine, q, jnp.zeros_like(q))
                do_head = jnp.where(mine, do, jnp.zeros_like(do))
                scores = mm_last(q_head, k_ref[...])
                prob = jnp.exp(jnp.where(allowed, scores, big_negative) - lse[:, head : head + 1])
                d_prob = mm_last(do_head, v_ref[...])
                product = prob * d_prob
                centre = jnp.sum(product, axis=-1, keepdims=True)
                d_scores = (product - prob * centre).astype(bf16)
                dv_sum[...] += mm_first(prob.astype(bf16), do_head)
                dk_sum[...] += mm_first(d_scores, q_head)
                dq = jnp.where(mine, mm(d_scores, k_ref[...]), dq)
            dq = turned(dq * (HEAD_DIM**-0.5), cos_ref[there, :], -sin_ref[there, :])
            dq_ref[there, :] = dq.astype(bf16)
            return carry

        lax.fori_loop(0, half, one_block, 0)

    one_side(0, near_q_ref, near_lse_ref)
    one_side(half * rows, far_q_ref, far_lse_ref)
    for j in reversed(range(blocks)):
        here = slice(j * rows, (j + 1) * rows)
        dk_ref[here, :] = turned(dk_sum[here, :], cos_ref[here, :], -sin_ref[here, :]).astype(bf16)
        dv_ref[here, :] = dv_sum[here, :].astype(bf16)
        if j >= half:
            part_refs[j - half][...] = input_terms(
                weights, dq_ref[here, :], dk_ref[here, :], dv_ref[here, :]
            )


def gelu_parts(u):
    root = math.sqrt(2.0 / math.pi)
    square = u * u
    th = jnp.tanh(root * u * (1.0 + 0.044715 * square))
    return root, square, th


def feed_kernel(blocks, parts, copies, *refs):
    a_refs = refs[:blocks]
    rows, width = a_refs[0].shape
    bias_ref, u_ref, g_ref = refs[blocks + parts : blocks + parts + 3]
    units = bias_ref.shape[1] // copies
    weights = Feed(refs[blocks : blocks + parts], width, units, copies)
    part_refs = refs[blocks + parts + 3 :]
    depth = weights.depth
    for j in reversed(range(blocks)):
        here = slice(j * rows, (j + 1) * rows)
        for start, w_up in weights.ups():
            columns = slice(start, start + weights.lanes)
            u = mm(a_refs[j][...], w_up) + bias_ref[:, columns]
            u_ref[here, columns] = u
            _, _, th = gelu_parts(u)
            g_ref[here, columns] = (0.5 * u * (1.0 + th)).astype(bf16)
        for k in range(weights.groups):
            part_refs[j][:, k * depth : (k + 1) * depth] = sum(
                mm(g_ref[here, copy * units : (copy + 1) * units], weights.down(copy, k))
                for copy in range(copies)
            ).astype(bf16)


def feed_back_kernel(blocks, parts, copies, *refs):
    dz_refs = refs[:blocks]
    rows, width = dz_refs[0].shape
    u_ref, du_ref = refs[blocks + parts : blocks + parts + 2]
    units = u_ref.shape[1] // copies
    weights = Feed(refs[blocks : blocks + parts], width, units, copies)
    part_refs = refs[blocks + parts + 2 :]
    depth = weights.depth
    for j in reversed(range(blocks)):
        here = slice(j * rows, (j + 1) * rows)
        for copy in range(copies):
            columns = slice(copy * units, (copy + 1) * units)
            dg = sum(
                mm_last(dz_refs[j][:, k * depth : (k + 1) * depth], weights.down(copy, k))
                for k in range(weights.groups)
            )
            u = u_ref[here, columns]
            root, square, th = gelu_parts(u)
            slope = 0.5 * (1.0 + th) + 0.5 * u * (1.0 - th * th) * (
                root * (1.0 + 0.134145 * square)
            )
            du_ref[here, columns] = (dg * slope).astype(bf16)
        part_refs[j][...] = sum(
            mm_last(du_ref[here, start : start + weights.lanes], w_up)
            for start, w_up in weights.ups()
        ).astype(bf16)


def feed_grads_kernel(blocks, sides, copies, *refs):
    a_refs, dz_refs = refs[:blocks], refs[blocks : 2 * blocks]
    g_refs = refs[2 * blocks : 2 * blocks + sides]
    du_refs = refs[2 * blocks + sides : 2 * blocks + 2 * sides]
    outs, bias_up_ref = refs[2 * blocks + 2 * sides : -1], refs[-1]
    width, units = a_refs[0].shape[1], g_refs[0].shape[1] // copies
    places = Feed(outs, width, units, copies)
    depth, lanes = places.depth, places.lanes
    dz = jnp.concatenate([ref[...] for ref in dz_refs], axis=0)
    a2 = jnp.concatenate([ref[...] for ref in a_refs], axis=0)
    g = jnp.concatenate([ref[...] for ref in g_refs], axis=0)
    du = jnp.concatenate([ref[...] for ref in du_refs], axis=0)
    for k in range(places.groups):
        here = slice(k * depth, (k + 1) * depth)
        for copy in range(copies):
            ref, row = places.down_place(copy)
            ref[k, row : row + units, :] = mm_first(
                g[:, copy * units : (copy + 1) * units], dz[:, here]
            ).astype(bf16)
            for chunk in range(places.chunks):
                ref, row = places.up_place(copy, chunk)
                start = copy * units + chunk * lanes
                ref[k, row : row + depth, :] = mm_first(
                    a2[:, here], du[:, start : start + lanes]
                ).astype(bf16)
    bias_up_ref[...] = column_sums(du)


def attention_grads_kernel(blocks, parts, *refs):
    a_refs, dz_refs = refs[:blocks], refs[blocks : 2 * blocks]
    rows, width = a_refs[0].shape
    weights = Attention(refs[2 * blocks : 2 * blocks + parts], width)
    rest = refs[2 * blocks + parts :]
    dq_ref, dk_ref, dv_ref, near_o_ref, far_o_ref = rest[:5]
    half = blocks // 2
    part_refs, outs, bias_ref = rest[5 : 5 + half], rest[5 + half : -1], rest[-1]
    depth, local = weights.depth, weights.local
    for j in reversed(range(half)):
        here = slice(j * rows, (j + 1) * rows)
        part_refs[j][...] = input_terms(
            weights, dq_ref[here, :], dk_ref[here, :], dv_ref[here, :]
        )
    dz = jnp.concatenate([ref[...] for ref in dz_refs], axis=0)
    a1 = jnp.concatenate([ref[...] for ref in a_refs], axis=0)
    o = jnp.concatenate([near_o_ref[...], far_o_ref[...]], axis=0)
    for p, ref in enumerate((dq_ref, dk_ref, dv_ref)):
        bias_ref[p] = column_sums(ref[...])
        for k in range(weights.groups):
            outs[0][k, p * depth : (p + 1) * depth, :] = mm_first(
                a1[:, k * depth : (k + 1) * depth], ref[...]
            ).astype(bf16)
    for k in range(weights.groups):
        outs[-1][k, weights.offset : weights.offset + local, :] = mm_first(
            o, dz[:, k * depth : (k + 1) * depth]
        ).astype(bf16)


def mod_grads_kernel(blocks, codes_ref, place_ref, *refs):
    out_ref = refs[-1]
    strip = refs[0].shape[1]
    for j in range(blocks):
        here = pl.ds(pl.multiple_of(place_ref[j] * strip, 128), strip)
        out_ref[:, here] = mm_first(codes_ref[...], refs[j][...])


def per_device(
    endpoints,
    lengths,
    timesteps,
    w_qkv,
    b_qkv,
    w_out,
    b_out,
    w_up,
    b_up,
    w_down,
    b_down,
    w_mod,
    b_mod,
):
    section = lax.axis_index("section")
    tensor = lax.axis_index("tensor")
    group = lax.axis_index("dp")
    tensors, groups = lax.axis_size("tensor"), lax.axis_size("dp")
    half = tensors // 2
    rows, width = endpoints.shape[3], endpoints.shape[4]
    slots = lengths.shape[2]
    frames = rows * tensors
    depth = width // groups
    local = w_qkv.shape[3]
    units = w_up.shape[2]
    mod_width = w_mod.shape[2]
    strip = mod_width // tensors
    first = section == 0
    terms = len(list(bits_of(tensors))) + 1
    packed = depth == local

    def pick(here, other):
        return jnp.where(first, here, other), jnp.where(first, other, here)

    def mine_of(array):
        return jnp.where(first, array[0], array[1])

    def others_of(array):
        return jnp.where(first, array[1], array[0])

    flat_qkv = w_qkv[0].reshape(3 * depth, local)
    packs = [jnp.concatenate([flat_qkv, w_out[0]], axis=0)] if packed else [flat_qkv, w_out[0]]
    wholes = [lax.all_gather(pack, ("section", "dp"), axis=0, tiled=False) for pack in packs]
    attention = [[Half(pack, layer) for pack in wholes] for layer in range(2)]
    steps = jnp.pad(timesteps[:, 0], ((0, 0), (0, SLOT_ROWS - slots)))
    steps = after(steps, *packs)
    all_steps = jnp.stack([steps] + [swap(steps, "dp", j) for j in range(1, groups)])
    taken = swap(others_of(endpoints[0, :, 0]), "section", 1)
    kept = mine_of(endpoints[0, :, 0])
    h0, cotangent = pick(kept, taken)
    h_all = gather_rows(h0)

    column = group * depth + jnp.arange(depth, dtype=jnp.int32)
    frequency = jnp.exp(
        (column % (width // 2)).astype(f32) * (-math.log(10000.0) / (width // 2 - 1))
    )
    angle = all_steps.astype(f32)[..., None] * frequency
    codes = jax.nn.silu(
        jnp.where(column < width // 2, jnp.sin(angle), jnp.cos(angle))
    ).astype(bf16)
    share = b_mod.shape[1]
    bias_all = jnp.where(
        jnp.arange(mod_width)[None] // share == group,
        jnp.concatenate([b_mod] * groups, axis=1),
        jnp.zeros((), bf16),
    )
    mod_part = jnp.dot(
        codes.reshape(-1, depth),
        lax.dynamic_slice_in_dim(w_mod[0], tensor * strip, strip, 1),
        preferred_element_type=f32,
    ) + lax.dynamic_slice_in_dim(bias_all, tensor * strip, strip, 1).astype(f32)
    bias_sizes = [local // groups] * 3 + [depth, units // groups, depth]
    bias_row = jnp.concatenate([b_qkv[:, p] for p in range(3)] + [b_out, b_up, b_down], axis=1)
    bias_row = jnp.pad(bias_row, ((0, 0), (0, strip - bias_row.shape[1]))).astype(f32)
    slot_row = jnp.arange(SLOT_ROWS)[:, None]
    mod_part = jnp.where(
        slot_row < slots, mod_part.reshape(groups, 2, SLOT_ROWS, strip), bias_row
    )
    own_layer, other_layer = [], []
    for j in range(groups):
        for across, terms_of in enumerate((own_layer, other_layer)):
            term = (others_of if across else mine_of)(mod_part[j])
            here = across * groups + j
            route = [(i, i ^ here) for i in range(2 * groups)]
            terms_of.append(lax.ppermute(term, ("section", "dp"), route) if here else term)

    def with_biases(parts):
        biases_of = jnp.stack([part[slots] for part in parts])
        return jnp.concatenate([functools.reduce(jnp.add, parts), biases_of], axis=0)

    layer_mods = jnp.stack(pick(with_biases(own_layer), with_biases(other_layer)))
    other_up = swap(after(w_up[0], layer_mods), "section", 1)
    other_down = swap(after(w_down[0], layer_mods), "section", 1)
    own_strip = layer_mods[:, :SLOT_ROWS]
    strips_all = [own_strip] + [swap(own_strip, "tensor", j) for j in range(1, tensors)]
    strips_all = absolute(strips_all, tensor)
    mod_all = jnp.where(slot_row < slots, jnp.concatenate(strips_all, axis=-1), 0.0)

    def biases(layer):
        rel = [layer_mods[layer, SLOT_ROWS + j].astype(f32) for j in range(groups)]
        full = jnp.stack(absolute(rel, group))
        pieces, start = [], 0
        for size in bias_sizes:
            pieces.append(full[:, start : start + size].reshape(1, groups * size))
            start += size
        qkv = jnp.concatenate(pieces[:3] + [jnp.zeros((SLOT_ROWS - 3, local), f32)], axis=0)
        return qkv, *pieces[3:]

    lengths_here = mine_of(lengths[:, 0])
    block_index = tensor ^ jnp.arange(tensors, dtype=jnp.int32)
    frame = (block_index[:, None] * rows + jnp.arange(rows, dtype=jnp.int32)).reshape(-1)
    ends = jnp.cumsum(lengths_here)
    segment = jnp.sum((frame[:, None] >= ends[None, :]).astype(jnp.int32), axis=1)
    member = segment[:, None] == jnp.arange(slots, dtype=jnp.int32)[None, :]
    begin = jnp.sum(jnp.where(member, (ends - lengths_here)[None, :], 0), axis=1)
    position = (frame - begin).astype(f32)
    lane = jnp.arange(128, dtype=jnp.int32) % HEAD_DIM
    inverse = jnp.exp((lane // 2).astype(f32) * (-2.0 * math.log(10000.0) / HEAD_DIM))
    angles = position[:, None] * inverse[None, :]
    cos_table = jnp.cos(angles)
    sin_table = jnp.sin(angles) * jnp.where(lane % 2 == 0, -1.0, 1.0)
    seg_col, seg_row = segment[:, None], segment[None, :]
    own_col, own_row = seg_col[:rows], seg_row[:, :rows]

    block = shape((rows, width), bf16)
    block32 = shape((rows, width), f32)
    half_local = shape((frames // 2, local), bf16)
    wide_local = shape((frames, local), bf16)
    half_lse = shape((frames // 2, 128), f32)
    slot_block = shape((SLOT_ROWS, width), f32)
    project = 2 * frames * width * local
    scores = 2 * frames * frames * max(local, 256)

    a1_all = call(
        "first_norm",
        functools.partial(first_norm_kernel, width, tensors),
        [block] * tensors,
        *h_all,
        seg_col,
        mod_all[0],
    )
    a1_near, a1_far = list(a1_all[:half]), a1_all[half:]


    def feed_packs(layer, layer_up, layer_down):
        if packed:
            chunks = [layer_up[layer][:, i : i + local] for i in range(0, units, local)]
            return [jnp.concatenate([*chunks, layer_down[layer]], axis=0)]
        return [layer_up[layer], layer_down[layer]]

    other_up, other_down, a1_near[0] = tie(other_up, other_down, a1_near[0])
    pairs = pick(w_up[0], other_up), pick(w_down[0], other_down)
    feed = [[gather_groups(pack) for pack in feed_packs(0, *pairs)]]
    last_packs = feed_packs(1, *pairs)
    partner_packs = [cross(pack) for pack in last_packs]
    if packed:
        last_packs = [jnp.concatenate(last_packs + partner_packs, axis=0)]
    else:
        last_packs = last_packs + partner_packs
    feed.append([gather_groups(pack) for pack in last_packs])

    layer_in = h0
    saved = []
    outputs = []
    for layer in range(2):
        mods = mod_all[layer]
        bias_qkv, bias_out, bias_up, bias_down = biases(layer)
        w_att = attention[layer]
        near_q, near_k, near_v = call(
            "project_near",
            functools.partial(project_kernel, half, len(w_att)),
            [half_local] * 3,
            *a1_near,
            *w_att,
            bias_qkv,
            cos_table,
            sin_table,
            flops=3 * project // 2,
        )
        a1_all = a1_near + (
            gather_near(after(a1_far, near_k)) if layer else list(a1_far)
        )
        far_q, k, v, far_o, far_lse, *parts = call(
            "attend_far",
            functools.partial(attend_far_kernel, half, len(w_att)),
            [half_local, wide_local, wide_local, half_local, half_lse] + [block] * half,
            *a1_all[half:],
            *w_att,
            bias_qkv,
            cos_table,
            sin_table,
            seg_col,
            seg_row,
            near_k,
            near_v,
        )
        summed, near_q = tie(near_sum(parts), near_q)
        far = cross(summed)
        near_o, near_lse, *parts = call(
            "attend_near",
            functools.partial(attend_near_kernel, half, len(w_att), width),
            [half_local, half_lse] + [block] * half,
            *w_att,
            seg_col,
            seg_row,
            near_q,
            k,
            v,
            flops=project // 2 + scores,
        )
        far = after(far, near_o)
        z1, h1, a2 = call(
            "middle",
            functools.partial(middle_kernel, width, terms),
            [block, block32, block],
            *scatter_near(parts),
            far,
            layer_in,
            bias_out,
            own_col,
            mods,
        )
        w_feed = feed[layer]
        copies = layer + 1
        a2_near = gather_near(a2)
        if copies == 2:
            bias_up = jnp.concatenate([bias_up, cross(bias_up)], axis=1)

        def feed_half(blocks_of):
            columns = units * copies
            return call(
                "feed",
                functools.partial(feed_kernel, half, len(w_feed), copies),
                [shape((frames // 2, columns), f32), shape((frames // 2, columns), bf16)]
                + [block] * half,
                *blocks_of,
                *w_feed,
                bias_up,
                flops=2 * frames * width * units,
            )

        if copies == 1:
            a2_far = cross(a2)
            near_u, near_g, *near_parts = feed_half(a2_near)
            a2_far = gather_near(after(a2_far, near_u))
            far_u, far_g, *far_parts = feed_half(a2_far)
            sums = [*scatter_near(near_parts), cross(near_sum(far_parts))]
            a2_all = a2_near + a2_far
            u_all, g_all = (near_u, far_u), (near_g, far_g)
        else:
            near_u, near_g, *near_parts = feed_half(a2_near)
            sums = scatter_near(near_parts)
            a2_all, u_all, g_all = a2_near, (near_u,), (near_g,)
        kept_state = (layer_in, a1_all, near_q, far_q, k, v, near_o, far_o, near_lse, far_lse)
        kept_state += (z1, h1, a2_all, u_all, g_all)
        if layer == 0:
            z2, y, a1 = call(
                "layer_end",
                functools.partial(layer_end_kernel, width, len(sums)),
                [block] * 3,
                *sums,
                h1,
                bias_down,
                own_col,
                mods,
                mod_all[layer + 1],
            )
            layer_in = y
            a1_near, a1_far = gather_near(a1), cross(a1)
        else:
            z2 = None
            y, grad, dz2, dgate_b, d_bias_down = call(
                "turn",
                functools.partial(turn_kernel, width, slots, len(sums)),
                [block, block, block, slot_block, slot_block],
                *sums,
                h1,
                bias_down,
                own_col,
                own_row,
                mods,
                cotangent,
            )
        outputs.append(y)
        saved.append((*kept_state, z2))

    attention_shards, feed_shards, in_grads, d_mods, d_biases = ([None, None] for _ in range(5))
    strip_index = jnp.arange(SLOT_ROWS)[:, None]
    for layer in (1, 0):
        mods = mod_all[layer]
        w_att, w_feed = attention[layer], feed[layer]
        (layer_in, a1_all, near_q, far_q, k, v, near_o, far_o, near_lse, far_lse) = saved[layer][:10]
        (z1, h1, a2_all, u_all, g_all, _) = saved[layer][10:]
        copies = layer + 1
        dz2_near = gather_near(dz2)

        def feed_back_half(blocks_of, u):
            return call(
                "feed_back",
                functools.partial(feed_back_kernel, half, len(w_feed), copies),
                [shape((frames // 2, units * copies), bf16)] + [block] * half,
                *blocks_of,
                *w_feed,
                u,
            )

        if copies == 1:
            dz2_far = cross(dz2)
            near_du, *near_parts = feed_back_half(dz2_near, u_all[0])
            dz2_all = dz2_near + gather_near(after(dz2_far, near_du))
            far_du, *far_parts = feed_back_half(dz2_all[half:], u_all[1])
            summed, far_du = tie(near_sum(far_parts), far_du)
            sums = [*scatter_near(near_parts), cross(summed)]
            du_all = (near_du, far_du)
        else:
            dz2_all = dz2_near
            near_du, *near_parts = feed_back_half(dz2_near, u_all[0])
            sums = scatter_near(near_parts)
            du_all = (near_du,)

        def feed_grads(du_all):
            pack_rows = units // local * depth + units
            feed_outs = (
                [(groups, copies * pack_rows, local)]
                if packed
                else [(groups, depth, units), (groups, units, depth)] * copies
            )
            return call(
                "feed_grads",
                functools.partial(feed_grads_kernel, len(a2_all), len(du_all), copies),
                [shape(dims, bf16) for dims in feed_outs]
                + [shape((SLOT_ROWS, units * copies), f32)],
                *a2_all,
                *dz2_all,
                *g_all,
                *du_all,
                flops=4 * frames * width * units,
            )

        if copies == 1:
            *d_feed, d_bias_up = feed_grads(du_all)
            sums = [*sums[:-1], after(sums[-1], d_bias_up)]
            sums[-1], *feed_shards[1] = tie(sums[-1], *feed_shards[1])
        dh1, dz1, d_mod_middle, d_bias_out = call(
            "middle_back",
            functools.partial(middle_back_kernel, width, slots, len(sums)),
            [block32, block, shape((SLOT_ROWS, 3 * width), f32), slot_block],
            *sums,
            h1,
            grad,
            z1,
            own_col,
            own_row,
            mods,
        )
        dz1_far = cross(dz1)
        if copies == 2:
            dz1, *du_all = tie(dz1, *du_all)
            *d_feed, d_bias_up = feed_grads(du_all)
            dz1_far = after(dz1_far, d_bias_up)
            d_bias_up = d_bias_up[:, :units] + cross(d_bias_up[:, units:])
        feed_shards[layer] = [
            lax.psum_scatter(value, "dp", scatter_dimension=0, tiled=False) for value in d_feed
        ]
        dz1_all = gather_near(dz1) + gather_near(dz1_far)
        dq, dk, dv, *far_parts = call(
            "attend_back",
            functools.partial(attend_back_kernel, tensors, len(w_att)),
            [wide_local] * 3 + [block] * half,
            *dz1_all,
            *w_att,
            near_q,
            far_q,
            k,
            v,
            near_lse,
            far_lse,
            cos_table,
            sin_table,
            seg_col,
            seg_row,
            scratch=[
                pltpu.VMEM((frames, local), bf16),
                pltpu.VMEM((frames, local), f32),
                pltpu.VMEM((frames, local), f32),
            ],
        )
        summed, dk = tie(near_sum(far_parts), dk)
        far = cross(summed)
        if layer == 0:
            dq, *attention_shards[1] = tie(dq, *attention_shards[1])
        att_outs = (
            [(groups, 3 * depth + local, local)]
            if packed
            else [(groups, 3 * depth, local), (groups, local, depth)]
        )
        results = call(
            "attention_grads",
            functools.partial(attention_grads_kernel, tensors, len(w_att)),
            [block] * half
            + [shape(dims, bf16) for dims in att_outs]
            + [shape((3, SLOT_ROWS, local), f32)],
            *a1_all,
            *dz1_all,
            *w_att,
            dq,
            dk,
            dv,
            near_o,
            far_o,
            flops=11 * project // 2,
        )
        near_parts, d_att, d_bias_qkv = results[:half], results[half:-1], results[-1]
        far = after(far, d_bias_qkv)
        if layer == 0:
            far, *feed_shards[0] = tie(far, *feed_shards[0])
        attention_shards[layer] = [
            lax.psum_scatter(value, "dp", scatter_dimension=0, tiled=False) for value in d_att
        ]
        sums = [*scatter_near(near_parts), far]
        kernel = functools.partial(layer_back_kernel, width, slots, terms, layer > 0)
        arrays = [*sums, layer_in, dh1, own_col, own_row, mods]
        outs = [block, shape((SLOT_ROWS, 2 * width), f32)]
        bias_sums = jnp.concatenate([d_bias_out[:1], d_bias_down[:1]], axis=1)
        gate_sums = dgate_b
        if layer > 0:
            grad, d_mod_first, dz2, dgate_b, d_bias_down = call(
                "layer_back",
                kernel,
                outs + [block, slot_block, slot_block],
                *arrays,
                saved[layer - 1][-1],
                mod_all[layer - 1],
            )
        else:
            grad, d_mod_first = call("first_back", kernel, outs, *arrays)
        in_grads[layer] = grad
        bias_sums = jnp.pad(bias_sums, ((0, 0), (0, mod_width - bias_sums.shape[1])))
        d_mod = jnp.concatenate([d_mod_first, d_mod_middle, gate_sums], axis=1)
        d_mod = jnp.where(strip_index == slots, bias_sums, d_mod)
        blocks = [d_mod[:, b * strip : (b + 1) * strip] for b in range(tensors)]
        own = functools.reduce(
            jnp.add, reduce_rows(absolute(blocks, tensor), list(bits_of(tensors)))
        )
        own_bias = jnp.concatenate([d_bias_qkv[p, :1] for p in range(3)] + [d_bias_up[:1]], axis=1)
        own_bias = jnp.pad(own_bias, ((0, 0), (0, strip - own_bias.shape[1])))
        d_mods[layer] = jnp.where(strip_index == slots + 1, own_bias, own)

    count = len(feed_shards[1])
    if packed:
        shard = feed_shards[1][0]
        pack_rows = shard.shape[0] // 2
        pieces = [(shard[:pack_rows], shard[pack_rows:])]
    else:
        pieces = list(
            zip(feed_shards[1][: count // 2], feed_shards[1][count // 2 :])
        )
    feed_shards[1] = [
        (own.astype(f32) + cross(partner).astype(f32)).astype(bf16)
        for own, partner in pieces
    ]

    def to_section(low, high):
        own = jnp.where(first, low, high)
        return own, swap(jnp.where(first, high, low), "section", 1)

    def add_sections(low, high):
        own, arrived = to_section(low, high)
        return own.astype(f32) + arrived.astype(f32)

    def frames_out(low, high):
        own, arrived = to_section(low, high)
        return jnp.where(first, jnp.stack([own, arrived]), jnp.stack([arrived, own]))

    activations = frames_out(*outputs)
    g_feed = [add_sections(*pair) for pair in zip(*feed_shards, strict=True)]
    input_grads = frames_out(*in_grads)
    d_mod, d_mod_other = to_section(*d_mods)
    pair = jnp.stack([d_mod, d_mod_other]).astype(bf16)
    pairs = jnp.stack([pair] + [swap(pair, "dp", j) for j in range(1, groups)])
    g_attention = [add_sections(*pair) for pair in zip(*attention_shards, strict=True)]
    everything = gather_rows(pairs.reshape(-1, strip))
    own_first = jnp.where(first, codes, codes[:, ::-1])
    live = jnp.where(slot_row < slots, own_first, jnp.zeros_like(own_first))
    places = tensor ^ jnp.arange(tensors, dtype=jnp.int32)
    (g_wmod,) = pl.pallas_call(
        functools.partial(mod_grads_kernel, tensors),
        name="mod_grads",
        out_shape=(shape((depth, mod_width), f32),),
        in_specs=[
            pl.BlockSpec(memory_space=pltpu.VMEM),
            pl.BlockSpec(memory_space=pltpu.SMEM),
        ]
        + [pl.BlockSpec(memory_space=pltpu.VMEM)] * tensors,
        compiler_params=pltpu.CompilerParams(vmem_limit_bytes=vmem_limit),
    )(live.reshape(-1, depth), places, *everything)
    row_sums = [
        jnp.sum(part.reshape(2 * groups, SLOT_ROWS, strip).astype(f32), axis=0)
        for part in everything
    ]
    own_sums = row_sums[0][slots + 1]
    all_sums = jnp.concatenate(absolute(row_sums, tensor), axis=1)

    def my_share(vector):
        count = vector.shape[-1] // groups
        return lax.dynamic_slice_in_dim(vector, group * count, count, vector.ndim - 1)

    g_bmod = my_share(jnp.sum(all_sums[:slots], axis=0))
    g_bqkv = my_share(own_sums[: 3 * local].reshape(3, local))
    g_bup = my_share(own_sums[3 * local : 3 * local + units])
    g_bout = my_share(all_sums[slots, :width])
    g_bdown = my_share(all_sums[slots, width : 2 * width])
    chunks = units // local * depth
    if packed:
        g_qkv, g_out = g_attention[0][: 3 * depth], g_attention[0][3 * depth :]
        g_up = jnp.concatenate(
            [g_feed[0][i : i + depth] for i in range(0, chunks, depth)], axis=1
        )
        g_down = g_feed[0][chunks:]
    else:
        g_qkv, g_out = g_attention
        g_up, g_down = g_feed
    return (
        activations[None, :, None],
        input_grads[None, :, None],
        g_qkv.reshape(1, 3, depth, local),
        g_bqkv[None],
        g_out[None],
        g_bout[None],
        g_up[None],
        g_bup[None],
        g_down[None],
        g_bdown[None],
        g_wmod[None],
        g_bmod[None],
    )


def solution(mesh):
    return jax.shard_map(
        per_device,
        mesh=mesh,
        in_specs=(
            P("section", None, "dp", "tensor", None),
            P(None, "dp", None),
            P(None, "dp", None),
            P("section", None, "dp", "tensor"),
            P("section", None, ("tensor", "dp")),
            P("section", "tensor", "dp"),
            P("section", "dp"),
            P("section", "dp", "tensor"),
            P("section", ("tensor", "dp")),
            P("section", "tensor", "dp"),
            P("section", "dp"),
            P("section", "dp", None),
            P("section", "dp"),
        ),
        out_specs=(
            P("section", None, "dp", "tensor", None),
            P("section", None, "dp", "tensor", None),
            P("section", None, "dp", "tensor"),
            P("section", None, ("tensor", "dp")),
            P("section", "tensor", "dp"),
            P("section", "dp"),
            P("section", "dp", "tensor"),
            P("section", ("tensor", "dp")),
            P("section", "tensor", "dp"),
            P("section", "dp"),
            P("section", "dp", None),
            P("section", "dp"),
        ),
        check_vma=False,
    )
```

```python
import functools
import math

import jax
import jax.numpy as jnp
from jax import lax
from jax.experimental import pallas as pl
from jax.experimental.pallas import tpu as pltpu
from jax.sharding import PartitionSpec as P

HEAD_DIM = 64
SLOT_ROWS = 8
norm_eps = 1e-06
big_negative = -1e30
f32 = jnp.float32
bf16 = jnp.bfloat16
vmem_limit = 52 * 1024 * 1024


def swap(block, axis, bit):
    return lax.ppermute(block, axis, [(i, i ^ bit) for i in range(lax.axis_size(axis))])


def after(value, *others):
    return lax.optimization_barrier((value, *others))[0]


def bits_of(count):
    bit = 1
    while bit < count:
        yield bit
        bit *= 2


def gather_near(block):
    blocks = {0: block}
    for bit in reversed(list(bits_of(lax.axis_size("tensor") // 2))):
        blocks.update({j | bit: swap(part, "tensor", bit) for j, part in list(blocks.items())})
    return [blocks[j] for j in range(len(blocks))]


def cross(block):
    return swap(block, "tensor", lax.axis_size("tensor") // 2)


def gather_rows(block):
    far = cross(block)
    return gather_near(block) + gather_near(far)


def reduce_rows(parts, bits):
    kept = dict(enumerate(parts))
    addends = [parts[0]]
    for bit in bits:
        arrived = {j: swap(kept[j | bit], "tensor", bit) for j in kept if not j & bit}
        addends.append(arrived.pop(0))
        kept = {
            0: parts[0],
            **{
                j: (kept[j].astype(f32) + part.astype(f32)).astype(parts[0].dtype)
                for j, part in arrived.items()
            },
        }
    return addends


def near_sum(parts):
    near = reduce_rows(parts, list(bits_of(len(parts))))
    summed = functools.reduce(jnp.add, [part.astype(f32) for part in near])
    return summed.astype(parts[0].dtype)


def scatter_near(parts):
    return reduce_rows(parts, list(bits_of(len(parts))))


def absolute(blocks, index):
    for bit in bits_of(len(blocks)):
        blocks = [
            jnp.where(index & bit, blocks[b ^ bit], blocks[b]) for b in range(len(blocks))
        ]
    return blocks


def gather_groups(block):
    return lax.all_gather(block, "dp", axis=0, tiled=False)


def tie(*values):
    return lax.optimization_barrier(values)


class Half:
    def __init__(self, array, index):
        self.array, self.index = array, index


def spec_of(arg):
    if isinstance(arg, Half):
        dims = arg.array.shape
        place = (arg.index,) + (0,) * (len(dims) - 1)
        return pl.BlockSpec((dims[0] // 2, *dims[1:]), lambda i: place)
    return pl.BlockSpec(memory_space=pltpu.VMEM)


def call(name, body, outs, *args, scratch=(), flops=0, micros=0):
    flops = flops or micros * 1_150_000_000
    whole = pl.BlockSpec(memory_space=pltpu.VMEM)
    grid = {"grid": (1,)} if any(isinstance(arg, Half) for arg in args) else {}
    return pl.pallas_call(
        body,
        in_specs=[spec_of(arg) for arg in args],
        out_specs=(whole,) * len(outs),
        **grid,
        out_shape=tuple(outs),
        name=name,
        scratch_shapes=scratch,
        compiler_params=pltpu.CompilerParams(vmem_limit_bytes=vmem_limit),
        cost_estimate=pl.CostEstimate(flops=flops, bytes_accessed=0, transcendentals=0),
    )(*[arg.array if isinstance(arg, Half) else arg for arg in args])


def shape(dims, dtype):
    return jax.ShapeDtypeStruct(dims, dtype)


def mm(left, right):
    return lax.dot_general(left, right, (((1,), (0,)), ((), ())), preferred_element_type=f32)


def mm_last(left, right):
    return lax.dot_general(left, right, (((1,), (1,)), ((), ())), preferred_element_type=f32)


def mm_first(left, right):
    return lax.dot_general(left, right, (((0,), (0,)), ((), ())), preferred_element_type=f32)


def slot_pick(seg_col):
    rows = seg_col.shape[0]
    lane = lax.broadcasted_iota(jnp.int32, (rows, SLOT_ROWS), 1)
    return (lane == seg_col).astype(f32).astype(bf16)


def part_of(picked, mod_ref, index, width):
    values = mod_ref[:, index * width : (index + 1) * width]
    high = values.astype(bf16)
    rest = (values - high.astype(f32)).astype(bf16)
    return mm(picked, high) + mm(picked, rest)


def slot_sums(seg_row, slots, values):
    row = lax.broadcasted_iota(jnp.int32, (SLOT_ROWS, seg_row.shape[1]), 0)
    picked = ((row == seg_row) & (row < slots)).astype(f32).astype(bf16)
    return mm(picked, values.astype(bf16))


def normed(values):
    centre = values - jnp.mean(values, axis=-1, keepdims=True)
    spread = jnp.mean(centre * centre, axis=-1, keepdims=True)
    inverse = lax.rsqrt(spread + norm_eps)
    return centre * inverse, inverse


def norm_back(norm, inverse, d_norm):
    mean_d = jnp.mean(d_norm, axis=-1, keepdims=True)
    mean_dn = jnp.mean(d_norm * norm, axis=-1, keepdims=True)
    return inverse * (d_norm - mean_d - norm * mean_dn)


def total(refs):
    value = refs[0][...].astype(f32)
    for ref in refs[1:]:
        value = value + ref[...].astype(f32)
    return value


def first_norm_kernel(width, blocks, *refs):
    seg_ref, mod_ref = refs[blocks : blocks + 2]
    rows = refs[0].shape[0]
    for j in range(blocks):
        picked = slot_pick(seg_ref[j * rows : (j + 1) * rows, :])
        norm, _ = normed(refs[j][...].astype(f32))
        scale = part_of(picked, mod_ref, 1, width)
        shift = part_of(picked, mod_ref, 0, width)
        refs[blocks + 2 + j][...] = (norm * (1.0 + scale) + shift).astype(bf16)


def middle_kernel(width, terms, *refs):
    sums = refs[:terms]
    h_ref, bias_ref, seg_ref, mod_ref, z1_ref, h1_ref, a2_ref = refs[terms:]
    picked = slot_pick(seg_ref[...])
    z1 = total(sums) + bias_ref[...]
    z1_ref[...] = z1.astype(bf16)
    h1 = h_ref[...].astype(f32) + part_of(picked, mod_ref, 2, width) * z1
    h1_ref[...] = h1
    norm, _ = normed(h1)
    a2_ref[...] = (
        norm * (1.0 + part_of(picked, mod_ref, 4, width)) + part_of(picked, mod_ref, 3, width)
    ).astype(bf16)


def layer_end_kernel(width, terms, *refs):
    sums = refs[:terms]
    h1_ref, bias_ref, seg_ref, mod_ref, next_ref, z2_ref, y_ref, a1_ref = refs[terms:]
    picked = slot_pick(seg_ref[...])
    z2 = total(sums) + bias_ref[...]
    z2_ref[...] = z2.astype(bf16)
    y = (h1_ref[...] + part_of(picked, mod_ref, 5, width) * z2).astype(bf16)
    y_ref[...] = y
    norm, _ = normed(y.astype(f32))
    a1_ref[...] = (
        norm * (1.0 + part_of(picked, next_ref, 1, width)) + part_of(picked, next_ref, 0, width)
    ).astype(bf16)


def column_sums(values):
    return mm(jnp.ones((SLOT_ROWS, values.shape[0]), bf16), values)


def branch_back(width, slots, grad, z2, picked, seg_row, mod_ref, dz2_ref, dgate_ref, bias_ref):
    dz2 = (grad * part_of(picked, mod_ref, 5, width)).astype(bf16)
    dz2_ref[...] = dz2
    dgate_ref[...] = slot_sums(seg_row, slots, grad * z2)
    bias_ref[...] = column_sums(dz2)


def turn_kernel(width, slots, terms, *refs):
    sums = refs[:terms]
    (h1_ref, bias_ref, seg_ref, seg_row_ref, mod_ref, cot_ref) = refs[terms : terms + 6]
    y_ref, c_ref = refs[terms + 6 : terms + 8]
    seg = seg_ref[...]
    picked = slot_pick(seg)
    z2 = total(sums) + bias_ref[...]
    y_ref[...] = (h1_ref[...] + part_of(picked, mod_ref, 5, width) * z2).astype(bf16)
    grad = jnp.where(seg < slots, cot_ref[...].astype(f32), 0.0)
    c_ref[...] = grad.astype(bf16)
    branch_back(width, slots, grad, z2, picked, seg_row_ref[...], mod_ref, *refs[terms + 8 :])


def middle_back_kernel(width, slots, terms, *refs):
    sums = refs[:terms]
    h1_ref, c_ref, z1_ref, seg_ref, seg_row_ref, mod_ref = refs[terms : terms + 6]
    dh1_ref, dz1_ref, d_mod_ref, bias_ref = refs[terms + 6 :]
    picked = slot_pick(seg_ref[...])
    seg_row = seg_row_ref[...]
    da2 = total(sums)
    norm, inverse = normed(h1_ref[...])
    d_mod_ref[:, width : 2 * width] = slot_sums(seg_row, slots, da2)
    d_mod_ref[:, 2 * width :] = slot_sums(seg_row, slots, da2 * norm)
    d_norm = da2 * (1.0 + part_of(picked, mod_ref, 4, width))
    dh1 = c_ref[...].astype(f32) + norm_back(norm, inverse, d_norm)
    dh1_ref[...] = dh1
    dz1 = (dh1 * part_of(picked, mod_ref, 2, width)).astype(bf16)
    dz1_ref[...] = dz1
    d_mod_ref[:, :width] = slot_sums(seg_row, slots, dh1 * z1_ref[...].astype(f32))
    bias_ref[...] = column_sums(dz1)


def layer_back_kernel(width, slots, terms, more, *refs):
    sums = refs[:terms]
    h_ref, dh1_ref, seg_ref, seg_row_ref, mod_ref = refs[terms : terms + 5]
    rest = refs[terms + 5 :]
    if more:
        z2_ref, before_ref = rest[:2]
        rest = rest[2:]
    g_ref, d_mod_ref = rest[:2]
    picked = slot_pick(seg_ref[...])
    seg_row = seg_row_ref[...]
    da1 = total(sums)
    norm, inverse = normed(h_ref[...].astype(f32))
    d_mod_ref[:, :width] = slot_sums(seg_row, slots, da1)
    d_mod_ref[:, width:] = slot_sums(seg_row, slots, da1 * norm)
    d_norm = da1 * (1.0 + part_of(picked, mod_ref, 1, width))
    grad = (dh1_ref[...] + norm_back(norm, inverse, d_norm)).astype(bf16)
    g_ref[...] = grad
    if more:
        branch_back(
            width,
            slots,
            grad.astype(f32),
            z2_ref[...].astype(f32),
            picked,
            seg_row,
            before_ref,
            *rest[2:],
        )


def turned(values, cos, sin):
    groups = []
    for start in range(0, values.shape[1], 128):
        part = values[:, start : start + 128]
        lane = lax.broadcasted_iota(jnp.int32, part.shape, 1)
        other = jnp.where(lane % 2 == 0, pltpu.roll(part, 127, 1), pltpu.roll(part, 1, 1))
        groups.append(part * cos + other * sin)
    return groups[0] if len(groups) == 1 else jnp.concatenate(groups, axis=1)


def head_mask(lane, head):
    return (lane >= head * HEAD_DIM) & (lane < (head + 1) * HEAD_DIM)


class Attention:
    def __init__(self, refs, width):
        self.refs, self.width = refs, width
        self.groups, _, self.local = refs[0].shape
        self.depth = width // self.groups
        self.offset = 3 * self.depth if len(refs) == 1 else 0

    def project(self, p):
        part = self.refs[0][:, p * self.depth : (p + 1) * self.depth, :]
        return part.reshape(self.width, self.local)

    def out(self, g):
        return self.refs[-1][g, self.offset : self.offset + self.local, :]


class Feed:
    def __init__(self, refs, width, units, copies):
        self.refs, self.width, self.units, self.copies = refs, width, units, copies
        self.groups, _, self.lanes = refs[0].shape
        self.depth = width // self.groups
        self.chunks = units // self.lanes
        self.packed = len(refs) == 1

    def up_place(self, copy, chunk):
        if self.packed:
            return self.refs[0], copy * (self.chunks * self.depth + self.units) + chunk * self.depth
        return self.refs[2 * copy], 0

    def down_place(self, copy):
        if self.packed:
            return self.refs[0], self.up_place(copy, self.chunks)[1]
        return self.refs[2 * copy + 1], 0

    def ups(self):
        for copy in range(self.copies):
            for chunk in range(self.chunks):
                ref, row = self.up_place(copy, chunk)
                block = ref[:, row : row + self.depth, :].reshape(self.width, self.lanes)
                yield copy * self.units + chunk * self.lanes, block

    def down(self, copy, g):
        ref, row = self.down_place(copy)
        return ref[g, row : row + self.units, :]


def qkv_of(x, weights, bias_ref, cos, sin):
    q = turned(mm(x, weights[0]) + bias_ref[0:1, :], cos, sin).astype(bf16)
    k = turned(mm(x, weights[1]) + bias_ref[1:2, :], cos, sin).astype(bf16)
    v = (mm(x, weights[2]) + bias_ref[2:3, :]).astype(bf16)
    return (q.astype(f32) * (HEAD_DIM**-0.5)).astype(bf16), k, v


def attend_rows(q, allowed, k_ref, v_ref):
    rows, local = q.shape
    lane = lax.broadcasted_iota(jnp.int32, (rows, local), 1)
    wide_lane = lax.broadcasted_iota(jnp.int32, (rows, 128), 1)
    mixed = jnp.zeros((rows, local), f32)
    lse = jnp.zeros((rows, 128), f32)
    for head in range(local // HEAD_DIM):
        mine = head_mask(lane, head)
        scores = mm_last(jnp.where(mine, q, jnp.zeros_like(q)), k_ref[...])
        scores = jnp.where(allowed, scores, big_negative)
        top = jnp.max(scores, axis=-1, keepdims=True)
        weight = jnp.exp(scores - top)
        weight_sum = jnp.sum(weight, axis=-1, keepdims=True)
        mixed = jnp.where(mine, mm(weight.astype(bf16), v_ref[...]) / weight_sum, mixed)
        lse = jnp.where(wide_lane == head, top + jnp.log(weight_sum), lse)
    return mixed.astype(bf16), lse


def project_kernel(blocks, parts, *refs):
    x_refs = refs[:blocks]
    weights = Attention(refs[blocks : blocks + parts], x_refs[0].shape[1])
    bias_ref, cos_ref, sin_ref, q_ref, k_ref, v_ref = refs[blocks + parts :]
    rows = x_refs[0].shape[0]
    mats = [weights.project(p) for p in range(3)]
    for j in range(blocks):
        here = slice(j * rows, (j + 1) * rows)
        q, k, v = qkv_of(x_refs[j][...], mats, bias_ref, cos_ref[here, :], sin_ref[here, :])
        q_ref[here, :] = q
        k_ref[here, :] = k
        v_ref[here, :] = v


def attend_far_kernel(blocks, parts, *refs):
    x_refs = refs[:blocks]
    rows, width = x_refs[0].shape
    weights = Attention(refs[blocks : blocks + parts], width)
    (
        bias_ref,
        cos_ref,
        sin_ref,
        seg_ref,
        seg_row_ref,
        near_k_ref,
        near_v_ref,
        q_ref,
        k_ref,
        v_ref,
        o_ref,
        lse_ref,
    ) = refs[blocks + parts : blocks + parts + 12]
    part_refs = refs[blocks + parts + 12 :]
    half = rows * blocks
    mats = [weights.project(p) for p in range(3)]
    k_ref[:half, :] = near_k_ref[...]
    v_ref[:half, :] = near_v_ref[...]
    for j in range(blocks):
        here = slice(j * rows, (j + 1) * rows)
        there = slice(half + j * rows, half + (j + 1) * rows)
        q, k, v = qkv_of(x_refs[j][...], mats, bias_ref, cos_ref[there, :], sin_ref[there, :])
        q_ref[here, :] = q
        k_ref[there, :] = k
        v_ref[there, :] = v
    attend_blocks(blocks, half, weights, seg_ref, seg_row_ref, q_ref, k_ref, v_ref, o_ref, lse_ref, part_refs)


def attend_blocks(blocks, start, weights, seg_ref, seg_row_ref, q_ref, k_ref, v_ref, o_ref, lse_ref, part_refs):
    rows = q_ref.shape[0] // blocks
    for j in reversed(range(blocks)):
        here = slice(j * rows, (j + 1) * rows)
        there = slice(start + j * rows, start + (j + 1) * rows)
        allowed = seg_ref[there, :] == seg_row_ref[...]
        mixed, lse = attend_rows(q_ref[here, :], allowed, k_ref, v_ref)
        o_ref[here, :] = mixed
        lse_ref[here, :] = lse
        for g in range(weights.groups):
            columns = slice(g * weights.depth, (g + 1) * weights.depth)
            part_refs[j][:, columns] = mm(mixed, weights.out(g)).astype(bf16)


def attend_near_kernel(blocks, parts, width, *refs):
    weights = Attention(refs[:parts], width)
    seg_ref, seg_row_ref, q_ref, k_ref, v_ref, o_ref, lse_ref = refs[parts : parts + 7]
    attend_blocks(
        blocks, 0, weights, seg_ref, seg_row_ref, q_ref, k_ref, v_ref, o_ref, lse_ref, refs[parts + 7 :]
    )


def input_terms(weights, dq, dk, dv):
    return (
        mm_last(dq, weights.project(0))
        + mm_last(dk, weights.project(1))
        + mm_last(dv, weights.project(2))
    ).astype(bf16)


def attend_back_kernel(blocks, parts, *refs):
    dz_refs = refs[:blocks]
    rows, width = dz_refs[0].shape
    weights = Attention(refs[blocks : blocks + parts], width)
    (
        near_q_ref,
        far_q_ref,
        k_ref,
        v_ref,
        near_lse_ref,
        far_lse_ref,
        cos_ref,
        sin_ref,
        seg_ref,
        seg_row_ref,
        dq_ref,
        dk_ref,
        dv_ref,
    ) = refs[blocks + parts : blocks + parts + 13]
    part_refs = refs[blocks + parts + 13 : -3]
    do_ref, dk_sum, dv_sum = refs[-3:]
    local, depth = weights.local, weights.depth
    half = blocks // 2
    for j in range(blocks):
        value = jnp.zeros((rows, local), f32)
        for g in range(weights.groups):
            value = value + mm_last(dz_refs[j][:, g * depth : (g + 1) * depth], weights.out(g))
        do_ref[j * rows : (j + 1) * rows, :] = value.astype(bf16)
    dk_sum[...] = jnp.zeros_like(dk_sum)
    dv_sum[...] = jnp.zeros_like(dv_sum)

    def one_side(start, q_ref, lse_ref):
        def one_block(i, carry):
            here = pl.ds(pl.multiple_of(i * rows, rows), rows)
            there = pl.ds(pl.multiple_of(start + i * rows, rows), rows)
            q, do, lse = q_ref[here, :], do_ref[there, :], lse_ref[here, :]
            allowed = seg_ref[there, :] == seg_row_ref[...]
            lane = lax.broadcasted_iota(jnp.int32, (rows, local), 1)
            dq = jnp.zeros((rows, local), f32)
            for head in range(local // HEAD_DIM):
                mine = head_mask(lane, head)
                q_head = jnp.where(mine, q, jnp.zeros_like(q))
                do_head = jnp.where(mine, do, jnp.zeros_like(do))
                scores = mm_last(q_head, k_ref[...])
                prob = jnp.exp(jnp.where(allowed, scores, big_negative) - lse[:, head : head + 1])
                d_prob = mm_last(do_head, v_ref[...])
                product = prob * d_prob
                centre = jnp.sum(product, axis=-1, keepdims=True)
                d_scores = (product - prob * centre).astype(bf16)
                dv_sum[...] += mm_first(prob.astype(bf16), do_head)
                dk_sum[...] += mm_first(d_scores, q_head)
                dq = jnp.where(mine, mm(d_scores, k_ref[...]), dq)
            dq = turned(dq * (HEAD_DIM**-0.5), cos_ref[there, :], -sin_ref[there, :])
            dq_ref[there, :] = dq.astype(bf16)
            return carry

        lax.fori_loop(0, half, one_block, 0)

    one_side(0, near_q_ref, near_lse_ref)
    one_side(half * rows, far_q_ref, far_lse_ref)
    for j in reversed(range(blocks)):
        here = slice(j * rows, (j + 1) * rows)
        dk_ref[here, :] = turned(dk_sum[here, :], cos_ref[here, :], -sin_ref[here, :]).astype(bf16)
        dv_ref[here, :] = dv_sum[here, :].astype(bf16)
        if j >= half:
            part_refs[j - half][...] = input_terms(
                weights, dq_ref[here, :], dk_ref[here, :], dv_ref[here, :]
            )


def gelu_parts(u):
    root = math.sqrt(2.0 / math.pi)
    square = u * u
    th = jnp.tanh(root * u * (1.0 + 0.044715 * square))
    return root, square, th


def feed_kernel(blocks, parts, copies, *refs):
    a_refs = refs[:blocks]
    rows, width = a_refs[0].shape
    bias_ref, u_ref, g_ref = refs[blocks + parts : blocks + parts + 3]
    units = bias_ref.shape[1] // copies
    weights = Feed(refs[blocks : blocks + parts], width, units, copies)
    part_refs = refs[blocks + parts + 3 :]
    depth = weights.depth
    for j in reversed(range(blocks)):
        here = slice(j * rows, (j + 1) * rows)
        for start, w_up in weights.ups():
            columns = slice(start, start + weights.lanes)
            u = mm(a_refs[j][...], w_up) + bias_ref[:, columns]
            u_ref[here, columns] = u
            _, _, th = gelu_parts(u)
            g_ref[here, columns] = (0.5 * u * (1.0 + th)).astype(bf16)
        for k in range(weights.groups):
            part_refs[j][:, k * depth : (k + 1) * depth] = sum(
                mm(g_ref[here, copy * units : (copy + 1) * units], weights.down(copy, k))
                for copy in range(copies)
            ).astype(bf16)


def feed_back_kernel(blocks, parts, copies, *refs):
    dz_refs = refs[:blocks]
    rows, width = dz_refs[0].shape
    u_ref, du_ref = refs[blocks + parts : blocks + parts + 2]
    units = u_ref.shape[1] // copies
    weights = Feed(refs[blocks : blocks + parts], width, units, copies)
    part_refs = refs[blocks + parts + 2 :]
    depth = weights.depth
    for j in reversed(range(blocks)):
        here = slice(j * rows, (j + 1) * rows)
        for copy in range(copies):
            columns = slice(copy * units, (copy + 1) * units)
            dg = sum(
                mm_last(dz_refs[j][:, k * depth : (k + 1) * depth], weights.down(copy, k))
                for k in range(weights.groups)
            )
            u = u_ref[here, columns]
            root, square, th = gelu_parts(u)
            slope = 0.5 * (1.0 + th) + 0.5 * u * (1.0 - th * th) * (
                root * (1.0 + 0.134145 * square)
            )
            du_ref[here, columns] = (dg * slope).astype(bf16)
        part_refs[j][...] = sum(
            mm_last(du_ref[here, start : start + weights.lanes], w_up)
            for start, w_up in weights.ups()
        ).astype(bf16)


def feed_grads_kernel(blocks, sides, copies, *refs):
    a_refs, dz_refs = refs[:blocks], refs[blocks : 2 * blocks]
    g_refs = refs[2 * blocks : 2 * blocks + sides]
    du_refs = refs[2 * blocks + sides : 2 * blocks + 2 * sides]
    outs, bias_up_ref = refs[2 * blocks + 2 * sides : -1], refs[-1]
    width, units = a_refs[0].shape[1], g_refs[0].shape[1] // copies
    places = Feed(outs, width, units, copies)
    depth, lanes = places.depth, places.lanes
    dz = jnp.concatenate([ref[...] for ref in dz_refs], axis=0)
    a2 = jnp.concatenate([ref[...] for ref in a_refs], axis=0)
    g = jnp.concatenate([ref[...] for ref in g_refs], axis=0)
    du = jnp.concatenate([ref[...] for ref in du_refs], axis=0)
    for k in range(places.groups):
        here = slice(k * depth, (k + 1) * depth)
        for copy in range(copies):
            ref, row = places.down_place(copy)
            ref[k, row : row + units, :] = mm_first(
                g[:, copy * units : (copy + 1) * units], dz[:, here]
            ).astype(bf16)
            for chunk in range(places.chunks):
                ref, row = places.up_place(copy, chunk)
                start = copy * units + chunk * lanes
                ref[k, row : row + depth, :] = mm_first(
                    a2[:, here], du[:, start : start + lanes]
                ).astype(bf16)
    bias_up_ref[...] = column_sums(du)


def attention_grads_kernel(blocks, parts, *refs):
    a_refs, dz_refs = refs[:blocks], refs[blocks : 2 * blocks]
    rows, width = a_refs[0].shape
    weights = Attention(refs[2 * blocks : 2 * blocks + parts], width)
    rest = refs[2 * blocks + parts :]
    dq_ref, dk_ref, dv_ref, near_o_ref, far_o_ref = rest[:5]
    half = blocks // 2
    part_refs, outs, bias_ref = rest[5 : 5 + half], rest[5 + half : -1], rest[-1]
    depth, local = weights.depth, weights.local
    for j in reversed(range(half)):
        here = slice(j * rows, (j + 1) * rows)
        part_refs[j][...] = input_terms(
            weights, dq_ref[here, :], dk_ref[here, :], dv_ref[here, :]
        )
    dz = jnp.concatenate([ref[...] for ref in dz_refs], axis=0)
    a1 = jnp.concatenate([ref[...] for ref in a_refs], axis=0)
    o = jnp.concatenate([near_o_ref[...], far_o_ref[...]], axis=0)
    for p, ref in enumerate((dq_ref, dk_ref, dv_ref)):
        bias_ref[p] = column_sums(ref[...])
        for k in range(weights.groups):
            outs[0][k, p * depth : (p + 1) * depth, :] = mm_first(
                a1[:, k * depth : (k + 1) * depth], ref[...]
            ).astype(bf16)
    for k in range(weights.groups):
        outs[-1][k, weights.offset : weights.offset + local, :] = mm_first(
            o, dz[:, k * depth : (k + 1) * depth]
        ).astype(bf16)


def mod_grads_kernel(blocks, codes_ref, place_ref, *refs):
    out_ref = refs[-1]
    strip = refs[0].shape[1]
    for j in range(blocks):
        here = pl.ds(pl.multiple_of(place_ref[j] * strip, 128), strip)
        out_ref[:, here] = mm_first(codes_ref[...], refs[j][...])


def per_device(
    endpoints,
    lengths,
    timesteps,
    w_qkv,
    b_qkv,
    w_out,
    b_out,
    w_up,
    b_up,
    w_down,
    b_down,
    w_mod,
    b_mod,
):
    section = lax.axis_index("section")
    tensor = lax.axis_index("tensor")
    group = lax.axis_index("dp")
    tensors, groups = lax.axis_size("tensor"), lax.axis_size("dp")
    half = tensors // 2
    rows, width = endpoints.shape[3], endpoints.shape[4]
    slots = lengths.shape[2]
    frames = rows * tensors
    depth = width // groups
    local = w_qkv.shape[3]
    units = w_up.shape[2]
    mod_width = w_mod.shape[2]
    strip = mod_width // tensors
    first = section == 0
    terms = len(list(bits_of(tensors))) + 1
    packed = depth == local

    def pick(here, other):
        return jnp.where(first, here, other), jnp.where(first, other, here)

    def mine_of(array):
        return jnp.where(first, array[0], array[1])

    def others_of(array):
        return jnp.where(first, array[1], array[0])

    flat_qkv = w_qkv[0].reshape(3 * depth, local)
    packs = [jnp.concatenate([flat_qkv, w_out[0]], axis=0)] if packed else [flat_qkv, w_out[0]]
    wholes = [lax.all_gather(pack, ("section", "dp"), axis=0, tiled=False) for pack in packs]
    attention = [[Half(pack, layer) for pack in wholes] for layer in range(2)]
    steps = jnp.pad(timesteps[:, 0], ((0, 0), (0, SLOT_ROWS - slots)))
    steps = after(steps, *packs)
    all_steps = jnp.stack([steps] + [swap(steps, "dp", j) for j in range(1, groups)])
    taken = swap(others_of(endpoints[0, :, 0]), "section", 1)
    kept = mine_of(endpoints[0, :, 0])
    h0, cotangent = pick(kept, taken)
    h_all = gather_rows(h0)

    column = group * depth + jnp.arange(depth, dtype=jnp.int32)
    frequency = jnp.exp(
        (column % (width // 2)).astype(f32) * (-math.log(10000.0) / (width // 2 - 1))
    )
    angle = all_steps.astype(f32)[..., None] * frequency
    codes = jax.nn.silu(
        jnp.where(column < width // 2, jnp.sin(angle), jnp.cos(angle))
    ).astype(bf16)
    share = b_mod.shape[1]
    bias_all = jnp.where(
        jnp.arange(mod_width)[None] // share == group,
        jnp.concatenate([b_mod] * groups, axis=1),
        jnp.zeros((), bf16),
    )
    mod_part = jnp.dot(
        codes.reshape(-1, depth),
        lax.dynamic_slice_in_dim(w_mod[0], tensor * strip, strip, 1),
        preferred_element_type=f32,
    ) + lax.dynamic_slice_in_dim(bias_all, tensor * strip, strip, 1).astype(f32)
    bias_sizes = [local // groups] * 3 + [depth, units // groups, depth]
    bias_row = jnp.concatenate([b_qkv[:, p] for p in range(3)] + [b_out, b_up, b_down], axis=1)
    bias_row = jnp.pad(bias_row, ((0, 0), (0, strip - bias_row.shape[1]))).astype(f32)
    slot_row = jnp.arange(SLOT_ROWS)[:, None]
    mod_part = jnp.where(
        slot_row < slots, mod_part.reshape(groups, 2, SLOT_ROWS, strip), bias_row
    )
    own_layer, other_layer = [], []
    for j in range(groups):
        for across, terms_of in enumerate((own_layer, other_layer)):
            term = (others_of if across else mine_of)(mod_part[j])
            here = across * groups + j
            route = [(i, i ^ here) for i in range(2 * groups)]
            terms_of.append(lax.ppermute(term, ("section", "dp"), route) if here else term)

    def with_biases(parts):
        biases_of = jnp.stack([part[slots] for part in parts])
        return jnp.concatenate([functools.reduce(jnp.add, parts), biases_of], axis=0)

    layer_mods = jnp.stack(pick(with_biases(own_layer), with_biases(other_layer)))
    other_up = swap(after(w_up[0], layer_mods), "section", 1)
    other_down = swap(after(w_down[0], layer_mods), "section", 1)
    own_strip = layer_mods[:, :SLOT_ROWS]
    strips_all = [own_strip] + [swap(own_strip, "tensor", j) for j in range(1, tensors)]
    strips_all = absolute(strips_all, tensor)
    mod_all = jnp.where(slot_row < slots, jnp.concatenate(strips_all, axis=-1), 0.0)

    def biases(layer):
        rel = [layer_mods[layer, SLOT_ROWS + j].astype(f32) for j in range(groups)]
        full = jnp.stack(absolute(rel, group))
        pieces, start = [], 0
        for size in bias_sizes:
            pieces.append(full[:, start : start + size].reshape(1, groups * size))
            start += size
        qkv = jnp.concatenate(pieces[:3] + [jnp.zeros((SLOT_ROWS - 3, local), f32)], axis=0)
        return qkv, *pieces[3:]

    lengths_here = mine_of(lengths[:, 0])
    block_index = tensor ^ jnp.arange(tensors, dtype=jnp.int32)
    frame = (block_index[:, None] * rows + jnp.arange(rows, dtype=jnp.int32)).reshape(-1)
    ends = jnp.cumsum(lengths_here)
    segment = jnp.sum((frame[:, None] >= ends[None, :]).astype(jnp.int32), axis=1)
    member = segment[:, None] == jnp.arange(slots, dtype=jnp.int32)[None, :]
    begin = jnp.sum(jnp.where(member, (ends - lengths_here)[None, :], 0), axis=1)
    position = (frame - begin).astype(f32)
    lane = jnp.arange(128, dtype=jnp.int32) % HEAD_DIM
    inverse = jnp.exp((lane // 2).astype(f32) * (-2.0 * math.log(10000.0) / HEAD_DIM))
    angles = position[:, None] * inverse[None, :]
    cos_table = jnp.cos(angles)
    sin_table = jnp.sin(angles) * jnp.where(lane % 2 == 0, -1.0, 1.0)
    seg_col, seg_row = segment[:, None], segment[None, :]
    own_col, own_row = seg_col[:rows], seg_row[:, :rows]

    block = shape((rows, width), bf16)
    block32 = shape((rows, width), f32)
    half_local = shape((frames // 2, local), bf16)
    wide_local = shape((frames, local), bf16)
    half_lse = shape((frames // 2, 128), f32)
    slot_block = shape((SLOT_ROWS, width), f32)
    project = 2 * frames * width * local
    scores = 2 * frames * frames * max(local, 256)

    a1_all = call(
        "first_norm",
        functools.partial(first_norm_kernel, width, tensors),
        [block] * tensors,
        *h_all,
        seg_col,
        mod_all[0],
    )
    a1_near, a1_far = list(a1_all[:half]), a1_all[half:]


    def feed_packs(layer, layer_up, layer_down):
        if packed:
            chunks = [layer_up[layer][:, i : i + local] for i in range(0, units, local)]
            return [jnp.concatenate([*chunks, layer_down[layer]], axis=0)]
        return [layer_up[layer], layer_down[layer]]

    other_up, other_down, a1_near[0] = tie(other_up, other_down, a1_near[0])
    pairs = pick(w_up[0], other_up), pick(w_down[0], other_down)
    feed = [[gather_groups(pack) for pack in feed_packs(0, *pairs)]]
    last_packs = feed_packs(1, *pairs)
    partner_packs = [cross(pack) for pack in last_packs]
    if packed:
        last_packs = [jnp.concatenate(last_packs + partner_packs, axis=0)]
    else:
        last_packs = last_packs + partner_packs
    feed.append([gather_groups(pack) for pack in last_packs])

    layer_in = h0
    saved = []
    outputs = []
    for layer in range(2):
        mods = mod_all[layer]
        bias_qkv, bias_out, bias_up, bias_down = biases(layer)
        w_att = attention[layer]
        near_q, near_k, near_v = call(
            "project_near",
            functools.partial(project_kernel, half, len(w_att)),
            [half_local] * 3,
            *a1_near,
            *w_att,
            bias_qkv,
            cos_table,
            sin_table,
            flops=3 * project // 2,
        )
        a1_all = a1_near + (
            gather_near(after(a1_far, near_k)) if layer else list(a1_far)
        )
        far_q, k, v, far_o, far_lse, *parts = call(
            "attend_far",
            functools.partial(attend_far_kernel, half, len(w_att)),
            [half_local, wide_local, wide_local, half_local, half_lse] + [block] * half,
            *a1_all[half:],
            *w_att,
            bias_qkv,
            cos_table,
            sin_table,
            seg_col,
            seg_row,
            near_k,
            near_v,
        )
        summed, near_q = tie(near_sum(parts), near_q)
        far = cross(summed)
        near_o, near_lse, *parts = call(
            "attend_near",
            functools.partial(attend_near_kernel, half, len(w_att), width),
            [half_local, half_lse] + [block] * half,
            *w_att,
            seg_col,
            seg_row,
            near_q,
            k,
            v,
            flops=project // 2 + scores,
        )
        far = after(far, near_o)
        z1, h1, a2 = call(
            "middle",
            functools.partial(middle_kernel, width, terms),
            [block, block32, block],
            *scatter_near(parts),
            far,
            layer_in,
            bias_out,
            own_col,
            mods,
        )
        w_feed = feed[layer]
        copies = layer + 1
        a2_near = gather_near(a2)
        if copies == 2:
            bias_up = jnp.concatenate([bias_up, cross(bias_up)], axis=1)

        def feed_half(blocks_of):
            columns = units * copies
            return call(
                "feed",
                functools.partial(feed_kernel, half, len(w_feed), copies),
                [shape((frames // 2, columns), f32), shape((frames // 2, columns), bf16)]
                + [block] * half,
                *blocks_of,
                *w_feed,
                bias_up,
                flops=2 * frames * width * units,
            )

        if copies == 1:
            a2_far = cross(a2)
            near_u, near_g, *near_parts = feed_half(a2_near)
            a2_far = gather_near(after(a2_far, near_u))
            far_u, far_g, *far_parts = feed_half(a2_far)
            sums = [*scatter_near(near_parts), cross(near_sum(far_parts))]
            a2_all = a2_near + a2_far
            u_all, g_all = (near_u, far_u), (near_g, far_g)
        else:
            near_u, near_g, *near_parts = feed_half(a2_near)
            sums = scatter_near(near_parts)
            a2_all, u_all, g_all = a2_near, (near_u,), (near_g,)
        kept_state = (layer_in, a1_all, near_q, far_q, k, v, near_o, far_o, near_lse, far_lse)
        kept_state += (z1, h1, a2_all, u_all, g_all)
        if layer == 0:
            z2, y, a1 = call(
                "layer_end",
                functools.partial(layer_end_kernel, width, len(sums)),
                [block] * 3,
                *sums,
                h1,
                bias_down,
                own_col,
                mods,
                mod_all[layer + 1],
            )
            layer_in = y
            a1_near, a1_far = gather_near(a1), cross(a1)
        else:
            z2 = None
            y, grad, dz2, dgate_b, d_bias_down = call(
                "turn",
                functools.partial(turn_kernel, width, slots, len(sums)),
                [block, block, block, slot_block, slot_block],
                *sums,
                h1,
                bias_down,
                own_col,
                own_row,
                mods,
                cotangent,
            )
        outputs.append(y)
        saved.append((*kept_state, z2))

    attention_shards, feed_shards, in_grads, d_mods, d_biases = ([None, None] for _ in range(5))
    strip_index = jnp.arange(SLOT_ROWS)[:, None]
    for layer in (1, 0):
        mods = mod_all[layer]
        w_att, w_feed = attention[layer], feed[layer]
        (layer_in, a1_all, near_q, far_q, k, v, near_o, far_o, near_lse, far_lse) = saved[layer][:10]
        (z1, h1, a2_all, u_all, g_all, _) = saved[layer][10:]
        copies = layer + 1
        dz2_near = gather_near(dz2)

        def feed_back_half(blocks_of, u):
            return call(
                "feed_back",
                functools.partial(feed_back_kernel, half, len(w_feed), copies),
                [shape((frames // 2, units * copies), bf16)] + [block] * half,
                *blocks_of,
                *w_feed,
                u,
                micros=4 * copies,
            )

        if copies == 1:
            dz2_far = cross(dz2)
            near_du, *near_parts = feed_back_half(dz2_near, u_all[0])
            dz2_all = dz2_near + gather_near(after(dz2_far, near_du))
            far_du, *far_parts = feed_back_half(dz2_all[half:], u_all[1])
            summed, far_du = tie(near_sum(far_parts), far_du)
            sums = [*scatter_near(near_parts), cross(summed)]
            du_all = (near_du, far_du)
        else:
            dz2_all = dz2_near
            near_du, *near_parts = feed_back_half(dz2_near, u_all[0])
            sums = scatter_near(near_parts)
            du_all = (near_du,)

        def feed_grads(du_all):
            pack_rows = units // local * depth + units
            feed_outs = (
                [(groups, copies * pack_rows, local)]
                if packed
                else [(groups, depth, units), (groups, units, depth)] * copies
            )
            return call(
                "feed_grads",
                functools.partial(feed_grads_kernel, len(a2_all), len(du_all), copies),
                [shape(dims, bf16) for dims in feed_outs]
                + [shape((SLOT_ROWS, units * copies), f32)],
                *a2_all,
                *dz2_all,
                *g_all,
                *du_all,
                micros=6,
            )

        *d_feed, d_bias_up = feed_grads(du_all)
        sums = [*sums[:-1], after(sums[-1], d_bias_up)]
        dh1, dz1, d_mod_middle, d_bias_out = call(
            "middle_back",
            functools.partial(middle_back_kernel, width, slots, len(sums)),
            [block32, block, shape((SLOT_ROWS, 3 * width), f32), slot_block],
            *sums,
            h1,
            grad,
            z1,
            own_col,
            own_row,
            mods,
            micros=4,
        )
        dz1_far = cross(dz1)
        if copies == 2:
            d_bias_up = d_bias_up[:, :units] + cross(d_bias_up[:, units:])
        feed_shards[layer] = [
            lax.psum_scatter(value, "dp", scatter_dimension=0, tiled=False) for value in d_feed
        ]
        if layer == 0:
            count = len(feed_shards[1])
            if packed:
                shard = feed_shards[1][0]
                kept_units = [shard[: shard.shape[0] // 2]]
                given_units = [shard[shard.shape[0] // 2 :]]
            else:
                kept_units, given_units = feed_shards[1][: count // 2], feed_shards[1][count // 2 :]
            dz1_far, *given_units = tie(dz1_far, *given_units)
            arrived_units = [cross(part) for part in given_units]
        dz1_all = gather_near(dz1) + gather_near(dz1_far)
        dq, dk, dv, *far_parts = call(
            "attend_back",
            functools.partial(attend_back_kernel, tensors, len(w_att)),
            [wide_local] * 3 + [block] * half,
            *dz1_all,
            *w_att,
            near_q,
            far_q,
            k,
            v,
            near_lse,
            far_lse,
            cos_table,
            sin_table,
            seg_col,
            seg_row,
            scratch=[
                pltpu.VMEM((frames, local), bf16),
                pltpu.VMEM((frames, local), f32),
                pltpu.VMEM((frames, local), f32),
            ],
            micros=22,
        )
        summed, dk = tie(near_sum(far_parts), dk)
        far = cross(summed)
        if layer == 0:
            dq, *arrived_units = tie(dq, *arrived_units)
        att_outs = (
            [(groups, 3 * depth + local, local)]
            if packed
            else [(groups, 3 * depth, local), (groups, local, depth)]
        )
        results = call(
            "attention_grads",
            functools.partial(attention_grads_kernel, tensors, len(w_att)),
            [block] * half
            + [shape(dims, bf16) for dims in att_outs]
            + [shape((3, SLOT_ROWS, local), f32)],
            *a1_all,
            *dz1_all,
            *w_att,
            dq,
            dk,
            dv,
            near_o,
            far_o,
            micros=8,
        )
        near_parts, d_att, d_bias_qkv = results[:half], results[half:-1], results[-1]
        far = after(far, d_bias_qkv)
        if layer == 0:
            far, *attention_shards[1] = tie(far, *attention_shards[1])
            far, *feed_shards[0] = tie(far, *feed_shards[0])
        attention_shards[layer] = [
            lax.psum_scatter(value, "dp", scatter_dimension=0, tiled=False) for value in d_att
        ]
        sums = [*scatter_near(near_parts), far]
        kernel = functools.partial(layer_back_kernel, width, slots, terms, layer > 0)
        arrays = [*sums, layer_in, dh1, own_col, own_row, mods]
        outs = [block, shape((SLOT_ROWS, 2 * width), f32)]
        bias_sums = jnp.concatenate([d_bias_out[:1], d_bias_down[:1]], axis=1)
        gate_sums = dgate_b
        if layer > 0:
            grad, d_mod_first, dz2, dgate_b, d_bias_down = call(
                "layer_back",
                kernel,
                outs + [block, slot_block, slot_block],
                *arrays,
                saved[layer - 1][-1],
                mod_all[layer - 1],
                micros=4,
            )
        else:
            grad, d_mod_first = call("first_back", kernel, outs, *arrays)
        in_grads[layer] = grad
        bias_sums = jnp.pad(bias_sums, ((0, 0), (0, mod_width - bias_sums.shape[1])))
        d_mod = jnp.concatenate([d_mod_first, d_mod_middle, gate_sums], axis=1)
        d_mod = jnp.where(strip_index == slots, bias_sums, d_mod)
        blocks = [d_mod[:, b * strip : (b + 1) * strip] for b in range(tensors)]
        own = functools.reduce(
            jnp.add, reduce_rows(absolute(blocks, tensor), list(bits_of(tensors)))
        )
        own_bias = jnp.concatenate([d_bias_qkv[p, :1] for p in range(3)] + [d_bias_up[:1]], axis=1)
        own_bias = jnp.pad(own_bias, ((0, 0), (0, strip - own_bias.shape[1])))
        d_mods[layer] = jnp.where(strip_index == slots + 1, own_bias, own)

    feed_shards[1] = [
        (own.astype(f32) + partner.astype(f32)).astype(bf16)
        for own, partner in zip(kept_units, arrived_units, strict=True)
    ]

    def to_section(low, high):
        own = jnp.where(first, low, high)
        return own, swap(jnp.where(first, high, low), "section", 1)

    def add_sections(low, high):
        own, arrived = to_section(low, high)
        return own.astype(f32) + arrived.astype(f32)

    def frames_out(low, high):
        own, arrived = to_section(low, high)
        return jnp.where(first, jnp.stack([own, arrived]), jnp.stack([arrived, own]))

    activations = frames_out(*outputs)
    g_feed = [add_sections(*pair) for pair in zip(*feed_shards, strict=True)]
    input_grads = frames_out(*in_grads)
    d_mod, d_mod_other = to_section(*d_mods)
    pair = jnp.stack([d_mod, d_mod_other]).astype(bf16)
    pairs = jnp.stack([pair] + [swap(pair, "dp", j) for j in range(1, groups)])
    g_attention = []
    for low, high in zip(*attention_shards, strict=True):
        up = lax.ppermute(high, "section", [(0, 1)])
        down = lax.ppermute(low, "section", [(1, 0)])
        g_attention.append(
            jnp.where(first, low, high).astype(f32) + jnp.where(first, down, up).astype(f32)
        )
    everything = gather_rows(pairs.reshape(-1, strip))
    own_first = jnp.where(first, codes, codes[:, ::-1])
    live = jnp.where(slot_row < slots, own_first, jnp.zeros_like(own_first))
    places = tensor ^ jnp.arange(tensors, dtype=jnp.int32)
    (g_wmod,) = pl.pallas_call(
        functools.partial(mod_grads_kernel, tensors),
        name="mod_grads",
        out_shape=(shape((depth, mod_width), f32),),
        in_specs=[
            pl.BlockSpec(memory_space=pltpu.VMEM),
            pl.BlockSpec(memory_space=pltpu.SMEM),
        ]
        + [pl.BlockSpec(memory_space=pltpu.VMEM)] * tensors,
        compiler_params=pltpu.CompilerParams(vmem_limit_bytes=vmem_limit),
    )(live.reshape(-1, depth), places, *everything)
    row_sums = [
        jnp.sum(part.reshape(2 * groups, SLOT_ROWS, strip).astype(f32), axis=0)
        for part in everything
    ]
    own_sums = row_sums[0][slots + 1]
    all_sums = jnp.concatenate(absolute(row_sums, tensor), axis=1)

    def my_share(vector):
        count = vector.shape[-1] // groups
        return lax.dynamic_slice_in_dim(vector, group * count, count, vector.ndim - 1)

    g_bmod = my_share(jnp.sum(all_sums[:slots], axis=0))
    g_bqkv = my_share(own_sums[: 3 * local].reshape(3, local))
    g_bup = my_share(own_sums[3 * local : 3 * local + units])
    g_bout = my_share(all_sums[slots, :width])
    g_bdown = my_share(all_sums[slots, width : 2 * width])
    chunks = units // local * depth
    if packed:
        g_qkv, g_out = g_attention[0][: 3 * depth], g_attention[0][3 * depth :]
        g_up = jnp.concatenate(
            [g_feed[0][i : i + depth] for i in range(0, chunks, depth)], axis=1
        )
        g_down = g_feed[0][chunks:]
    else:
        g_qkv, g_out = g_attention
        g_up, g_down = g_feed
    return (
        activations[None, :, None],
        input_grads[None, :, None],
        g_qkv.reshape(1, 3, depth, local),
        g_bqkv[None],
        g_out[None],
        g_bout[None],
        g_up[None],
        g_bup[None],
        g_down[None],
        g_bdown[None],
        g_wmod[None],
        g_bmod[None],
    )


def solution(mesh):
    return jax.shard_map(
        per_device,
        mesh=mesh,
        in_specs=(
            P("section", None, "dp", "tensor", None),
            P(None, "dp", None),
            P(None, "dp", None),
            P("section", None, "dp", "tensor"),
            P("section", None, ("tensor", "dp")),
            P("section", "tensor", "dp"),
            P("section", "dp"),
            P("section", "dp", "tensor"),
            P("section", ("tensor", "dp")),
            P("section", "tensor", "dp"),
            P("section", "dp"),
            P("section", "dp", None),
            P("section", "dp"),
        ),
        out_specs=(
            P("section", None, "dp", "tensor", None),
            P("section", None, "dp", "tensor", None),
            P("section", None, "dp", "tensor"),
            P("section", None, ("tensor", "dp")),
            P("section", "tensor", "dp"),
            P("section", "dp"),
            P("section", "dp", "tensor"),
            P("section", ("tensor", "dp")),
            P("section", "tensor", "dp"),
            P("section", "dp"),
            P("section", "dp", None),
            P("section", "dp"),
        ),
        check_vma=False,
    )
```

```python
import functools
import math

import jax
import jax.numpy as jnp
from jax import lax
from jax.experimental import pallas as pl
from jax.experimental.pallas import tpu as pltpu
from jax.sharding import PartitionSpec as P

HEAD_DIM = 64
SLOT_ROWS = 8
norm_eps = 1e-06
big_negative = -1e30
f32 = jnp.float32
bf16 = jnp.bfloat16
vmem_limit = 32 * 1024 * 1024


def swap(block, axis, bit):
    return lax.ppermute(block, axis, [(i, i ^ bit) for i in range(lax.axis_size(axis))])


def after(value, *others):
    return lax.optimization_barrier((value, *others))[0]


def bits_of(count):
    bit = 1
    while bit < count:
        yield bit
        bit *= 2


def gather_near(block):
    blocks = {0: block}
    for bit in reversed(list(bits_of(lax.axis_size("tensor") // 2))):
        blocks.update({j | bit: swap(part, "tensor", bit) for j, part in list(blocks.items())})
    return [blocks[j] for j in range(len(blocks))]


def cross(block):
    return swap(block, "tensor", lax.axis_size("tensor") // 2)


def gather_rows(block):
    far = cross(block)
    return gather_near(block) + gather_near(far)


def reduce_rows(parts, bits):
    kept = dict(enumerate(parts))
    addends = [parts[0]]
    for bit in bits:
        arrived = {j: swap(kept[j | bit], "tensor", bit) for j in kept if not j & bit}
        addends.append(arrived.pop(0))
        kept = {
            0: parts[0],
            **{
                j: (kept[j].astype(f32) + part.astype(f32)).astype(parts[0].dtype)
                for j, part in arrived.items()
            },
        }
    return addends


def near_sum(parts):
    near = reduce_rows(parts, list(bits_of(len(parts))))
    summed = functools.reduce(jnp.add, [part.astype(f32) for part in near])
    return summed.astype(parts[0].dtype)


def scatter_near(parts):
    return reduce_rows(parts, list(bits_of(len(parts))))


def absolute(blocks, index):
    for bit in bits_of(len(blocks)):
        blocks = [
            jnp.where(index & bit, blocks[b ^ bit], blocks[b]) for b in range(len(blocks))
        ]
    return blocks


def gather_groups(block):
    return lax.all_gather(block, "dp", axis=0, tiled=False)


def tie(*values):
    return lax.optimization_barrier(values)


class Half:
    def __init__(self, array, index):
        self.array, self.index = array, index


def spec_of(arg):
    if isinstance(arg, Half):
        dims = arg.array.shape
        place = (arg.index,) + (0,) * (len(dims) - 1)
        return pl.BlockSpec((dims[0] // 2, *dims[1:]), lambda i: place)
    return pl.BlockSpec(memory_space=pltpu.VMEM)


def call(name, body, outs, *args, scratch=(), flops=0, micros=0):
    flops = flops or micros * 1_150_000_000
    whole = pl.BlockSpec(memory_space=pltpu.VMEM)
    grid = {"grid": (1,)} if any(isinstance(arg, Half) for arg in args) else {}
    return pl.pallas_call(
        body,
        in_specs=[spec_of(arg) for arg in args],
        out_specs=(whole,) * len(outs),
        **grid,
        out_shape=tuple(outs),
        name=name,
        scratch_shapes=scratch,
        compiler_params=pltpu.CompilerParams(vmem_limit_bytes=vmem_limit),
        cost_estimate=pl.CostEstimate(flops=flops, bytes_accessed=0, transcendentals=0),
    )(*[arg.array if isinstance(arg, Half) else arg for arg in args])


def shape(dims, dtype):
    return jax.ShapeDtypeStruct(dims, dtype)


def mm(left, right):
    return lax.dot_general(left, right, (((1,), (0,)), ((), ())), preferred_element_type=f32)


def mm_last(left, right):
    return lax.dot_general(left, right, (((1,), (1,)), ((), ())), preferred_element_type=f32)


def mm_first(left, right):
    return lax.dot_general(left, right, (((0,), (0,)), ((), ())), preferred_element_type=f32)


def slot_pick(seg_col):
    rows = seg_col.shape[0]
    lane = lax.broadcasted_iota(jnp.int32, (rows, SLOT_ROWS), 1)
    return (lane == seg_col).astype(f32).astype(bf16)


def part_of(picked, mod_ref, index, width):
    values = mod_ref[:, index * width : (index + 1) * width]
    high = values.astype(bf16)
    rest = (values - high.astype(f32)).astype(bf16)
    return mm(picked, high) + mm(picked, rest)


def slot_sums(seg_row, slots, values):
    row = lax.broadcasted_iota(jnp.int32, (SLOT_ROWS, seg_row.shape[1]), 0)
    picked = ((row == seg_row) & (row < slots)).astype(f32).astype(bf16)
    return mm(picked, values.astype(bf16))


def normed(values):
    centre = values - jnp.mean(values, axis=-1, keepdims=True)
    spread = jnp.mean(centre * centre, axis=-1, keepdims=True)
    inverse = lax.rsqrt(spread + norm_eps)
    return centre * inverse, inverse


def norm_back(norm, inverse, d_norm):
    mean_d = jnp.mean(d_norm, axis=-1, keepdims=True)
    mean_dn = jnp.mean(d_norm * norm, axis=-1, keepdims=True)
    return inverse * (d_norm - mean_d - norm * mean_dn)


def total(refs):
    value = refs[0][...].astype(f32)
    for ref in refs[1:]:
        value = value + ref[...].astype(f32)
    return value


def first_norm_kernel(width, blocks, *refs):
    seg_ref, mod_ref = refs[blocks : blocks + 2]
    rows = refs[0].shape[0]
    for j in range(blocks):
        picked = slot_pick(seg_ref[j * rows : (j + 1) * rows, :])
        norm, _ = normed(refs[j][...].astype(f32))
        scale = part_of(picked, mod_ref, 1, width)
        shift = part_of(picked, mod_ref, 0, width)
        refs[blocks + 2 + j][...] = (norm * (1.0 + scale) + shift).astype(bf16)


def middle_kernel(width, terms, *refs):
    sums = refs[:terms]
    h_ref, bias_ref, seg_ref, mod_ref, z1_ref, h1_ref, a2_ref = refs[terms:]
    picked = slot_pick(seg_ref[...])
    z1 = total(sums) + bias_ref[...]
    z1_ref[...] = z1.astype(bf16)
    h1 = h_ref[...].astype(f32) + part_of(picked, mod_ref, 2, width) * z1
    h1_ref[...] = h1
    norm, _ = normed(h1)
    a2_ref[...] = (
        norm * (1.0 + part_of(picked, mod_ref, 4, width)) + part_of(picked, mod_ref, 3, width)
    ).astype(bf16)


def layer_end_kernel(width, terms, *refs):
    sums = refs[:terms]
    h1_ref, bias_ref, seg_ref, mod_ref, next_ref, z2_ref, y_ref, a1_ref = refs[terms:]
    picked = slot_pick(seg_ref[...])
    z2 = total(sums) + bias_ref[...]
    z2_ref[...] = z2.astype(bf16)
    y = (h1_ref[...] + part_of(picked, mod_ref, 5, width) * z2).astype(bf16)
    y_ref[...] = y
    norm, _ = normed(y.astype(f32))
    a1_ref[...] = (
        norm * (1.0 + part_of(picked, next_ref, 1, width)) + part_of(picked, next_ref, 0, width)
    ).astype(bf16)


def column_sums(values):
    return mm(jnp.ones((SLOT_ROWS, values.shape[0]), bf16), values)


def branch_back(width, slots, grad, z2, picked, seg_row, mod_ref, dz2_ref, dgate_ref, bias_ref):
    dz2 = (grad * part_of(picked, mod_ref, 5, width)).astype(bf16)
    dz2_ref[...] = dz2
    dgate_ref[...] = slot_sums(seg_row, slots, grad * z2)
    bias_ref[...] = column_sums(dz2)


def turn_kernel(width, slots, terms, *refs):
    sums = refs[:terms]
    (h1_ref, bias_ref, seg_ref, seg_row_ref, mod_ref, cot_ref) = refs[terms : terms + 6]
    y_ref, c_ref = refs[terms + 6 : terms + 8]
    seg = seg_ref[...]
    picked = slot_pick(seg)
    z2 = total(sums) + bias_ref[...]
    y_ref[...] = (h1_ref[...] + part_of(picked, mod_ref, 5, width) * z2).astype(bf16)
    grad = jnp.where(seg < slots, cot_ref[...].astype(f32), 0.0)
    c_ref[...] = grad.astype(bf16)
    branch_back(width, slots, grad, z2, picked, seg_row_ref[...], mod_ref, *refs[terms + 8 :])


def middle_back_kernel(width, slots, terms, *refs):
    sums = refs[:terms]
    h1_ref, c_ref, z1_ref, seg_ref, seg_row_ref, mod_ref = refs[terms : terms + 6]
    dh1_ref, dz1_ref, d_mod_ref, bias_ref = refs[terms + 6 :]
    picked = slot_pick(seg_ref[...])
    seg_row = seg_row_ref[...]
    da2 = total(sums)
    norm, inverse = normed(h1_ref[...])
    d_mod_ref[:, width : 2 * width] = slot_sums(seg_row, slots, da2)
    d_mod_ref[:, 2 * width :] = slot_sums(seg_row, slots, da2 * norm)
    d_norm = da2 * (1.0 + part_of(picked, mod_ref, 4, width))
    dh1 = c_ref[...].astype(f32) + norm_back(norm, inverse, d_norm)
    dh1_ref[...] = dh1
    dz1 = (dh1 * part_of(picked, mod_ref, 2, width)).astype(bf16)
    dz1_ref[...] = dz1
    d_mod_ref[:, :width] = slot_sums(seg_row, slots, dh1 * z1_ref[...].astype(f32))
    bias_ref[...] = column_sums(dz1)


def layer_back_kernel(width, slots, terms, more, *refs):
    sums = refs[:terms]
    h_ref, dh1_ref, seg_ref, seg_row_ref, mod_ref = refs[terms : terms + 5]
    rest = refs[terms + 5 :]
    if more:
        z2_ref, before_ref = rest[:2]
        rest = rest[2:]
    g_ref, d_mod_ref = rest[:2]
    picked = slot_pick(seg_ref[...])
    seg_row = seg_row_ref[...]
    da1 = total(sums)
    norm, inverse = normed(h_ref[...].astype(f32))
    d_mod_ref[:, :width] = slot_sums(seg_row, slots, da1)
    d_mod_ref[:, width:] = slot_sums(seg_row, slots, da1 * norm)
    d_norm = da1 * (1.0 + part_of(picked, mod_ref, 1, width))
    grad = (dh1_ref[...] + norm_back(norm, inverse, d_norm)).astype(bf16)
    g_ref[...] = grad
    if more:
        branch_back(
            width,
            slots,
            grad.astype(f32),
            z2_ref[...].astype(f32),
            picked,
            seg_row,
            before_ref,
            *rest[2:],
        )


def turned(values, cos, sin):
    groups = []
    for start in range(0, values.shape[1], 128):
        part = values[:, start : start + 128]
        lane = lax.broadcasted_iota(jnp.int32, part.shape, 1)
        other = jnp.where(lane % 2 == 0, pltpu.roll(part, 127, 1), pltpu.roll(part, 1, 1))
        groups.append(part * cos + other * sin)
    return groups[0] if len(groups) == 1 else jnp.concatenate(groups, axis=1)


def head_mask(lane, head):
    return (lane >= head * HEAD_DIM) & (lane < (head + 1) * HEAD_DIM)


class Attention:
    def __init__(self, refs, width):
        self.refs, self.width = refs, width
        self.groups, _, self.local = refs[0].shape
        self.depth = width // self.groups
        self.offset = 3 * self.depth if len(refs) == 1 else 0

    def project(self, p):
        part = self.refs[0][:, p * self.depth : (p + 1) * self.depth, :]
        return part.reshape(self.width, self.local)

    def out(self, g):
        return self.refs[-1][g, self.offset : self.offset + self.local, :]


class Feed:
    def __init__(self, refs, width, units, copies):
        self.refs, self.width, self.units, self.copies = refs, width, units, copies
        self.groups, _, self.lanes = refs[0].shape
        self.depth = width // self.groups
        self.chunks = units // self.lanes
        self.packed = len(refs) == 1

    def up_place(self, copy, chunk):
        if self.packed:
            return self.refs[0], copy * (self.chunks * self.depth + self.units) + chunk * self.depth
        return self.refs[2 * copy], 0

    def down_place(self, copy):
        if self.packed:
            return self.refs[0], self.up_place(copy, self.chunks)[1]
        return self.refs[2 * copy + 1], 0

    def ups(self):
        for copy in range(self.copies):
            for chunk in range(self.chunks):
                ref, row = self.up_place(copy, chunk)
                block = ref[:, row : row + self.depth, :].reshape(self.width, self.lanes)
                yield copy * self.units + chunk * self.lanes, block

    def down(self, copy, g):
        ref, row = self.down_place(copy)
        return ref[g, row : row + self.units, :]


def qkv_of(x, weights, bias_ref, cos, sin):
    q = turned(mm(x, weights[0]) + bias_ref[0:1, :], cos, sin).astype(bf16)
    k = turned(mm(x, weights[1]) + bias_ref[1:2, :], cos, sin).astype(bf16)
    v = (mm(x, weights[2]) + bias_ref[2:3, :]).astype(bf16)
    return (q.astype(f32) * (HEAD_DIM**-0.5)).astype(bf16), k, v


def attend_rows(q, allowed, k_ref, v_ref):
    rows, local = q.shape
    lane = lax.broadcasted_iota(jnp.int32, (rows, local), 1)
    wide_lane = lax.broadcasted_iota(jnp.int32, (rows, 128), 1)
    mixed = jnp.zeros((rows, local), f32)
    lse = jnp.zeros((rows, 128), f32)
    for head in range(local // HEAD_DIM):
        mine = head_mask(lane, head)
        scores = mm_last(jnp.where(mine, q, jnp.zeros_like(q)), k_ref[...])
        scores = jnp.where(allowed, scores, big_negative)
        top = jnp.max(scores, axis=-1, keepdims=True)
        weight = jnp.exp(scores - top)
        weight_sum = jnp.sum(weight, axis=-1, keepdims=True)
        mixed = jnp.where(mine, mm(weight.astype(bf16), v_ref[...]) / weight_sum, mixed)
        lse = jnp.where(wide_lane == head, top + jnp.log(weight_sum), lse)
    return mixed.astype(bf16), lse


def project_kernel(blocks, parts, *refs):
    x_refs = refs[:blocks]
    weights = Attention(refs[blocks : blocks + parts], x_refs[0].shape[1])
    bias_ref, cos_ref, sin_ref, q_ref, k_ref, v_ref = refs[blocks + parts :]
    rows = x_refs[0].shape[0]
    mats = [weights.project(p) for p in range(3)]
    for j in range(blocks):
        here = slice(j * rows, (j + 1) * rows)
        q, k, v = qkv_of(x_refs[j][...], mats, bias_ref, cos_ref[here, :], sin_ref[here, :])
        q_ref[here, :] = q
        k_ref[here, :] = k
        v_ref[here, :] = v


def attend_far_kernel(blocks, parts, *refs):
    x_refs = refs[:blocks]
    rows, width = x_refs[0].shape
    weights = Attention(refs[blocks : blocks + parts], width)
    (
        bias_ref,
        cos_ref,
        sin_ref,
        seg_ref,
        seg_row_ref,
        near_k_ref,
        near_v_ref,
        q_ref,
        k_ref,
        v_ref,
        o_ref,
        lse_ref,
    ) = refs[blocks + parts : blocks + parts + 12]
    part_refs = refs[blocks + parts + 12 :]
    half = rows * blocks
    mats = [weights.project(p) for p in range(3)]
    k_ref[:half, :] = near_k_ref[...]
    v_ref[:half, :] = near_v_ref[...]
    for j in range(blocks):
        here = slice(j * rows, (j + 1) * rows)
        there = slice(half + j * rows, half + (j + 1) * rows)
        q, k, v = qkv_of(x_refs[j][...], mats, bias_ref, cos_ref[there, :], sin_ref[there, :])
        q_ref[here, :] = q
        k_ref[there, :] = k
        v_ref[there, :] = v
    attend_blocks(blocks, half, weights, seg_ref, seg_row_ref, q_ref, k_ref, v_ref, o_ref, lse_ref, part_refs)


def attend_blocks(blocks, start, weights, seg_ref, seg_row_ref, q_ref, k_ref, v_ref, o_ref, lse_ref, part_refs):
    rows = q_ref.shape[0] // blocks
    for j in reversed(range(blocks)):
        here = slice(j * rows, (j + 1) * rows)
        there = slice(start + j * rows, start + (j + 1) * rows)
        allowed = seg_ref[there, :] == seg_row_ref[...]
        mixed, lse = attend_rows(q_ref[here, :], allowed, k_ref, v_ref)
        o_ref[here, :] = mixed
        lse_ref[here, :] = lse
        for g in range(weights.groups):
            columns = slice(g * weights.depth, (g + 1) * weights.depth)
            part_refs[j][:, columns] = mm(mixed, weights.out(g)).astype(bf16)


def attend_near_kernel(blocks, parts, width, *refs):
    weights = Attention(refs[:parts], width)
    seg_ref, seg_row_ref, q_ref, k_ref, v_ref, o_ref, lse_ref = refs[parts : parts + 7]
    attend_blocks(
        blocks, 0, weights, seg_ref, seg_row_ref, q_ref, k_ref, v_ref, o_ref, lse_ref, refs[parts + 7 :]
    )


def input_terms(weights, dq, dk, dv):
    return (
        mm_last(dq, weights.project(0))
        + mm_last(dk, weights.project(1))
        + mm_last(dv, weights.project(2))
    ).astype(bf16)


def attend_back_kernel(blocks, parts, *refs):
    dz_refs = refs[:blocks]
    rows, width = dz_refs[0].shape
    weights = Attention(refs[blocks : blocks + parts], width)
    (
        near_q_ref,
        far_q_ref,
        k_ref,
        v_ref,
        near_lse_ref,
        far_lse_ref,
        cos_ref,
        sin_ref,
        seg_ref,
        seg_row_ref,
        dq_ref,
        dk_ref,
        dv_ref,
    ) = refs[blocks + parts : blocks + parts + 13]
    part_refs = refs[blocks + parts + 13 : -3]
    do_ref, dk_sum, dv_sum = refs[-3:]
    local, depth = weights.local, weights.depth
    half = blocks // 2
    for j in range(blocks):
        value = jnp.zeros((rows, local), f32)
        for g in range(weights.groups):
            value = value + mm_last(dz_refs[j][:, g * depth : (g + 1) * depth], weights.out(g))
        do_ref[j * rows : (j + 1) * rows, :] = value.astype(bf16)
    dk_sum[...] = jnp.zeros_like(dk_sum)
    dv_sum[...] = jnp.zeros_like(dv_sum)

    def one_side(start, q_ref, lse_ref):
        def one_block(i, carry):
            here = pl.ds(pl.multiple_of(i * rows, rows), rows)
            there = pl.ds(pl.multiple_of(start + i * rows, rows), rows)
            q, do, lse = q_ref[here, :], do_ref[there, :], lse_ref[here, :]
            allowed = seg_ref[there, :] == seg_row_ref[...]
            lane = lax.broadcasted_iota(jnp.int32, (rows, local), 1)
            dq = jnp.zeros((rows, local), f32)
            for head in range(local // HEAD_DIM):
                mine = head_mask(lane, head)
                q_head = jnp.where(mine, q, jnp.zeros_like(q))
                do_head = jnp.where(mine, do, jnp.zeros_like(do))
                scores = mm_last(q_head, k_ref[...])
                prob = jnp.exp(jnp.where(allowed, scores, big_negative) - lse[:, head : head + 1])
                d_prob = mm_last(do_head, v_ref[...])
                product = prob * d_prob
                centre = jnp.sum(product, axis=-1, keepdims=True)
                d_scores = (product - prob * centre).astype(bf16)
                dv_sum[...] += mm_first(prob.astype(bf16), do_head)
                dk_sum[...] += mm_first(d_scores, q_head)
                dq = jnp.where(mine, mm(d_scores, k_ref[...]), dq)
            dq = turned(dq * (HEAD_DIM**-0.5), cos_ref[there, :], -sin_ref[there, :])
            dq_ref[there, :] = dq.astype(bf16)
            return carry

        lax.fori_loop(0, half, one_block, 0)

    one_side(0, near_q_ref, near_lse_ref)
    one_side(half * rows, far_q_ref, far_lse_ref)
    for j in reversed(range(blocks)):
        here = slice(j * rows, (j + 1) * rows)
        dk_ref[here, :] = turned(dk_sum[here, :], cos_ref[here, :], -sin_ref[here, :]).astype(bf16)
        dv_ref[here, :] = dv_sum[here, :].astype(bf16)
        if j >= half:
            part_refs[j - half][...] = input_terms(
                weights, dq_ref[here, :], dk_ref[here, :], dv_ref[here, :]
            )


def gelu_parts(u):
    root = math.sqrt(2.0 / math.pi)
    square = u * u
    th = jnp.tanh(root * u * (1.0 + 0.044715 * square))
    return root, square, th


def feed_kernel(blocks, parts, copies, *refs):
    a_refs = refs[:blocks]
    rows, width = a_refs[0].shape
    bias_ref, u_ref, g_ref = refs[blocks + parts : blocks + parts + 3]
    units = bias_ref.shape[1] // copies
    weights = Feed(refs[blocks : blocks + parts], width, units, copies)
    part_refs = refs[blocks + parts + 3 :]
    depth = weights.depth
    for j in reversed(range(blocks)):
        here = slice(j * rows, (j + 1) * rows)
        for start, w_up in weights.ups():
            columns = slice(start, start + weights.lanes)
            u = mm(a_refs[j][...], w_up) + bias_ref[:, columns]
            u_ref[here, columns] = u
            _, _, th = gelu_parts(u)
            g_ref[here, columns] = (0.5 * u * (1.0 + th)).astype(bf16)
        for k in range(weights.groups):
            part_refs[j][:, k * depth : (k + 1) * depth] = sum(
                mm(g_ref[here, copy * units : (copy + 1) * units], weights.down(copy, k))
                for copy in range(copies)
            ).astype(bf16)


def feed_back_kernel(blocks, parts, copies, *refs):
    dz_refs = refs[:blocks]
    rows, width = dz_refs[0].shape
    u_ref, du_ref = refs[blocks + parts : blocks + parts + 2]
    units = u_ref.shape[1] // copies
    weights = Feed(refs[blocks : blocks + parts], width, units, copies)
    part_refs = refs[blocks + parts + 2 :]
    depth = weights.depth
    for j in reversed(range(blocks)):
        here = slice(j * rows, (j + 1) * rows)
        for copy in range(copies):
            columns = slice(copy * units, (copy + 1) * units)
            dg = sum(
                mm_last(dz_refs[j][:, k * depth : (k + 1) * depth], weights.down(copy, k))
                for k in range(weights.groups)
            )
            u = u_ref[here, columns]
            root, square, th = gelu_parts(u)
            slope = 0.5 * (1.0 + th) + 0.5 * u * (1.0 - th * th) * (
                root * (1.0 + 0.134145 * square)
            )
            du_ref[here, columns] = (dg * slope).astype(bf16)
        part_refs[j][...] = sum(
            mm_last(du_ref[here, start : start + weights.lanes], w_up)
            for start, w_up in weights.ups()
        ).astype(bf16)


def feed_grads_kernel(blocks, sides, copies, *refs):
    a_refs, dz_refs = refs[:blocks], refs[blocks : 2 * blocks]
    g_refs = refs[2 * blocks : 2 * blocks + sides]
    du_refs = refs[2 * blocks + sides : 2 * blocks + 2 * sides]
    outs, bias_up_ref = refs[2 * blocks + 2 * sides : -1], refs[-1]
    width, units = a_refs[0].shape[1], g_refs[0].shape[1] // copies
    places = Feed(outs, width, units, copies)
    depth, lanes = places.depth, places.lanes
    dz = jnp.concatenate([ref[...] for ref in dz_refs], axis=0)
    a2 = jnp.concatenate([ref[...] for ref in a_refs], axis=0)
    g = jnp.concatenate([ref[...] for ref in g_refs], axis=0)
    du = jnp.concatenate([ref[...] for ref in du_refs], axis=0)
    for k in range(places.groups):
        here = slice(k * depth, (k + 1) * depth)
        for copy in range(copies):
            ref, row = places.down_place(copy)
            ref[k, row : row + units, :] = mm_first(
                g[:, copy * units : (copy + 1) * units], dz[:, here]
            ).astype(bf16)
            for chunk in range(places.chunks):
                ref, row = places.up_place(copy, chunk)
                start = copy * units + chunk * lanes
                ref[k, row : row + depth, :] = mm_first(
                    a2[:, here], du[:, start : start + lanes]
                ).astype(bf16)
    bias_up_ref[...] = column_sums(du)


def attention_grads_kernel(blocks, parts, *refs):
    a_refs, dz_refs = refs[:blocks], refs[blocks : 2 * blocks]
    rows, width = a_refs[0].shape
    weights = Attention(refs[2 * blocks : 2 * blocks + parts], width)
    rest = refs[2 * blocks + parts :]
    dq_ref, dk_ref, dv_ref, near_o_ref, far_o_ref = rest[:5]
    half = blocks // 2
    part_refs, outs, bias_ref = rest[5 : 5 + half], rest[5 + half : -1], rest[-1]
    depth, local = weights.depth, weights.local
    for j in reversed(range(half)):
        here = slice(j * rows, (j + 1) * rows)
        part_refs[j][...] = input_terms(
            weights, dq_ref[here, :], dk_ref[here, :], dv_ref[here, :]
        )
    dz = jnp.concatenate([ref[...] for ref in dz_refs], axis=0)
    a1 = jnp.concatenate([ref[...] for ref in a_refs], axis=0)
    o = jnp.concatenate([near_o_ref[...], far_o_ref[...]], axis=0)
    for p, ref in enumerate((dq_ref, dk_ref, dv_ref)):
        bias_ref[p] = column_sums(ref[...])
        for k in range(weights.groups):
            outs[0][k, p * depth : (p + 1) * depth, :] = mm_first(
                a1[:, k * depth : (k + 1) * depth], ref[...]
            ).astype(bf16)
    for k in range(weights.groups):
        outs[-1][k, weights.offset : weights.offset + local, :] = mm_first(
            o, dz[:, k * depth : (k + 1) * depth]
        ).astype(bf16)


def mod_grads_kernel(blocks, codes_ref, place_ref, *refs):
    out_ref = refs[-1]
    strip = refs[0].shape[1]
    for j in range(blocks):
        here = pl.ds(pl.multiple_of(place_ref[j] * strip, 128), strip)
        out_ref[:, here] = mm_first(codes_ref[...], refs[j][...])


def per_device(
    endpoints,
    lengths,
    timesteps,
    w_qkv,
    b_qkv,
    w_out,
    b_out,
    w_up,
    b_up,
    w_down,
    b_down,
    w_mod,
    b_mod,
):
    section = lax.axis_index("section")
    tensor = lax.axis_index("tensor")
    group = lax.axis_index("dp")
    tensors, groups = lax.axis_size("tensor"), lax.axis_size("dp")
    half = tensors // 2
    rows, width = endpoints.shape[3], endpoints.shape[4]
    slots = lengths.shape[2]
    frames = rows * tensors
    depth = width // groups
    local = w_qkv.shape[3]
    units = w_up.shape[2]
    mod_width = w_mod.shape[2]
    strip = mod_width // tensors
    first = section == 0
    terms = len(list(bits_of(tensors))) + 1
    packed = depth == local

    def pick(here, other):
        return jnp.where(first, here, other), jnp.where(first, other, here)

    def mine_of(array):
        return jnp.where(first, array[0], array[1])

    def others_of(array):
        return jnp.where(first, array[1], array[0])

    flat_qkv = w_qkv[0].reshape(3 * depth, local)
    packs = [jnp.concatenate([flat_qkv, w_out[0]], axis=0)] if packed else [flat_qkv, w_out[0]]
    wholes = [lax.all_gather(pack, ("section", "dp"), axis=0, tiled=False) for pack in packs]
    attention = [[Half(pack, layer) for pack in wholes] for layer in range(2)]
    steps = jnp.pad(timesteps[:, 0], ((0, 0), (0, SLOT_ROWS - slots)))
    steps = after(steps, *packs)
    all_steps = jnp.stack([steps] + [swap(steps, "dp", j) for j in range(1, groups)])
    taken = swap(others_of(endpoints[0, :, 0]), "section", 1)
    kept = mine_of(endpoints[0, :, 0])
    h0, cotangent = pick(kept, taken)
    h_all = gather_rows(h0)

    column = group * depth + jnp.arange(depth, dtype=jnp.int32)
    frequency = jnp.exp(
        (column % (width // 2)).astype(f32) * (-math.log(10000.0) / (width // 2 - 1))
    )
    angle = all_steps.astype(f32)[..., None] * frequency
    codes = jax.nn.silu(
        jnp.where(column < width // 2, jnp.sin(angle), jnp.cos(angle))
    ).astype(bf16)
    share = b_mod.shape[1]
    bias_all = jnp.where(
        jnp.arange(mod_width)[None] // share == group,
        jnp.concatenate([b_mod] * groups, axis=1),
        jnp.zeros((), bf16),
    )
    mod_part = jnp.dot(
        codes.reshape(-1, depth),
        lax.dynamic_slice_in_dim(w_mod[0], tensor * strip, strip, 1),
        preferred_element_type=f32,
    ) + lax.dynamic_slice_in_dim(bias_all, tensor * strip, strip, 1).astype(f32)
    bias_sizes = [local // groups] * 3 + [depth, units // groups, depth]
    bias_row = jnp.concatenate([b_qkv[:, p] for p in range(3)] + [b_out, b_up, b_down], axis=1)
    bias_row = jnp.pad(bias_row, ((0, 0), (0, strip - bias_row.shape[1]))).astype(f32)
    slot_row = jnp.arange(SLOT_ROWS)[:, None]
    mod_part = jnp.where(
        slot_row < slots, mod_part.reshape(groups, 2, SLOT_ROWS, strip), bias_row
    )
    own_layer, other_layer = [], []
    for j in range(groups):
        for across, terms_of in enumerate((own_layer, other_layer)):
            term = (others_of if across else mine_of)(mod_part[j])
            here = across * groups + j
            route = [(i, i ^ here) for i in range(2 * groups)]
            terms_of.append(lax.ppermute(term, ("section", "dp"), route) if here else term)

    def with_biases(parts):
        biases_of = jnp.stack([part[slots] for part in parts])
        return jnp.concatenate([functools.reduce(jnp.add, parts), biases_of], axis=0)

    layer_mods = jnp.stack(pick(with_biases(own_layer), with_biases(other_layer)))
    other_up = swap(after(w_up[0], layer_mods), "section", 1)
    other_down = swap(after(w_down[0], layer_mods), "section", 1)
    own_strip = layer_mods[:, :SLOT_ROWS]
    strips_all = [own_strip] + [swap(own_strip, "tensor", j) for j in range(1, tensors)]
    strips_all = absolute(strips_all, tensor)
    mod_all = jnp.where(slot_row < slots, jnp.concatenate(strips_all, axis=-1), 0.0)

    def biases(layer):
        rel = [layer_mods[layer, SLOT_ROWS + j].astype(f32) for j in range(groups)]
        full = jnp.stack(absolute(rel, group))
        pieces, start = [], 0
        for size in bias_sizes:
            pieces.append(full[:, start : start + size].reshape(1, groups * size))
            start += size
        qkv = jnp.concatenate(pieces[:3] + [jnp.zeros((SLOT_ROWS - 3, local), f32)], axis=0)
        return qkv, *pieces[3:]

    lengths_here = mine_of(lengths[:, 0])
    block_index = tensor ^ jnp.arange(tensors, dtype=jnp.int32)
    frame = (block_index[:, None] * rows + jnp.arange(rows, dtype=jnp.int32)).reshape(-1)
    ends = jnp.cumsum(lengths_here)
    segment = jnp.sum((frame[:, None] >= ends[None, :]).astype(jnp.int32), axis=1)
    member = segment[:, None] == jnp.arange(slots, dtype=jnp.int32)[None, :]
    begin = jnp.sum(jnp.where(member, (ends - lengths_here)[None, :], 0), axis=1)
    position = (frame - begin).astype(f32)
    lane = jnp.arange(128, dtype=jnp.int32) % HEAD_DIM
    inverse = jnp.exp((lane // 2).astype(f32) * (-2.0 * math.log(10000.0) / HEAD_DIM))
    angles = position[:, None] * inverse[None, :]
    cos_table = jnp.cos(angles)
    sin_table = jnp.sin(angles) * jnp.where(lane % 2 == 0, -1.0, 1.0)
    seg_col, seg_row = segment[:, None], segment[None, :]
    own_col, own_row = seg_col[:rows], seg_row[:, :rows]

    block = shape((rows, width), bf16)
    block32 = shape((rows, width), f32)
    half_local = shape((frames // 2, local), bf16)
    wide_local = shape((frames, local), bf16)
    half_lse = shape((frames // 2, 128), f32)
    slot_block = shape((SLOT_ROWS, width), f32)
    project = 2 * frames * width * local
    scores = 2 * frames * frames * max(local, 256)

    a1_all = call(
        "first_norm",
        functools.partial(first_norm_kernel, width, tensors),
        [block] * tensors,
        *h_all,
        seg_col,
        mod_all[0],
    )
    a1_near, a1_far = list(a1_all[:half]), a1_all[half:]


    def feed_packs(layer, layer_up, layer_down):
        if packed:
            chunks = [layer_up[layer][:, i : i + local] for i in range(0, units, local)]
            return [jnp.concatenate([*chunks, layer_down[layer]], axis=0)]
        return [layer_up[layer], layer_down[layer]]

    other_up, other_down, a1_near[0] = tie(other_up, other_down, a1_near[0])
    pairs = pick(w_up[0], other_up), pick(w_down[0], other_down)
    feed = [[gather_groups(pack) for pack in feed_packs(0, *pairs)]]
    last_packs = feed_packs(1, *pairs)
    partner_packs = [cross(pack) for pack in last_packs]
    if packed:
        last_packs = [jnp.concatenate(last_packs + partner_packs, axis=0)]
    else:
        last_packs = last_packs + partner_packs
    feed.append([gather_groups(pack) for pack in last_packs])

    layer_in = h0
    saved = []
    outputs = []
    for layer in range(2):
        mods = mod_all[layer]
        bias_qkv, bias_out, bias_up, bias_down = biases(layer)
        w_att = attention[layer]
        near_q, near_k, near_v = call(
            "project_near",
            functools.partial(project_kernel, half, len(w_att)),
            [half_local] * 3,
            *a1_near,
            *w_att,
            bias_qkv,
            cos_table,
            sin_table,
            flops=3 * project // 2,
        )
        a1_all = a1_near + (
            gather_near(after(a1_far, near_k)) if layer else list(a1_far)
        )
        far_q, k, v, far_o, far_lse, *parts = call(
            "attend_far",
            functools.partial(attend_far_kernel, half, len(w_att)),
            [half_local, wide_local, wide_local, half_local, half_lse] + [block] * half,
            *a1_all[half:],
            *w_att,
            bias_qkv,
            cos_table,
            sin_table,
            seg_col,
            seg_row,
            near_k,
            near_v,
        )
        summed, near_q = tie(near_sum(parts), near_q)
        far = cross(summed)
        near_o, near_lse, *parts = call(
            "attend_near",
            functools.partial(attend_near_kernel, half, len(w_att), width),
            [half_local, half_lse] + [block] * half,
            *w_att,
            seg_col,
            seg_row,
            near_q,
            k,
            v,
            flops=project // 2 + scores,
        )
        far = after(far, near_o)
        z1, h1, a2 = call(
            "middle",
            functools.partial(middle_kernel, width, terms),
            [block, block32, block],
            *scatter_near(parts),
            far,
            layer_in,
            bias_out,
            own_col,
            mods,
        )
        w_feed = feed[layer]
        copies = layer + 1
        a2_near = gather_near(a2)
        if copies == 2:
            bias_up = jnp.concatenate([bias_up, cross(bias_up)], axis=1)

        def feed_half(blocks_of):
            columns = units * copies
            return call(
                "feed",
                functools.partial(feed_kernel, half, len(w_feed), copies),
                [shape((frames // 2, columns), f32), shape((frames // 2, columns), bf16)]
                + [block] * half,
                *blocks_of,
                *w_feed,
                bias_up,
                flops=2 * frames * width * units,
            )

        if copies == 1:
            a2_far = cross(a2)
            near_u, near_g, *near_parts = feed_half(a2_near)
            a2_far = gather_near(after(a2_far, near_u))
            far_u, far_g, *far_parts = feed_half(a2_far)
            sums = [*scatter_near(near_parts), cross(near_sum(far_parts))]
            a2_all = a2_near + a2_far
            u_all, g_all = (near_u, far_u), (near_g, far_g)
        else:
            near_u, near_g, *near_parts = feed_half(a2_near)
            sums = scatter_near(near_parts)
            a2_all, u_all, g_all = a2_near, (near_u,), (near_g,)
        kept_state = (layer_in, a1_all, near_q, far_q, k, v, near_o, far_o, near_lse, far_lse)
        kept_state += (z1, h1, a2_all, u_all, g_all)
        if layer == 0:
            z2, y, a1 = call(
                "layer_end",
                functools.partial(layer_end_kernel, width, len(sums)),
                [block] * 3,
                *sums,
                h1,
                bias_down,
                own_col,
                mods,
                mod_all[layer + 1],
            )
            layer_in = y
            a1_near, a1_far = gather_near(a1), cross(a1)
        else:
            z2 = None
            y, grad, dz2, dgate_b, d_bias_down = call(
                "turn",
                functools.partial(turn_kernel, width, slots, len(sums)),
                [block, block, block, slot_block, slot_block],
                *sums,
                h1,
                bias_down,
                own_col,
                own_row,
                mods,
                cotangent,
            )
        outputs.append(y)
        saved.append((*kept_state, z2))

    attention_shards, feed_shards, in_grads, d_mods, d_biases = ([None, None] for _ in range(5))
    strip_index = jnp.arange(SLOT_ROWS)[:, None]
    for layer in (1, 0):
        mods = mod_all[layer]
        w_att, w_feed = attention[layer], feed[layer]
        (layer_in, a1_all, near_q, far_q, k, v, near_o, far_o, near_lse, far_lse) = saved[layer][:10]
        (z1, h1, a2_all, u_all, g_all, _) = saved[layer][10:]
        copies = layer + 1
        dz2_near = gather_near(dz2)

        def feed_back_half(blocks_of, u):
            return call(
                "feed_back",
                functools.partial(feed_back_kernel, half, len(w_feed), copies),
                [shape((frames // 2, units * copies), bf16)] + [block] * half,
                *blocks_of,
                *w_feed,
                u,
                micros=4 * copies,
            )

        if copies == 1:
            dz2_far = cross(dz2)
            near_du, *near_parts = feed_back_half(dz2_near, u_all[0])
            dz2_all = dz2_near + gather_near(after(dz2_far, near_du))
            far_du, *far_parts = feed_back_half(dz2_all[half:], u_all[1])
            summed, far_du = tie(near_sum(far_parts), far_du)
            sums = [*scatter_near(near_parts), cross(summed)]
            du_all = (near_du, far_du)
        else:
            dz2_all = dz2_near
            near_du, *near_parts = feed_back_half(dz2_near, u_all[0])
            sums = scatter_near(near_parts)
            du_all = (near_du,)

        def feed_grads(du_all):
            pack_rows = units // local * depth + units
            feed_outs = (
                [(groups, copies * pack_rows, local)]
                if packed
                else [(groups, depth, units), (groups, units, depth)] * copies
            )
            return call(
                "feed_grads",
                functools.partial(feed_grads_kernel, len(a2_all), len(du_all), copies),
                [shape(dims, bf16) for dims in feed_outs]
                + [shape((SLOT_ROWS, units * copies), f32)],
                *a2_all,
                *dz2_all,
                *g_all,
                *du_all,
                micros=6,
            )

        *d_feed, d_bias_up = feed_grads(du_all)
        sums = [*sums[:-1], after(sums[-1], d_bias_up)]
        dh1, dz1, d_mod_middle, d_bias_out = call(
            "middle_back",
            functools.partial(middle_back_kernel, width, slots, len(sums)),
            [block32, block, shape((SLOT_ROWS, 3 * width), f32), slot_block],
            *sums,
            h1,
            grad,
            z1,
            own_col,
            own_row,
            mods,
            micros=4,
        )
        dz1_far = cross(dz1)
        if copies == 2:
            d_bias_up = d_bias_up[:, :units] + cross(d_bias_up[:, units:])
        feed_shards[layer] = [
            lax.psum_scatter(value, "dp", scatter_dimension=0, tiled=False) for value in d_feed
        ]
        if layer == 0:
            count = len(feed_shards[1])
            if packed:
                shard = feed_shards[1][0]
                kept_units = [shard[: shard.shape[0] // 2]]
                given_units = [shard[shard.shape[0] // 2 :]]
            else:
                kept_units, given_units = feed_shards[1][: count // 2], feed_shards[1][count // 2 :]
            dz1_far, *given_units = tie(dz1_far, *given_units)
            arrived_units = [cross(part) for part in given_units]
        dz1_all = gather_near(dz1) + gather_near(dz1_far)
        dq, dk, dv, *far_parts = call(
            "attend_back",
            functools.partial(attend_back_kernel, tensors, len(w_att)),
            [wide_local] * 3 + [block] * half,
            *dz1_all,
            *w_att,
            near_q,
            far_q,
            k,
            v,
            near_lse,
            far_lse,
            cos_table,
            sin_table,
            seg_col,
            seg_row,
            scratch=[
                pltpu.VMEM((frames, local), bf16),
                pltpu.VMEM((frames, local), f32),
                pltpu.VMEM((frames, local), f32),
            ],
            micros=22,
        )
        summed, dk = tie(near_sum(far_parts), dk)
        far = cross(summed)
        if layer == 0:
            dq, *arrived_units = tie(dq, *arrived_units)
        att_outs = (
            [(groups, 3 * depth + local, local)]
            if packed
            else [(groups, 3 * depth, local), (groups, local, depth)]
        )
        results = call(
            "attention_grads",
            functools.partial(attention_grads_kernel, tensors, len(w_att)),
            [block] * half
            + [shape(dims, bf16) for dims in att_outs]
            + [shape((3, SLOT_ROWS, local), f32)],
            *a1_all,
            *dz1_all,
            *w_att,
            dq,
            dk,
            dv,
            near_o,
            far_o,
            micros=8,
        )
        near_parts, d_att, d_bias_qkv = results[:half], results[half:-1], results[-1]
        far = after(far, d_bias_qkv)
        if layer == 0:
            far, *attention_shards[1] = tie(far, *attention_shards[1])
            far, *feed_shards[0] = tie(far, *feed_shards[0])
        attention_shards[layer] = [
            lax.psum_scatter(value, "dp", scatter_dimension=0, tiled=False) for value in d_att
        ]
        sums = [*scatter_near(near_parts), far]
        kernel = functools.partial(layer_back_kernel, width, slots, terms, layer > 0)
        arrays = [*sums, layer_in, dh1, own_col, own_row, mods]
        outs = [block, shape((SLOT_ROWS, 2 * width), f32)]
        bias_sums = jnp.concatenate([d_bias_out[:1], d_bias_down[:1]], axis=1)
        gate_sums = dgate_b
        if layer > 0:
            grad, d_mod_first, dz2, dgate_b, d_bias_down = call(
                "layer_back",
                kernel,
                outs + [block, slot_block, slot_block],
                *arrays,
                saved[layer - 1][-1],
                mod_all[layer - 1],
                micros=4,
            )
        else:
            grad, d_mod_first = call("first_back", kernel, outs, *arrays)
        in_grads[layer] = grad
        bias_sums = jnp.pad(bias_sums, ((0, 0), (0, mod_width - bias_sums.shape[1])))
        d_mod = jnp.concatenate([d_mod_first, d_mod_middle, gate_sums], axis=1)
        d_mod = jnp.where(strip_index == slots, bias_sums, d_mod)
        blocks = [d_mod[:, b * strip : (b + 1) * strip] for b in range(tensors)]
        own = functools.reduce(
            jnp.add, reduce_rows(absolute(blocks, tensor), list(bits_of(tensors)))
        )
        own_bias = jnp.concatenate([d_bias_qkv[p, :1] for p in range(3)] + [d_bias_up[:1]], axis=1)
        own_bias = jnp.pad(own_bias, ((0, 0), (0, strip - own_bias.shape[1])))
        d_mods[layer] = jnp.where(strip_index == slots + 1, own_bias, own)

    feed_shards[1] = [
        (own.astype(f32) + partner.astype(f32)).astype(bf16)
        for own, partner in zip(kept_units, arrived_units, strict=True)
    ]

    def to_section(low, high):
        own = jnp.where(first, low, high)
        return own, swap(jnp.where(first, high, low), "section", 1)

    def add_sections(low, high):
        own, arrived = to_section(low, high)
        return own.astype(f32) + arrived.astype(f32)

    def frames_out(low, high):
        own, arrived = to_section(low, high)
        return jnp.where(first, jnp.stack([own, arrived]), jnp.stack([arrived, own]))

    activations = frames_out(*outputs)
    g_feed = [add_sections(*pair) for pair in zip(*feed_shards, strict=True)]
    input_grads = frames_out(*in_grads)
    d_mod, d_mod_other = to_section(*d_mods)
    pair = jnp.stack([d_mod, d_mod_other]).astype(bf16)
    pairs = jnp.stack([pair] + [swap(pair, "dp", j) for j in range(1, groups)])
    g_attention = []
    for low, high in zip(*attention_shards, strict=True):
        up = lax.ppermute(high, "section", [(0, 1)])
        down = lax.ppermute(low, "section", [(1, 0)])
        g_attention.append(
            jnp.where(first, low, high).astype(f32) + jnp.where(first, down, up).astype(f32)
        )
    everything = gather_rows(pairs.reshape(-1, strip))
    own_first = jnp.where(first, codes, codes[:, ::-1])
    live = jnp.where(slot_row < slots, own_first, jnp.zeros_like(own_first))
    places = tensor ^ jnp.arange(tensors, dtype=jnp.int32)
    (g_wmod,) = pl.pallas_call(
        functools.partial(mod_grads_kernel, tensors),
        name="mod_grads",
        out_shape=(shape((depth, mod_width), f32),),
        in_specs=[
            pl.BlockSpec(memory_space=pltpu.VMEM),
            pl.BlockSpec(memory_space=pltpu.SMEM),
        ]
        + [pl.BlockSpec(memory_space=pltpu.VMEM)] * tensors,
        compiler_params=pltpu.CompilerParams(vmem_limit_bytes=vmem_limit),
    )(live.reshape(-1, depth), places, *everything)
    row_sums = [
        jnp.sum(part.reshape(2 * groups, SLOT_ROWS, strip).astype(f32), axis=0)
        for part in everything
    ]
    own_sums = row_sums[0][slots + 1]
    all_sums = jnp.concatenate(absolute(row_sums, tensor), axis=1)

    def my_share(vector):
        count = vector.shape[-1] // groups
        return lax.dynamic_slice_in_dim(vector, group * count, count, vector.ndim - 1)

    g_bmod = my_share(jnp.sum(all_sums[:slots], axis=0))
    g_bqkv = my_share(own_sums[: 3 * local].reshape(3, local))
    g_bup = my_share(own_sums[3 * local : 3 * local + units])
    g_bout = my_share(all_sums[slots, :width])
    g_bdown = my_share(all_sums[slots, width : 2 * width])
    chunks = units // local * depth
    if packed:
        g_qkv, g_out = g_attention[0][: 3 * depth], g_attention[0][3 * depth :]
        g_up = jnp.concatenate(
            [g_feed[0][i : i + depth] for i in range(0, chunks, depth)], axis=1
        )
        g_down = g_feed[0][chunks:]
    else:
        g_qkv, g_out = g_attention
        g_up, g_down = g_feed
    return (
        activations[None, :, None],
        input_grads[None, :, None],
        g_qkv.reshape(1, 3, depth, local),
        g_bqkv[None],
        g_out[None],
        g_bout[None],
        g_up[None],
        g_bup[None],
        g_down[None],
        g_bdown[None],
        g_wmod[None],
        g_bmod[None],
    )


def solution(mesh):
    return jax.shard_map(
        per_device,
        mesh=mesh,
        in_specs=(
            P("section", None, "dp", "tensor", None),
            P(None, "dp", None),
            P(None, "dp", None),
            P("section", None, "dp", "tensor"),
            P("section", None, ("tensor", "dp")),
            P("section", "tensor", "dp"),
            P("section", "dp"),
            P("section", "dp", "tensor"),
            P("section", ("tensor", "dp")),
            P("section", "tensor", "dp"),
            P("section", "dp"),
            P("section", "dp", None),
            P("section", "dp"),
        ),
        out_specs=(
            P("section", None, "dp", "tensor", None),
            P("section", None, "dp", "tensor", None),
            P("section", None, "dp", "tensor"),
            P("section", None, ("tensor", "dp")),
            P("section", "tensor", "dp"),
            P("section", "dp"),
            P("section", "dp", "tensor"),
            P("section", ("tensor", "dp")),
            P("section", "tensor", "dp"),
            P("section", "dp"),
            P("section", "dp", None),
            P("section", "dp"),
        ),
        check_vma=False,
    )
```
